32 devices in a mesh: ctx: 16 (over z, y, x), fsdp: 2 (over core).
Axes of the slice: x: 2, y: 2, z: 4, core: 2. Of those that a mesh axis runs over, the one named last changes fastest.
Arguments:
- inputs: bfloat16 [16384, 512], P(('ctx', 'fsdp')), may hold values from -6 to 6
- targets: bfloat16 [16384, 512], P(('ctx', 'fsdp')), may hold values from -6 to 6
- valid_mask: int32 [16384], P(('ctx', 'fsdp')), may hold values from 0 to 1
- block_seq: int32 [16], replicated, may hold values from 0 to 2, never falling along the last dimension, each value on 1 to 8 neighbouring positions
- w_qkv: bfloat16 [512, 1536], P('fsdp'), may hold values from -0.25 to 0.25
- w_out: bfloat16 [512, 512], P('fsdp'), may hold values from -1 to 1
- w_up: bfloat16 [512, 2048], P('fsdp'), may hold values from -0.25 to 0.25
- w_down: bfloat16 [2048, 512], P('fsdp'), may hold values from -0.125 to 0.125
- norm_gains: bfloat16 [2, 512], P(None, 'fsdp'), may hold values from 0.44 to 1.66
- biases: bfloat16 [10, 512], P(None, 'fsdp'), may hold values from -0.25 to 0.25
- first_qkv: float32 [512, 1536], P('fsdp'), may hold values from -9.536743e-06 to 9.536743e-06
- first_out: float32 [512, 512], P('fsdp'), may hold values from -9.536743e-06 to 9.536743e-06
- first_up: float32 [512, 2048], P('fsdp'), may hold values from -9.536743e-06 to 9.536743e-06
- first_down: float32 [2048, 512], P('fsdp'), may hold values from -9.536743e-06 to 9.536743e-06
- first_gains: float32 [2, 512], P(None, 'fsdp'), may hold values from -9.536743e-06 to 9.536743e-06
- first_biases: float32 [10, 512], P(None, 'fsdp'), may hold values from -9.536743e-06 to 9.536743e-06
- second_qkv: float32 [512, 1536], P('fsdp'), may hold values from 1.6815403e-12 to 6.6627073e-12
- second_out: float32 [512, 512], P('fsdp'), may hold values from 1.6815403e-12 to 6.6627073e-12
- second_up: float32 [512, 2048], P('fsdp'), may hold values from 1.6815403e-12 to 6.6627073e-12
- second_down: float32 [2048, 512], P('fsdp'), may hold values from 1.6815403e-12 to 6.6627073e-12
- second_gains: float32 [2, 512], P(None, 'fsdp'), may hold values from 1.6815403e-12 to 6.6627073e-12
- second_biases: float32 [10, 512], P(None, 'fsdp'), may hold values from 1.6815403e-12 to 6.6627073e-12
Outputs:
- outputs: bfloat16 [16384, 512], P(('ctx', 'fsdp'))
- grad_inputs: float32 [16384, 512], P(('ctx', 'fsdp'))
- grad_qkv: float32 [512, 1536], P('fsdp')
- grad_out: float32 [512, 512], P('fsdp')
- grad_up: float32 [512, 2048], P('fsdp')
- grad_down: float32 [2048, 512], P('fsdp')
- grad_gains: float32 [2, 512], P(None, 'fsdp')
- grad_biases: float32 [10, 512], P(None, 'fsdp')
- grad_norm: float32 [], replicated
- new_first_qkv: float32 [512, 1536], P('fsdp')
- new_first_out: float32 [512, 512], P('fsdp')
- new_first_up: float32 [512, 2048], P('fsdp')
- new_first_down: float32 [2048, 512], P('fsdp')
- new_first_gains: float32 [2, 512], P(None, 'fsdp')
- new_first_biases: float32 [10, 512], P(None, 'fsdp')
- new_second_qkv: float32 [512, 1536], P('fsdp')
- new_second_out: float32 [512, 512], P('fsdp')
- new_second_up: float32 [512, 2048], P('fsdp')
- new_second_down: float32 [2048, 512], P('fsdp')
- new_second_gains: float32 [2, 512], P(None, 'fsdp')
- new_second_biases: float32 [10, 512], P(None, 'fsdp')
- step_qkv: float32 [512, 1536], P('fsdp')
- step_out: float32 [512, 512], P('fsdp')
- step_up: float32 [512, 2048], P('fsdp')
- step_down: float32 [2048, 512], P('fsdp')
- step_gains: float32 [2, 512], P(None, 'fsdp')
- step_biases: float32 [10, 512], P(None, 'fsdp')
The draws below stay inside these ranges and needn't reach their ends.
Inputs may be any that keep to these rules, and one draw needn't show every extreme that they name: `block_seq`: sequence numbers of the blocks in order never fall; each sequence covers 1 to 8 consecutive blocks and some sequence covers exactly 8.
All inputs are finite; a program needn't handle non-finite values.
Results may differ from the reference program's by a relative error of at most 0.018.
Values may be sent and summed in bfloat16 or wider, within the bound.
No kernel may reach another device: no remote copies, remote signals or barrier semaphores. Data moves between devices by JAX's collectives and lax.ppermute only.
A program may use at most 576 MiB of HBM per device.

```python
import math
import jax
import jax.numpy as jnp
import numpy as np
from jax import lax

D = 512
H = 8
HD = 64
FF = 2048
T_DEV = 512
MOST = 8
STEP = 10
BLOCK = 1024
TOKENS = 16384
SEQS = 3
NB = 10
PARAMS = 3151872
N_CTX = 16
N_FSDP = 2


def draw_valid_mask(key, part):
    positions = jnp.arange(TOKENS, dtype=jnp.int32)
    block_index = positions // (T_DEV * N_FSDP)
    limit = 20 + 40 * block_index // max(N_CTX - 1, 1)
    rolls = jax.random.randint(key, (TOKENS,), 0, 64, dtype=jnp.int32)
    return (rolls < limit).astype(jnp.int32)


def draw_norm_gains(key, part):
    columns = jnp.arange(D, dtype=jnp.float32) / max(D - 1, 1)
    factors = jax.random.uniform(jax.random.fold_in(key, 11), (2, D), jnp.float32, -0.1, 0.1)
    base = 0.5 + columns
    return (base[None, :] * (1.0 + factors)).astype(jnp.bfloat16)


def draw_biases(key, part):
    noise = jnp.clip(0.1 * jax.random.normal(jax.random.fold_in(key, 23), (NB, D), jnp.float32), -0.25, 0.25)
    return noise.astype(jnp.bfloat16)


def levels(rng, shape, cuts, least, high):
    def one(dim, shards_of):
        draws = jax.random.uniform(jax.random.fold_in(jax.random.fold_in(rng, 6), dim), (shards_of,), jnp.float32, least / len(cuts), high / len(cuts))
        return jnp.repeat(jnp.exp(draws), shape[dim] // shards_of).reshape((-1,) + (1,) * (len(shape) - dim - 1))

    gain = one(*cuts[0])
    for cut in cuts[1:]:
        gain = gain * one(*cut)
    return gain


def length_profile(number_of, total, most, lean):
    loads = [(1 << 20) // math.isqrt(grade ** lean) + 1 for grade in range(2, number_of + 1)]
    spare, counts = total - most - (number_of - 1), [1] * (number_of - 1)
    while spare > 0:
        candidates = [i for i in range(number_of - 1) if counts[i] < most]
        pool, left = sum([loads[i] for i in candidates]), spare
        for i in candidates:
            extra = min(most - counts[i], max(1, left * loads[i] // pool), spare)
            counts[i] = counts[i] + extra
            spare = spare - extra
    return np.array([most] + counts)


def uneven(stream_key, number_of, total, bound, lean):
    if number_of == 2:
        one = jax.random.randint(stream_key, (), max(1, total - bound), min(bound, total - 1) + 1)
        return jnp.stack([one, total - one])
    lengths = jnp.asarray(length_profile(number_of, total, bound, lean), jnp.int32)
    pairs = (number_of - 1) // 2
    source_of, receiver = lengths[1:1 + 2 * pairs:2], lengths[2:2 + 2 * pairs:2]
    margin = jnp.minimum(source_of - 1, bound - receiver)
    passed = jax.random.randint(jax.random.fold_in(stream_key, 1), (pairs,), 0, 1 << 20) % (margin + 1)
    lengths = lengths.at[1:1 + 2 * pairs:2].set(source_of - passed).at[2:2 + 2 * pairs:2].set(receiver + passed)
    return lengths[jax.random.permutation(jax.random.fold_in(stream_key, 2), number_of)]


def bell_draw(rng, shape, scale, most, shards=(), kind=jnp.bfloat16):
    level = levels(rng, shape, shards, -0.22, 0.18) if shards else 1.0
    entries = jax.random.normal(rng, shape, jnp.float32) * scale * level
    return jnp.minimum(jnp.maximum(entries, -most), most).astype(kind)


def setup_inputs(seed: int = 0) -> dict:
    arg_keys = jax.random.split(jax.random.key(seed), 23)
    return {
        "inputs": bell_draw(arg_keys[0], (TOKENS, D), 1.0, 6.0, ((0, 32),)),
        "targets": bell_draw(arg_keys[1], (TOKENS, D), 1.0, 6.0, ((0, 32),)),
        "valid_mask": draw_valid_mask(jax.random.fold_in(arg_keys[22], 71), 0),
        "block_seq": jnp.searchsorted(jnp.cumsum(uneven(arg_keys[3], SEQS, N_CTX, MOST, 1)), jnp.arange(N_CTX), side="right").astype(jnp.int32),
        "w_qkv": bell_draw(arg_keys[4], (D, 3 * D), D ** -0.5, 0.25, ((0, 2),)),
        "w_out": bell_draw(arg_keys[5], (D, D), (D // 16) ** -0.5, 1.0, ((0, 2),)),
        "w_up": bell_draw(arg_keys[6], (D, FF), D ** -0.5, 0.25, ((0, 2),)),
        "w_down": bell_draw(arg_keys[7], (FF, D), FF ** -0.5, 0.125, ((0, 2),)),
        "norm_gains": draw_norm_gains(jax.random.fold_in(arg_keys[22], 71), 0),
        "biases": draw_biases(jax.random.fold_in(arg_keys[22], 71), 0),
        "first_qkv": bell_draw(arg_keys[10], (D, 3 * D), (0.0011 / PARAMS ** 0.5), 9.5367431640625e-06, ((0, 2),), jnp.float32),
        "first_out": bell_draw(arg_keys[11], (D, D), (0.0011 / PARAMS ** 0.5), 9.5367431640625e-06, ((0, 2),), jnp.float32),
        "first_up": bell_draw(arg_keys[12], (D, FF), (0.0011 / PARAMS ** 0.5), 9.5367431640625e-06, ((0, 2),), jnp.float32),
        "first_down": bell_draw(arg_keys[13], (FF, D), (0.0011 / PARAMS ** 0.5), 9.5367431640625e-06, ((0, 2),), jnp.float32),
        "first_gains": bell_draw(arg_keys[14], (2, D), (0.0011 / PARAMS ** 0.5), 9.5367431640625e-06, ((1, 2),), jnp.float32),
        "first_biases": bell_draw(arg_keys[15], (NB, D), (0.0011 / PARAMS ** 0.5), 9.5367431640625e-06, ((1, 2),), jnp.float32),
        "second_qkv": jnp.clip(jnp.exp(math.log(6.662707278254354e-12) - 1.3768157 * jax.random.uniform(arg_keys[16], (D, 3 * D), jnp.float32) ** levels(arg_keys[16], (D, 3 * D), ((0, 2),), -0.2, 0.2)), 1.6815403236503101e-12, 6.662707278254354e-12),
        "second_out": jnp.clip(jnp.exp(math.log(6.662707278254354e-12) - 1.3768157 * jax.random.uniform(arg_keys[17], (D, D), jnp.float32) ** levels(arg_keys[17], (D, D), ((0, 2),), -0.2, 0.2)), 1.6815403236503101e-12, 6.662707278254354e-12),
        "second_up": jnp.clip(jnp.exp(math.log(6.662707278254354e-12) - 1.3768157 * jax.random.uniform(arg_keys[18], (D, FF), jnp.float32) ** levels(arg_keys[18], (D, FF), ((0, 2),), -0.2, 0.2)), 1.6815403236503101e-12, 6.662707278254354e-12),
        "second_down": jnp.clip(jnp.exp(math.log(6.662707278254354e-12) - 1.3768157 * jax.random.uniform(arg_keys[19], (FF, D), jnp.float32) ** levels(arg_keys[19], (FF, D), ((0, 2),), -0.2, 0.2)), 1.6815403236503101e-12, 6.662707278254354e-12),
        "second_gains": jnp.clip(jnp.exp(math.log(6.662707278254354e-12) - 1.3768157 * jax.random.uniform(arg_keys[20], (2, D), jnp.float32) ** levels(arg_keys[20], (2, D), ((1, 2),), -0.2, 0.2)), 1.6815403236503101e-12, 6.662707278254354e-12),
        "second_biases": jnp.clip(jnp.exp(math.log(6.662707278254354e-12) - 1.3768157 * jax.random.uniform(arg_keys[21], (NB, D), jnp.float32) ** levels(arg_keys[21], (NB, D), ((1, 2),), -0.2, 0.2)), 1.6815403236503101e-12, 6.662707278254354e-12),
    }


@jax.custom_vjp
def low(v):
    return lax.optimization_barrier(v.astype(jnp.bfloat16)).astype(jnp.float32)

@jax.custom_vjp
def low_back(v):
    return v

def low_keep(v):
    return (low(v), None)

def low_pass(kept, grad):
    return (grad,)

def back_keep(v):
    return (v, None)

def back_low(kept, grad):
    return (low(grad),)
low.defvjp(low_keep, low_pass)
low_back.defvjp(back_keep, back_low)
norm_floor = 1e-05
first_decay = 0.9
second_decay = 0.95
adam_floor = 1e-08
learn_rate = 0.02
weight_decay = 0.1
clip_limit = 0.01
very_low = -1e+30
highest = lax.Precision.HIGHEST

def matmul(left, right):
    return jnp.dot(left, right, precision=highest, preferred_element_type=jnp.float32)

def layer_norm(row_data, gain_row, offset):
    center = row_data - lax.optimization_barrier(jnp.mean(row_data, axis=-1, keepdims=True))
    spread = lax.optimization_barrier(jnp.mean(center * center, axis=-1, keepdims=True))
    return center * lax.rsqrt(spread + norm_floor) * gain_row + offset

def attention(queries, key_rows, value_rows, block_seq):
    window = MOST * BLOCK
    padding = jnp.zeros(((MOST - 1) * BLOCK, D), jnp.float32)
    key_pad = jnp.concatenate([padding, key_rows], 0)
    value_pad = jnp.concatenate([padding, value_rows], 0)
    scale_value = HD ** (-0.5)

    def one_block(block_index):
        row_start = (block_index * BLOCK).astype(jnp.int32)
        q_block = lax.dynamic_slice_in_dim(queries, row_start, BLOCK, 0).reshape(BLOCK, H, HD)
        k_block = lax.dynamic_slice_in_dim(key_pad, row_start, window, 0).reshape(window, H, HD)
        v_block = lax.dynamic_slice_in_dim(value_pad, row_start, window, 0).reshape(window, H, HD)
        scores = low_back(jnp.einsum('qhd,khd->hqk', q_block, k_block, precision=highest) * scale_value)
        key_pos = (block_index - MOST + 1) * BLOCK + jnp.arange(window, dtype=jnp.int32)
        query_pos = block_index * BLOCK + jnp.arange(BLOCK, dtype=jnp.int32)
        key_owner = jnp.clip(key_pos // BLOCK, 0, N_CTX - 1).astype(jnp.int32)
        same_seq = (block_seq[key_owner] == block_seq[block_index]) & (key_pos >= 0)
        visible = same_seq[None, :] & (key_pos[None, :] <= query_pos[:, None])
        scores = jnp.where(visible[None], scores, very_low)
        weights = low(jax.nn.softmax(scores, axis=-1))
        mixed_rows = jnp.einsum('hqk,khd->qhd', weights, v_block, precision=highest)
        return mixed_rows.reshape(BLOCK, D)
    blocks = lax.map(jax.checkpoint(one_block), jnp.arange(N_CTX, dtype=jnp.int32))
    return blocks.reshape(TOKENS, D)

def forward(inputs32, w_qkv, w_out, w_up, w_down, norm_gains, biases, block_seq):
    normed = low(layer_norm(inputs32, norm_gains[0], biases[0]))
    zero_bias = jnp.zeros((D,), jnp.float32)
    qkv_bias = jnp.concatenate([biases[1], zero_bias, biases[2]])
    projected = low(low_back(matmul(normed, w_qkv) + qkv_bias))
    attended = attention(projected[:, :D], projected[:, D:2 * D], projected[:, 2 * D:], block_seq)
    attended = low(low_back(attended))
    hidden = inputs32 + low_back(matmul(attended, w_out)) + biases[3]
    normed_two = low(layer_norm(hidden, norm_gains[1], biases[4]))
    up_bias = biases[6:].reshape(FF)
    lifted = low_back(matmul(normed_two, w_up) + up_bias)
    active = low(jax.nn.gelu(lifted, approximate=True))
    return hidden + low_back(matmul(active, w_down)) + biases[5]

def adam_step(weight, gradient, first_old, second_old, scale_back, decay_rate):
    clipped = gradient * scale_back
    new_first = first_decay * first_old + (1.0 - first_decay) * clipped
    new_second = second_decay * second_old + (1.0 - second_decay) * clipped * clipped
    first_hat = new_first / (1.0 - first_decay ** STEP)
    second_hat = new_second / (1.0 - second_decay ** STEP)
    update = -learn_rate * (first_hat / (jnp.sqrt(second_hat) + adam_floor) + decay_rate * weight)
    return (new_first, new_second, update)

def reference(inputs, targets, valid_mask, block_seq, w_qkv, w_out, w_up, w_down, norm_gains, biases, first_qkv, first_out, first_up, first_down, first_gains, first_biases, second_qkv, second_out, second_up, second_down, second_gains, second_biases):
    inputs32 = inputs.astype(jnp.float32)
    targets32 = targets.astype(jnp.float32)
    valid_rows = valid_mask.astype(jnp.float32)
    valid_count = jnp.sum(valid_rows)
    params = [w_qkv.astype(jnp.float32), w_out.astype(jnp.float32), w_up.astype(jnp.float32), w_down.astype(jnp.float32), norm_gains.astype(jnp.float32), biases.astype(jnp.float32)]

    def loss_of(inputs_f, qkv_f, out_f, up_f, down_f, gains_f, biases_f):
        out_f32 = forward(inputs_f, qkv_f, out_f, up_f, down_f, gains_f, biases_f, block_seq)
        error = out_f32 - targets32
        loss_value = jnp.sum(valid_rows[:, None] * error * error) * (0.5 * TOKENS) / valid_count
        return (loss_value, out_f32)
    loss_value, pullback, out_f32 = jax.vjp(loss_of, inputs32, *params, has_aux=True)
    grads = pullback(jnp.ones((), jnp.float32))
    grad_inputs = grads[0]
    weight_grads = grads[1:]
    sumsq = jnp.zeros((), jnp.float32)
    for gradient in weight_grads:
        sumsq = sumsq + jnp.sum(gradient * gradient)
    grad_norm = jnp.sqrt(sumsq) / TOKENS
    clip_factor = jnp.minimum(1.0, clip_limit / grad_norm)
    scale_back = clip_factor / TOKENS
    firsts = [first_qkv, first_out, first_up, first_down, first_gains, first_biases]
    seconds = [second_qkv, second_out, second_up, second_down, second_gains, second_biases]
    decays = [weight_decay, weight_decay, weight_decay, weight_decay, 0.0, 0.0]
    results = [adam_step(params[index], weight_grads[index], firsts[index], seconds[index], scale_back, decays[index]) for index in range(6)]
    return (out_f32.astype(jnp.bfloat16), grad_inputs, weight_grads[0], weight_grads[1], weight_grads[2], weight_grads[3], weight_grads[4], weight_grads[5], grad_norm, results[0][0], results[1][0], results[2][0], results[3][0], results[4][0], results[5][0], results[0][1], results[1][1], results[2][1], results[3][1], results[4][1], results[5][1], results[0][2], results[1][2], results[2][2], results[3][2], results[4][2], results[5][2])
```

```python
import functools

import jax
import jax.numpy as jnp
from jax import lax
from jax.experimental import pallas as pl
from jax.experimental.pallas import tpu as pltpu
from jax.sharding import PartitionSpec as P

HD = 64
STEP = 10

very_low = -1e30
norm_floor = 1e-05
first_decay = 0.9
second_decay = 0.95
adam_floor = 1e-08
learn_rate = 0.02
weight_decay = 0.1
clip_limit = 0.01

bf16 = jnp.bfloat16
f32 = jnp.float32
NN = (((1,), (0,)), ((), ()))
NT = (((1,), (1,)), ((), ()))


def mxu(left, right, dims):
    return lax.dot_general(left, right, dims, preferred_element_type=f32)


def below_diagonal(scores):
    key_pos = lax.broadcasted_iota(jnp.int32, scores.shape, 0)
    query_pos = lax.broadcasted_iota(jnp.int32, scores.shape, 1)
    return jnp.where(key_pos <= query_pos, scores, very_low)


def column_sum(values):
    return jnp.sum(values, axis=0, keepdims=True)


def column_max(values):
    return jnp.max(values, axis=0, keepdims=True)


def attend_kernel(starts, core, qkv, other_kv, *refs, group, with_prev):
    if with_prev:
        prev_own, prev_other, out, log_total, kv_rows, q_pad, acc, high, total = refs
    else:
        out, log_total, kv_rows, q_pad, acc, high, total = refs
    tokens = q_pad.shape[1]
    for place in range(group):
        kv_rows[0, place] = qkv[place, HD:, :].T
        kv_rows[1, place] = other_kv[place].T
        if with_prev:
            kv_rows[2, place] = prev_own[place].T
            kv_rows[3, place] = prev_other[place].T
    q_pad[HD:, :] = jnp.zeros((HD, tokens), bf16)

    def values_of(kind, place):
        if kind == 0:
            return qkv[place, 2 * HD :, :]
        return (other_kv, prev_own, prev_other)[kind - 1][place, HD:, :] if with_prev else other_kv[place, HD:, :]

    def take(kinds, place, masked):
        scores = [mxu(kv_rows[kind, place], q_pad[...], NN) for kind in kinds]
        if masked:
            scores = [below_diagonal(one) for one in scores]
        old = high[...]
        new = functools.reduce(jnp.maximum, [column_max(one) for one in scores], old)
        shrink = jnp.exp(old - new)
        probs = [jnp.exp(one - new) for one in scores]
        total[...] = total[...] * shrink + sum(column_sum(one) for one in probs)
        acc[...] = acc[...] * shrink + sum(
            mxu(values_of(kind, place), one.astype(bf16), NN) for kind, one in zip(kinds, probs)
        )
        high[...] = new

    def loop(kinds, first, last):
        def body(place, nothing):
            take(kinds, place, False)
            return nothing

        lax.fori_loop(first, last, body, 0)

    def chunk(place, nothing):
        q_pad[:HD, :] = qkv[place, :HD, :] * bf16(HD**-0.5)
        high[...] = jnp.full(high.shape, very_low, f32)
        total[...] = jnp.zeros(total.shape, f32)
        acc[...] = jnp.zeros(acc.shape, f32)
        take((0,), place, True)
        loop((1,), place, place + core[0])
        start = starts[place]
        loop((0, 1), jnp.maximum(start - group, 0), place)
        if with_prev:
            loop((2, 3), jnp.minimum(start, group), group)
        out[place] = acc[...] * (1.0 / total[...])
        log_total[place] = high[...] + jnp.log(total[...])
        return nothing

    lax.fori_loop(0, group, chunk, 0)


def attend_back_kernel(starts, core, qkv, other_kv, *refs, group, with_prev):
    if with_prev:
        prev_own, prev_other = refs[:2]
        refs = refs[2:]
    d_out, out, log_total, d_query, d_kv, kv_rows, q_pad, d_pad, d_kv_sum, d_query_sum = refs
    tokens = q_pad.shape[1]
    for place in range(group):
        kv_rows[0, place] = qkv[place, HD:, :].T
        kv_rows[1, place] = other_kv[place].T
        if with_prev:
            kv_rows[2, place] = prev_own[place].T
            kv_rows[3, place] = prev_other[place].T
    q_pad[HD:, :] = jnp.zeros((HD, tokens), bf16)
    d_pad[:HD, :] = jnp.zeros((HD, tokens), bf16)
    d_kv_sum[...] = jnp.zeros(d_kv_sum.shape, f32)

    def keys_of(kind, place):
        if kind == 0:
            return qkv[place, HD : 2 * HD, :]
        return (other_kv, prev_own, prev_other)[kind - 1][place, :HD, :] if with_prev else other_kv[place, :HD, :]

    def tile(kind, place, masked, delta, log_row):
        rows = kv_rows[kind, place]
        scores = mxu(rows, q_pad[...], NN)
        if masked:
            scores = below_diagonal(scores)
        probs = jnp.exp(scores - log_row)
        d_probs = mxu(rows, d_pad[...], NN)
        d_scores = (probs * (d_probs - delta)).astype(bf16)
        d_kv_sum[kind, place] += mxu(q_pad[...], d_scores, NT) + mxu(d_pad[...], probs.astype(bf16), NT)
        return mxu(keys_of(kind, place), d_scores, NN)

    def chunk(place, nothing):
        q_pad[:HD, :] = qkv[place, :HD, :] * bf16(HD**-0.5)
        d_here = d_out[place]
        d_pad[HD:, :] = d_here
        delta = column_sum(d_here.astype(f32) * out[place])
        log_row = log_total[place]

        def loop(kinds, first, last):
            def body(key_place, nothing):
                d_query_sum[...] += sum(tile(kind, key_place, False, delta, log_row) for kind in kinds)
                return nothing

            lax.fori_loop(first, last, body, 0)

        d_query_sum[...] = tile(0, place, True, delta, log_row)
        loop((1,), place, place + core[0])
        start = starts[place]
        loop((0, 1), jnp.maximum(start - group, 0), place)
        if with_prev:
            loop((2, 3), jnp.minimum(start, group), group)
        d_query[place] = (d_query_sum[...] * HD**-0.5).astype(bf16)
        return nothing

    lax.fori_loop(0, group, chunk, 0)
    d_kv[...] = d_kv_sum[...].astype(bf16)


in_vmem = pl.BlockSpec(memory_space=pltpu.VMEM)
in_smem = pl.BlockSpec(memory_space=pltpu.SMEM)


def attend(starts, core, qkv, *kv):
    group, _, tokens = qkv.shape
    with_prev = len(kv) > 1
    kinds = 4 if with_prev else 2
    return pl.pallas_call(
        functools.partial(attend_kernel, group=group, with_prev=with_prev),
        out_shape=(
            jax.ShapeDtypeStruct((group, HD, tokens), f32),
            jax.ShapeDtypeStruct((group, 1, tokens), f32),
        ),
        in_specs=[in_smem, in_smem] + [in_vmem] * (1 + len(kv)),
        out_specs=(in_vmem, in_vmem),
        scratch_shapes=[
            pltpu.VMEM((kinds, group, tokens, 2 * HD), bf16),
            pltpu.VMEM((2 * HD, tokens), bf16),
            pltpu.VMEM((HD, tokens), f32),
            pltpu.VMEM((1, tokens), f32),
            pltpu.VMEM((1, tokens), f32),
        ],
        cost_estimate=pl.CostEstimate(flops=36 * 4 * 2**20 * 64, bytes_accessed=5 * 2**20, transcendentals=2**24),
        compiler_params=pltpu.CompilerParams(vmem_limit_bytes=56 * 2**20),
        name="attend",
    )(starts, core, qkv, *kv)


def attend_back(starts, core, qkv, kv, d_out, out, log_total):
    group, _, tokens = qkv.shape
    with_prev = len(kv) > 1
    kinds = 4 if with_prev else 2
    return pl.pallas_call(
        functools.partial(attend_back_kernel, group=group, with_prev=with_prev),
        out_shape=(
            jax.ShapeDtypeStruct((group, HD, tokens), bf16),
            jax.ShapeDtypeStruct((kinds, group, 2 * HD, tokens), bf16),
        ),
        in_specs=[in_smem, in_smem] + [in_vmem] * (4 + len(kv)),
        out_specs=(in_vmem, in_vmem),
        scratch_shapes=[
            pltpu.VMEM((kinds, group, tokens, 2 * HD), bf16),
            pltpu.VMEM((2 * HD, tokens), bf16),
            pltpu.VMEM((2 * HD, tokens), bf16),
            pltpu.VMEM((kinds, group, 2 * HD, tokens), f32),
            pltpu.VMEM((HD, tokens), f32),
        ],
        cost_estimate=pl.CostEstimate(flops=36 * 10 * 2**20 * 64, bytes_accessed=8 * 2**20, transcendentals=2**24),
        compiler_params=pltpu.CompilerParams(vmem_limit_bytes=56 * 2**20),
        name="attend_back",
    )(starts, core, qkv, *kv, d_out, out, log_total)


def layer_norm(row_data, gain_row, offset):
    center = row_data - jnp.mean(row_data, axis=-1, keepdims=True)
    spread = jnp.mean(center * center, axis=-1, keepdims=True)
    return center * lax.rsqrt(spread + norm_floor) * gain_row + offset


def gelu_tanh(values):
    return jax.nn.gelu(values, approximate=True)


def adam_step(weight, gradient, first_old, second_old, scale_back, decay_rate):
    weight32 = weight.astype(f32)
    clipped = gradient * scale_back
    new_first = first_decay * first_old + (1.0 - first_decay) * clipped
    new_second = second_decay * second_old + (1.0 - second_decay) * clipped * clipped
    first_hat = new_first / (1.0 - first_decay**STEP)
    second_hat = new_second / (1.0 - second_decay**STEP)
    update = -learn_rate * (first_hat / (jnp.sqrt(second_hat) + adam_floor) + decay_rate * weight32)
    return (new_first, new_second, update)


def from_other_core(value):
    return lax.ppermute(value, "fsdp", [(0, 1), (1, 0)])


def whole_of(value, axis):
    other = from_other_core(value)
    first = lax.axis_index("fsdp") == 0
    return jnp.concatenate([jnp.where(first, value, other), jnp.where(first, other, value)], axis)


def swap_ctx(value, bit):
    size = lax.axis_size("ctx")
    return lax.ppermute(value, "ctx", [(i, i ^ bit) for i in range(size)])


def across_groups(value, group, step_type):
    bit = group
    while bit < lax.axis_size("ctx"):
        sent = value.astype(step_type)
        value = sent.astype(f32) + swap_ctx(sent, bit).astype(f32)
        bit *= 2
    return value


def sum_small(value):
    bit = 1
    value = value + from_other_core(value)
    while bit < lax.axis_size("ctx"):
        value = value + swap_ctx(value, bit)
        bit *= 2
    return value


def per_device(
    inputs,
    targets,
    valid_mask,
    block_seq,
    w_qkv,
    w_out,
    w_up,
    w_down,
    norm_gains,
    biases,
    first_qkv,
    first_out,
    first_up,
    first_down,
    first_gains,
    first_biases,
    second_qkv,
    second_out,
    second_up,
    second_down,
    second_gains,
    second_biases,
):
    rows_here, width = inputs.shape
    group = width // HD
    ctx_size = lax.axis_size("ctx")
    block_rows = rows_here * 2
    total_rows = float(block_rows * ctx_size)
    ctx_place = lax.axis_index("ctx")
    core_place = lax.axis_index("fsdp")
    members = [[first + i for i in range(group)] for first in range(0, ctx_size, group)]

    def exchange(value):
        return lax.all_to_all(value, "ctx", 0, 0, axis_index_groups=members, tiled=True)

    full_qkv, full_out, full_up, full_down = (
        whole_of(w_qkv, 0),
        whole_of(w_out, 0),
        whole_of(w_up, 0),
        whole_of(w_down, 0),
    )
    vectors = whole_of(jnp.concatenate([norm_gains, biases], 0), 1).astype(f32)
    gains32 = vectors[:2]
    biases32 = vectors[2:]
    valid_rows = valid_mask.astype(f32)
    valid_count = sum_small(jnp.full((8, 128), jnp.sum(valid_rows), f32))[0, 0]

    inputs32 = inputs.astype(f32)
    normed32, first_pull = jax.vjp(layer_norm, inputs32, gains32[0], biases32[0])
    normed = normed32.astype(bf16)
    qkv_bias = jnp.concatenate([biases32[1], jnp.zeros((width,), f32), biases32[2]])
    projected = lax.dot_general(full_qkv, normed, (((0,), (1,)), ((), ())), preferred_element_type=f32)
    projected = (projected + qkv_bias[:, None]).astype(bf16)
    by_head = projected.reshape(3, group, HD, rows_here).transpose(1, 0, 2, 3)
    qkv = exchange(by_head.reshape(group, 3 * HD, rows_here))
    own_kv = qkv[:, HD:]
    other_kv = from_other_core(own_kv)

    first_block = (ctx_place // group) * group
    own_seq = lax.dynamic_slice_in_dim(block_seq, first_block, group, 0)
    starts = jnp.sum((block_seq[None, :] < own_seq[:, None]).astype(jnp.int32), axis=1)
    starts = jnp.maximum(starts - first_block + group, 0)
    core = jnp.full((1,), core_place, jnp.int32)
    edges = list(range(group, ctx_size, group))
    straddles = jnp.zeros((), bool)
    for edge in edges:
        straddles = straddles | (block_seq[edge - 1] == block_seq[edge])

    def forward_with(own, other):
        prev_own = lax.ppermute(own, "ctx", [(i, i + group) for i in range(ctx_size - group)])
        prev_other = from_other_core(prev_own)
        return attend(starts, core, qkv, other, prev_own, prev_other) + (prev_own, prev_other)

    def forward_without(own, other):
        nothing = jnp.zeros(own.shape, bf16)
        return attend(starts, core, qkv, other) + (nothing, nothing)

    mixed, log_total, prev_own, prev_other = lax.cond(straddles, forward_with, forward_without, own_kv, other_kv)
    attended = exchange(mixed.astype(bf16)).reshape(width, rows_here)

    hidden = (
        inputs32
        + lax.dot_general(attended, full_out, (((0,), (0,)), ((), ())), preferred_element_type=f32)
        + biases32[3]
    )
    normed_two32, second_pull = jax.vjp(layer_norm, hidden, gains32[1], biases32[4])
    normed_two = normed_two32.astype(bf16)
    up_bias = biases32[6:].reshape(-1)
    lifted = jnp.dot(normed_two, full_up, preferred_element_type=f32) + up_bias
    active32, gelu_pull = jax.vjp(gelu_tanh, lifted)
    active = active32.astype(bf16)
    out_f32 = hidden + jnp.dot(active, full_down, preferred_element_type=f32) + biases32[5]
    error = out_f32 - targets.astype(f32)
    d_out = valid_rows[:, None] * error * (total_rows / valid_count)
    d_out_low = d_out.astype(bf16)
    grad_down = jnp.einsum("tf,td->fd", active, d_out_low, preferred_element_type=f32)
    d_active = jnp.einsum("td,fd->tf", d_out_low, full_down, preferred_element_type=f32)
    d_lifted = gelu_pull(d_active)[0].astype(bf16)
    grad_up = jnp.einsum("td,tf->df", normed_two, d_lifted, preferred_element_type=f32)
    d_normed_two = jnp.einsum("tf,df->td", d_lifted, full_up, preferred_element_type=f32)
    d_hidden_part, grad_gain_two, grad_offset_two = second_pull(d_normed_two)
    d_hidden = d_out + d_hidden_part
    d_hidden_low = d_hidden.astype(bf16)
    grad_out = jnp.dot(attended, d_hidden_low, preferred_element_type=f32)
    d_attended = jnp.einsum("ab,tb->at", full_out, d_hidden_low, preferred_element_type=f32).astype(bf16)
    d_mixed = exchange(d_attended.reshape(group, HD, rows_here))

    def backward_with(d_mixed):
        d_query, d_kv = attend_back(starts, core, qkv, (other_kv, prev_own, prev_other), d_mixed, mixed, log_total)
        d_prev = d_kv[2].astype(f32) + from_other_core(d_kv[3]).astype(f32)
        d_prev = lax.ppermute(d_prev.astype(bf16), "ctx", [(i + group, i) for i in range(ctx_size - group)])
        return d_query, d_kv[0], d_kv[1], d_prev

    def backward_without(d_mixed):
        d_query, d_kv = attend_back(starts, core, qkv, (other_kv,), d_mixed, mixed, log_total)
        return d_query, d_kv[0], d_kv[1], jnp.zeros(other_kv.shape, bf16)

    d_query, d_own, d_other, d_prev = lax.cond(straddles, backward_with, backward_without, d_mixed)
    d_kv = d_own.astype(f32) + from_other_core(d_other).astype(f32) + d_prev.astype(f32)
    d_heads = exchange(jnp.concatenate([d_query, d_kv.astype(bf16)], 1))
    d_projected = d_heads.reshape(group, 3, HD, rows_here).transpose(1, 0, 2, 3).reshape(3 * width, rows_here)
    grad_qkv = jnp.einsum("td,et->de", normed, d_projected, preferred_element_type=f32)
    d_normed = jnp.einsum("et,de->td", d_projected, full_qkv, preferred_element_type=f32)
    d_inputs_part, grad_gain_one, grad_offset_one = first_pull(d_normed)
    grad_inputs = d_hidden + d_inputs_part
    d_bias = jnp.sum(d_projected.astype(f32), axis=1)
    small = jnp.concatenate(
        [
            jnp.stack(
                [
                    grad_gain_one,
                    grad_gain_two,
                    grad_offset_one,
                    d_bias[:width],
                    d_bias[2 * width :],
                    jnp.sum(d_hidden, axis=0),
                    grad_offset_two,
                    jnp.sum(d_out, axis=0),
                ]
            ),
            jnp.sum(d_lifted.astype(f32), axis=0).reshape(-1, width),
        ],
        0,
    )

    def reduced(gradient):
        half = gradient.shape[0] // 2
        sent = lax.dynamic_slice_in_dim(gradient, (1 - core_place) * half, half, 0).astype(bf16)
        kept = lax.dynamic_slice_in_dim(gradient, core_place * half, half, 0)
        pair = (kept + from_other_core(sent).astype(f32)).astype(bf16)
        shares = exchange(pair.reshape(group, half // group, -1))
        mine = across_groups(jnp.sum(shares.astype(f32), axis=0), group, bf16).astype(bf16)
        spread = exchange(jnp.broadcast_to(mine[None], (group,) + mine.shape))
        return spread.reshape(half, -1).astype(f32)

    small = sum_small(small)
    small_half = lax.dynamic_slice_in_dim(small, core_place * (width // 2), width // 2, 1)
    shares = [
        reduced(grad_qkv),
        reduced(grad_out),
        reduced(grad_up),
        reduced(grad_down),
        small_half[:2],
        small_half[2:],
    ]
    local_squares = jnp.zeros((), f32)
    for gradient in shares:
        local_squares = local_squares + jnp.sum(gradient * gradient)
    squares = jnp.full((8, 128), local_squares, f32)
    total_squares = (squares + from_other_core(squares))[0, 0]
    grad_norm = jnp.sqrt(total_squares) / total_rows
    clip_factor = jnp.minimum(1.0, clip_limit / grad_norm)
    scale_back = clip_factor / total_rows
    weights_here = [w_qkv, w_out, w_up, w_down, norm_gains, biases]
    firsts = [first_qkv, first_out, first_up, first_down, first_gains, first_biases]
    seconds = [second_qkv, second_out, second_up, second_down, second_gains, second_biases]
    decays = [weight_decay, weight_decay, weight_decay, weight_decay, 0.0, 0.0]
    results = [
        adam_step(weights_here[i], shares[i], firsts[i], seconds[i], scale_back, decays[i]) for i in range(6)
    ]
    return (
        (out_f32.astype(bf16), grad_inputs)
        + tuple(shares)
        + (grad_norm,)
        + tuple(results[i][0] for i in range(6))
        + tuple(results[i][1] for i in range(6))
        + tuple(results[i][2] for i in range(6))
    )


def solution(mesh):
    tokens = P(("ctx", "fsdp"), None)
    weight = P("fsdp", None)
    vector = P(None, "fsdp")
    params = (weight, weight, weight, weight, vector, vector)
    in_specs = (tokens, tokens, P(("ctx", "fsdp")), P()) + params * 3
    out_specs = (tokens, tokens) + params + (P(),) + params * 3
    return jax.shard_map(per_device, mesh=mesh, in_specs=in_specs, out_specs=out_specs, check_vma=False)
```

```python
import functools
import math

import jax
import jax.numpy as jnp
from jax import lax
from jax.experimental import pallas as pl
from jax.experimental.pallas import tpu as pltpu
from jax.sharding import PartitionSpec as P

HD = 64
STEP = 10

very_low = -1e30
norm_floor = 1e-05
first_decay = 0.9
second_decay = 0.95
adam_floor = 1e-08
learn_rate = 0.02
weight_decay = 0.1
clip_limit = 0.01
gelu_scale = (2.0 / math.pi) ** 0.5
gelu_cubic = 0.044715

BASE_LIMIT = 1e20
ONES = 16

bf16 = jnp.bfloat16
f32 = jnp.float32
NN = (((1,), (0,)), ((), ()))
NT = (((1,), (1,)), ((), ()))
TN = (((0,), (0,)), ((), ()))


def mxu(left, right, dims):
    return lax.dot_general(left, right, dims, preferred_element_type=f32)


def below_diagonal(scores):
    key_pos = lax.broadcasted_iota(jnp.int32, scores.shape, 0)
    query_pos = lax.broadcasted_iota(jnp.int32, scores.shape, 1)
    return jnp.where(key_pos <= query_pos, scores, very_low)


def column_sum(values):
    return jnp.sum(values, axis=0, keepdims=True)


def column_max(values):
    return jnp.max(values, axis=0, keepdims=True)


def attend_kernel(starts, core, qkv, other_kv, *refs, group, with_prev):
    if with_prev:
        prev_own, prev_other, out, log_total, kv_rows, v_ones, q_pad, acc, high = refs
    else:
        out, log_total, kv_rows, v_ones, q_pad, acc, high = refs
    tokens = q_pad.shape[1]
    ones = jnp.ones((ONES, tokens), bf16)

    def load(kind, place, kv):
        kv_rows[kind, place] = kv.T
        v_ones[kind, place, :HD, :] = kv[HD:]
        v_ones[kind, place, HD:, :] = ones

    for place in range(group):
        load(0, place, qkv[place, HD:, :])
        load(1, place, other_kv[place])
        if with_prev:
            load(2, place, prev_own[place])
            load(3, place, prev_other[place])
    q_pad[HD:, :] = jnp.zeros((HD, tokens), bf16)

    def score(kind, place):
        return mxu(kv_rows[kind, place], q_pad[...], NN)

    def weigh(kind, place, scores, base):
        return mxu(v_ones[kind, place], jnp.exp(scores - base).astype(bf16), NN)

    def chunk(place, nothing):
        q_pad[:HD, :] = qkv[place, :HD, :] * bf16(HD**-0.5)
        start = starts[place]

        def over(visit):
            def loop(kinds, first, last):
                def body(key_place, nothing):
                    visit(kinds, key_place)
                    return nothing

                lax.fori_loop(first, last, body, 0)

            loop((1,), place, place + core[0])
            loop((0, 1), jnp.maximum(start - group, 0), place)
            if with_prev:
                loop((2, 3), jnp.minimum(start, group), group)

        scores = below_diagonal(score(0, place))
        base = column_max(scores)
        high[...] = base
        acc[...] = weigh(0, place, scores, base)

        def add(kinds, key_place):
            base = high[...]
            acc[...] += sum(weigh(kind, key_place, score(kind, key_place), base) for kind in kinds)

        over(add)

        @pl.when(jnp.logical_not(jnp.max(acc[HD : HD + 1, :]) < BASE_LIMIT))
        def _():
            acc[...] = weigh(0, place, below_diagonal(score(0, place)), high[...])

            def rescale(kinds, key_place):
                for kind in kinds:
                    scores = score(kind, key_place)
                    old = high[...]
                    new = jnp.maximum(old, column_max(scores))
                    acc[...] = acc[...] * jnp.exp(old - new) + weigh(kind, key_place, scores, new)
                    high[...] = new

            over(rescale)

        total = acc[HD : HD + 1, :]
        out[place] = acc[:HD, :] * (1.0 / total)
        log_total[place] = high[...] + jnp.log(total)
        return nothing

    lax.fori_loop(0, group, chunk, 0)


def attend_back_kernel(starts, core, qkv, other_kv, *refs, group, with_prev):
    if with_prev:
        prev_own, prev_other = refs[:2]
        refs = refs[2:]
    d_out, out, log_total, d_query, d_kv, kv_rows, q_pad, d_pad, d_kv_sum, d_query_sum = refs
    tokens = q_pad.shape[1]
    for place in range(group):
        kv_rows[0, place] = qkv[place, HD:, :].T
        kv_rows[1, place] = other_kv[place].T
        if with_prev:
            kv_rows[2, place] = prev_own[place].T
            kv_rows[3, place] = prev_other[place].T
    q_pad[HD:, :] = jnp.zeros((HD, tokens), bf16)
    d_pad[:HD, :] = jnp.zeros((HD, tokens), bf16)
    d_kv_sum[...] = jnp.zeros(d_kv_sum.shape, f32)

    def keys_of(kind, place):
        if kind == 0:
            return qkv[place, HD : 2 * HD, :]
        return (other_kv, prev_own, prev_other)[kind - 1][place, :HD, :] if with_prev else other_kv[place, :HD, :]

    def tile(kind, place, masked, delta, log_row):
        rows = kv_rows[kind, place]
        scores = mxu(rows, q_pad[...], NN)
        if masked:
            scores = below_diagonal(scores)
        probs = jnp.exp(scores - log_row)
        d_probs = mxu(rows, d_pad[...], NN)
        d_scores = (probs * (d_probs - delta)).astype(bf16)
        d_kv_sum[kind, place] += mxu(q_pad[...], d_scores, NT) + mxu(d_pad[...], probs.astype(bf16), NT)
        return mxu(keys_of(kind, place), d_scores, NN)

    def chunk(place, nothing):
        q_pad[:HD, :] = qkv[place, :HD, :] * bf16(HD**-0.5)
        d_here = d_out[place]
        d_pad[HD:, :] = d_here
        delta = column_sum(d_here.astype(f32) * out[place])
        log_row = log_total[place]

        def loop(kinds, first, last):
            def body(key_place, nothing):
                d_query_sum[...] += sum(tile(kind, key_place, False, delta, log_row) for kind in kinds)
                return nothing

            lax.fori_loop(first, last, body, 0)

        d_query_sum[...] = tile(0, place, True, delta, log_row)
        loop((1,), place, place + core[0])
        start = starts[place]
        loop((0, 1), jnp.maximum(start - group, 0), place)
        if with_prev:
            loop((2, 3), jnp.minimum(start, group), group)
        d_query[place] = (d_query_sum[...] * HD**-0.5).astype(bf16)
        return nothing

    lax.fori_loop(0, group, chunk, 0)
    d_kv[...] = d_kv_sum[...].astype(bf16)


in_vmem = pl.BlockSpec(memory_space=pltpu.VMEM)
in_smem = pl.BlockSpec(memory_space=pltpu.SMEM)


def attend(starts, core, qkv, *kv):
    group, _, tokens = qkv.shape
    with_prev = len(kv) > 1
    kinds = 4 if with_prev else 2
    return pl.pallas_call(
        functools.partial(attend_kernel, group=group, with_prev=with_prev),
        out_shape=(
            jax.ShapeDtypeStruct((group, HD, tokens), f32),
            jax.ShapeDtypeStruct((group, 1, tokens), f32),
        ),
        in_specs=[in_smem, in_smem] + [in_vmem] * (1 + len(kv)),
        out_specs=(in_vmem, in_vmem),
        scratch_shapes=[
            pltpu.VMEM((kinds, group, tokens, 2 * HD), bf16),
            pltpu.VMEM((kinds, group, HD + ONES, tokens), bf16),
            pltpu.VMEM((2 * HD, tokens), bf16),
            pltpu.VMEM((HD + ONES, tokens), f32),
            pltpu.VMEM((1, tokens), f32),
        ],
        cost_estimate=pl.CostEstimate(flops=36 * 4 * 2**20 * 64, bytes_accessed=5 * 2**20, transcendentals=2**24),
        compiler_params=pltpu.CompilerParams(vmem_limit_bytes=56 * 2**20),
        name="attend",
    )(starts, core, qkv, *kv)


def attend_back(starts, core, qkv, kv, d_out, out, log_total):
    group, _, tokens = qkv.shape
    with_prev = len(kv) > 1
    kinds = 4 if with_prev else 2
    return pl.pallas_call(
        functools.partial(attend_back_kernel, group=group, with_prev=with_prev),
        out_shape=(
            jax.ShapeDtypeStruct((group, HD, tokens), bf16),
            jax.ShapeDtypeStruct((kinds, group, 2 * HD, tokens), bf16),
        ),
        in_specs=[in_smem, in_smem] + [in_vmem] * (4 + len(kv)),
        out_specs=(in_vmem, in_vmem),
        scratch_shapes=[
            pltpu.VMEM((kinds, group, tokens, 2 * HD), bf16),
            pltpu.VMEM((2 * HD, tokens), bf16),
            pltpu.VMEM((2 * HD, tokens), bf16),
            pltpu.VMEM((kinds, group, 2 * HD, tokens), f32),
            pltpu.VMEM((HD, tokens), f32),
        ],
        cost_estimate=pl.CostEstimate(flops=36 * 10 * 2**20 * 64, bytes_accessed=8 * 2**20, transcendentals=2**24),
        compiler_params=pltpu.CompilerParams(vmem_limit_bytes=56 * 2**20),
        name="attend_back",
    )(starts, core, qkv, *kv, d_out, out, log_total)


def normalize(rows):
    center = rows - jnp.mean(rows, axis=1, keepdims=True)
    inverse = lax.rsqrt(jnp.mean(center * center, axis=1, keepdims=True) + norm_floor)
    return center * inverse, inverse


def norm_back(d_rows, unit, inverse, gain):
    scaled = d_rows * gain
    first = jnp.mean(scaled, axis=1, keepdims=True)
    second = jnp.mean(scaled * unit, axis=1, keepdims=True)
    return inverse * (scaled - first - unit * second)


def span(start, size):
    return pl.ds(pl.multiple_of(start, size), size)


def feed_kernel(
    core,
    attended,
    inputs,
    targets,
    valid,
    vectors,
    out_own,
    out_other,
    up_own,
    up_other,
    down_own,
    down_other,
    outputs,
    d_hidden,
    d_hidden_low,
    d_attended,
    active,
    d_lifted,
    normed,
    d_out_low,
    small,
    hidden,
    unit,
    slope,
    acc,
    up_sum,
):
    tokens, width = inputs.shape
    half = width // 2
    f_half = down_own.shape[0]
    step = 256
    place = core[0]
    halves = ((place, out_own, up_own, down_own), (1 - place, out_other, up_other, down_other))
    hidden[...] = inputs[...].astype(f32) + vectors[5:6, :]
    for where, w_out, _, _ in halves:
        hidden[...] += mxu(attended[span(where * half, half), :], w_out[...], TN)
    unit_here, inverse = normalize(hidden[...])
    unit[...] = unit_here
    normed[...] = (unit_here * vectors[1:2, :] + vectors[6:7, :]).astype(bf16)
    for row in range(4):
        up_sum[:, row * width : (row + 1) * width] = vectors[8 + row : 9 + row, :]
    acc[...] = hidden[...] + vectors[7:8, :]
    for where, _, _, w_down in halves:

        def lift(index, nothing):
            columns = span(where * f_half + index * step, step)
            u = up_sum[:, columns]
            for other, _, w_up, _ in halves:
                u = u + mxu(normed[:, span(other * half, half)], w_up[:, columns], NN)
            square = u * u
            tanh = jnp.tanh(gelu_scale * (u + gelu_cubic * (square * u)))
            side = 0.5 * (1.0 + tanh)
            act = (u * side).astype(bf16)
            active[:, columns] = act
            slope[:, columns] = side + (0.5 * gelu_scale) * u * (1.0 - tanh * tanh) * (
                1.0 + (3.0 * gelu_cubic) * square
            )
            acc[...] += mxu(act, w_down[span(index * step, step), :], NN)
            return nothing

        lax.fori_loop(0, f_half // step, lift, 0)
    out_f32 = acc[...]
    outputs[...] = out_f32.astype(bf16)
    d_out = valid[...] * (out_f32 - targets[...].astype(f32))
    d_hidden[...] = d_out
    d_out_low[...] = d_out.astype(bf16)
    small[...] = jnp.zeros(small.shape, f32)
    small[3:4, :] = column_sum(d_out)
    acc[...] = jnp.zeros(acc.shape, f32)
    for where, _, _, w_down in halves:

        def lower(index, nothing):
            columns = span(where * f_half + index * step, step)
            d_active = mxu(d_out_low[...], w_down[span(index * step, step), :], NT)
            low = (d_active * slope[:, columns]).astype(bf16)
            d_lifted[:, columns] = low
            up_sum[:, columns] = column_sum(low.astype(f32))
            for other, _, w_up, _ in halves:
                acc[:, span(other * half, half)] += mxu(low, w_up[:, columns], NT)
            return nothing

        lax.fori_loop(0, f_half // step, lower, 0)
    for row in range(4):
        small[4 + row : 5 + row, :] = up_sum[:, row * width : (row + 1) * width]
    d_normed = acc[...]
    unit_here = unit[...]
    small[0:1, :] = column_sum(d_normed * unit_here)
    small[2:3, :] = column_sum(d_normed)
    d_rows = d_hidden[...] + norm_back(d_normed, unit_here, inverse, vectors[1:2, :])
    d_hidden[...] = d_rows
    small[1:2, :] = column_sum(d_rows)
    low = d_rows.astype(bf16)
    d_hidden_low[...] = low
    for where, w_out, _, _ in halves:
        d_attended[span(where * half, half), :] = mxu(w_out[...], low, NT).astype(bf16)
    lanes = lax.broadcasted_iota(jnp.int32, (tokens, 128), 1)
    rows = lax.broadcasted_iota(jnp.int32, (tokens, 128), 0)
    counts = column_sum(jnp.where(rows % 128 == lanes, valid[...], 0.0))
    small[8:9, :128] = counts
    small[8:9, half : half + 128] = counts


def spread_rows(target, gradient, first, rows):
    low = gradient.astype(bf16)
    for member in range(target.shape[0]):
        target[member, first : first + rows, :] = low[member * rows : (member + 1) * rows]


def feed_grads_kernel(core, active, d_out_low, normed, d_lifted, attended, d_hidden_low, small, keep, send):
    width = attended.shape[0]
    half = width // 2
    members = keep.shape[0]
    f_half = active.shape[1] // 2
    rows = f_half // members
    for target, where in ((keep, core[0]), (send, 1 - core[0])):

        def down(index, nothing):
            low = mxu(active[:, span(where * f_half + index * 2 * rows, 2 * rows)], d_out_low[...], TN).astype(bf16)
            target[2 * index, :rows, :] = low[:rows]
            target[2 * index + 1, :rows, :] = low[rows:]
            return nothing

        lax.fori_loop(0, members // 2, down, 0)
        here = span(where * half, half)
        first = rows
        for column in range(0, 2 * f_half, width):
            spread_rows(target, mxu(normed[:, here], d_lifted[:, column : column + width], TN), first, half // members)
            first += half // members
        spread_rows(target, mxu(attended[here, :], d_hidden_low[...], NN), first, half // members)
        first += half // members
        sums = jnp.concatenate([small[:, here], jnp.zeros(small[:, here].shape, f32)], 1).astype(bf16)
        for member in range(members):
            target[member, first:, :] = sums


def first_back_kernel(core, d_heads, inputs, vectors, d_hidden, own, other, d_inputs, keep, send, d_proj, d_normed):
    width = inputs.shape[1]
    half = width // 2
    members = keep.shape[0]
    place = core[0]
    for head in range(width // HD):
        for part in range(3):
            d_proj[part * width + head * HD : part * width + (head + 1) * HD, :] = d_heads[
                head, part * HD : (part + 1) * HD, :
            ]
    unit, inverse = normalize(inputs[...].astype(f32))
    normed = (unit * vectors[0:1, :] + vectors[2:3, :]).astype(bf16).T
    for where, weight in ((place, own), (1 - place, other)):
        d_normed[span(where * half, half), :] = mxu(weight[...], d_proj[...], NN)
    d_rows = d_normed[:width, :].T
    d_inputs[...] = d_hidden[...] + norm_back(d_rows, unit, inverse, vectors[0:1, :])
    gain_sum = column_sum(d_rows * unit)
    offset_sum = column_sum(d_rows)
    ones = jnp.ones((ONES, inputs.shape[0]), bf16)
    query_sum = mxu(ones, d_proj[:width], NT)[:1]
    value_sum = mxu(ones, d_proj[2 * width :], NT)[:1]
    sums = jnp.concatenate([gain_sum, offset_sum, query_sum, value_sum, jnp.zeros((ONES - 4, width), f32)], 0)
    rows = half // members
    d_normed[:ONES, :] = sums
    for part in range(3):
        gradient = mxu(normed, d_proj[part * width : (part + 1) * width], NT)
        d_normed[ONES : ONES + width, :] = gradient
        for target, where in ((keep, place), (send, 1 - place)):
            low = d_normed[pl.ds(pl.multiple_of(ONES + where * half, ONES), half), :]
            spread_rows(target, low, part * rows, rows)
    for target, where in ((keep, place), (send, 1 - place)):
        low = d_normed[:ONES, span(where * half, half)]
        low = jnp.concatenate([low, jnp.zeros(low.shape, f32)], 1).astype(bf16)
        for member in range(members):
            target[member, 3 * rows :, :] = low


def update_kernel(scales, early, late, d_raw, *refs):
    weights, firsts, seconds = refs[0:4], refs[4:8], refs[8:12]
    grad_inputs = refs[12]
    grads, new_firsts, new_seconds, steps = refs[13:17], refs[17:21], refs[21:25], refs[25:29]
    count_scale, scale_back = scales[0], scales[1]
    width = d_raw.shape[1]
    grad_inputs[...] = d_raw[...] * count_scale
    first_up = weights[3].shape[0]
    after_up = first_up + weights[2].shape[0] * (weights[2].shape[1] // width)
    place_of = ((late, 0), (early, after_up), (early, first_up), (early, 0))
    for index, (source, first) in enumerate(place_of):
        rows = weights[index].shape[0]
        for block in range(weights[index].shape[1] // width):
            columns = slice(block * width, (block + 1) * width)
            gradient = source[0, first + block * rows : first + (block + 1) * rows, :].astype(f32) * count_scale
            grads[index][:, columns] = gradient
            results = adam_step(
                weights[index][:, columns],
                gradient,
                firsts[index][:, columns],
                seconds[index][:, columns],
                scale_back,
                weight_decay,
            )
            new_firsts[index][:, columns], new_seconds[index][:, columns], steps[index][:, columns] = results


def adam_step(weight, gradient, first_old, second_old, scale_back, decay_rate):
    weight32 = weight.astype(f32)
    clipped = gradient * scale_back
    new_first = first_decay * first_old + (1.0 - first_decay) * clipped
    new_second = second_decay * second_old + (1.0 - second_decay) * clipped * clipped
    first_hat = new_first / (1.0 - first_decay**STEP)
    second_hat = new_second / (1.0 - second_decay**STEP)
    update = -learn_rate * (first_hat / (jnp.sqrt(second_hat) + adam_floor) + decay_rate * weight32)
    return (new_first, new_second, update)


roomy = pltpu.CompilerParams(vmem_limit_bytes=56 * 2**20)


def shaped(shape, kind):
    return jax.ShapeDtypeStruct(shape, kind)


def feed(core, attended, inputs, targets, valid, vectors, *weights):
    tokens, width = inputs.shape
    hidden_units = weights[2].shape[1]
    return pl.pallas_call(
        feed_kernel,
        out_shape=(
            shaped((tokens, width), bf16),
            shaped((tokens, width), f32),
            shaped((tokens, width), bf16),
            shaped((width, tokens), bf16),
            shaped((tokens, hidden_units), bf16),
            shaped((tokens, hidden_units), bf16),
            shaped((tokens, width), bf16),
            shaped((tokens, width), bf16),
            shaped((16, width), f32),
        ),
        in_specs=[in_smem] + [in_vmem] * 11,
        out_specs=(in_vmem,) * 9,
        scratch_shapes=[
            pltpu.VMEM((tokens, width), f32),
            pltpu.VMEM((tokens, width), f32),
            pltpu.VMEM((tokens, hidden_units), f32),
            pltpu.VMEM((tokens, width), f32),
            pltpu.VMEM((1, hidden_units), f32),
        ],
        cost_estimate=pl.CostEstimate(flops=10 * 2**30, bytes_accessed=14 * 2**20, transcendentals=2**20),
        compiler_params=roomy,
        name="feed",
    )(core, attended, inputs, targets, valid, vectors, *weights)


def feed_grads(group, core, *arrays):
    tokens, hidden_units = arrays[0].shape
    width = arrays[1].shape[1]
    rows = (hidden_units + width) // 2 // group + hidden_units // 2 // group + 16
    return pl.pallas_call(
        feed_grads_kernel,
        out_shape=(shaped((group, rows, width), bf16),) * 2,
        in_specs=[in_smem] + [in_vmem] * 7,
        out_specs=(in_vmem,) * 2,
        cost_estimate=pl.CostEstimate(flops=5 * 2**30, bytes_accessed=12 * 2**20, transcendentals=0),
        compiler_params=roomy,
        name="feed_grads",
    )(core, *arrays)


def first_back(group, core, d_heads, inputs, vectors, d_hidden, own, other):
    tokens, width = inputs.shape
    rows = own.shape[0] // group * 3 + 16
    return pl.pallas_call(
        first_back_kernel,
        out_shape=(shaped((tokens, width), f32),) + (shaped((group, rows, width), bf16),) * 2,
        in_specs=[in_smem] + [in_vmem] * 6,
        out_specs=(in_vmem,) * 3,
        scratch_shapes=[pltpu.VMEM((3 * width, tokens), bf16), pltpu.VMEM((width + 16, tokens), f32)],
        cost_estimate=pl.CostEstimate(flops=4 * 2**30, bytes_accessed=8 * 2**20, transcendentals=0),
        compiler_params=roomy,
        name="first_back",
    )(core, d_heads, inputs, vectors, d_hidden, own, other)


def update(group, scales, early, late, d_raw, weights, firsts, seconds):
    def rows_of(array):
        return pl.BlockSpec((array.shape[0] // group, array.shape[1]), lambda i: (i, 0))

    def member_of(array):
        return pl.BlockSpec((1,) + array.shape[1:], lambda i: (i, 0, 0))

    per_weight = [rows_of(weight) for weight in weights]
    like = tuple(shaped(weight.shape, f32) for weight in weights)
    return pl.pallas_call(
        update_kernel,
        grid=(group,),
        out_shape=(shaped(d_raw.shape, f32),) + like * 4,
        in_specs=[in_smem, member_of(early), member_of(late), rows_of(d_raw)] + per_weight * 3,
        out_specs=[rows_of(d_raw)] + per_weight * 4,
        cost_estimate=pl.CostEstimate(flops=2**26, bytes_accessed=44 * 2**20, transcendentals=2**22),
        compiler_params=roomy,
        name="update",
    )(scales, early, late, d_raw, *weights, *firsts, *seconds)


def from_other_core(value):
    return lax.ppermute(value, "fsdp", [(0, 1), (1, 0)])


def whole_of(value, axis):
    other = from_other_core(value)
    first = lax.axis_index("fsdp") == 0
    return jnp.concatenate([jnp.where(first, value, other), jnp.where(first, other, value)], axis)


def swap_ctx(value, bit):
    size = lax.axis_size("ctx")
    return lax.ppermute(value, "ctx", [(i, i ^ bit) for i in range(size)])


def across_groups(value, group, step_type):
    bit = group
    while bit < lax.axis_size("ctx"):
        sent = value.astype(step_type)
        value = sent.astype(f32) + swap_ctx(sent, bit).astype(f32)
        bit *= 2
    return value


def per_device(
    inputs,
    targets,
    valid_mask,
    block_seq,
    w_qkv,
    w_out,
    w_up,
    w_down,
    norm_gains,
    biases,
    first_qkv,
    first_out,
    first_up,
    first_down,
    first_gains,
    first_biases,
    second_qkv,
    second_out,
    second_up,
    second_down,
    second_gains,
    second_biases,
):
    rows_here, width = inputs.shape
    group = width // HD
    ctx_size = lax.axis_size("ctx")
    block_rows = rows_here * 2
    total_rows = float(block_rows * ctx_size)
    ctx_place = lax.axis_index("ctx")
    core_place = lax.axis_index("fsdp")
    members = [[first + i for i in range(group)] for first in range(0, ctx_size, group)]

    def exchange(value):
        return lax.all_to_all(value, "ctx", 0, 0, axis_index_groups=members, tiled=True)

    core = jnp.full((1,), core_place, jnp.int32)
    vectors = whole_of(jnp.concatenate([norm_gains, biases], 0), 1).astype(f32)
    other_qkv = from_other_core(w_qkv)
    other_out, other_up, other_down = (from_other_core(w_out), from_other_core(w_up), from_other_core(w_down))
    first = core_place == 0
    full_qkv = jnp.concatenate([jnp.where(first, w_qkv, other_qkv), jnp.where(first, other_qkv, w_qkv)], 0)
    valid_rows = valid_mask.astype(f32)

    normed = (normalize(inputs.astype(f32))[0] * vectors[0] + vectors[2]).astype(bf16)
    qkv_bias = jnp.concatenate([vectors[3], jnp.zeros((width,), f32), vectors[4]])
    projected = lax.dot_general(full_qkv, normed, (((0,), (1,)), ((), ())), preferred_element_type=f32)
    projected = (projected + qkv_bias[:, None]).astype(bf16)
    by_head = projected.reshape(3, group, HD, rows_here).transpose(1, 0, 2, 3)
    qkv = exchange(by_head.reshape(group, 3 * HD, rows_here))
    own_kv = qkv[:, HD:]
    other_kv = from_other_core(own_kv)

    first_block = (ctx_place // group) * group
    own_seq = lax.dynamic_slice_in_dim(block_seq, first_block, group, 0)
    starts = jnp.sum((block_seq[None, :] < own_seq[:, None]).astype(jnp.int32), axis=1)
    starts = jnp.maximum(starts - first_block + group, 0)
    edges = list(range(group, ctx_size, group))
    straddles = jnp.zeros((), bool)
    for edge in edges:
        straddles = straddles | (block_seq[edge - 1] == block_seq[edge])

    def forward_with(own, other):
        prev_own = lax.ppermute(own, "ctx", [(i, i + group) for i in range(ctx_size - group)])
        prev_other = from_other_core(prev_own)
        return attend(starts, core, qkv, other, prev_own, prev_other) + (prev_own, prev_other)

    def forward_without(own, other):
        nothing = jnp.zeros(own.shape, bf16)
        return attend(starts, core, qkv, other) + (nothing, nothing)

    mixed, log_total, prev_own, prev_other = lax.cond(straddles, forward_with, forward_without, own_kv, other_kv)
    attended = exchange(mixed.astype(bf16)).reshape(width, rows_here)

    outputs, d_hidden, d_hidden_low, d_attended, active, d_lifted, normed_two, d_out_low, small = feed(
        core,
        attended,
        inputs,
        targets,
        valid_rows[:, None],
        vectors,
        w_out,
        other_out,
        w_up,
        other_up,
        w_down,
        other_down,
    )
    d_mixed = exchange(d_attended.reshape(group, HD, rows_here))
    keep, send = feed_grads(group, core, active, d_out_low, normed_two, d_lifted, attended, d_hidden_low, small)

    def reduced(keep, send):
        pair = (keep.astype(f32) + from_other_core(send).astype(f32)).astype(bf16)
        mine = across_groups(jnp.sum(exchange(pair).astype(f32), axis=0), group, bf16)
        return exchange(jnp.broadcast_to(mine.astype(bf16)[None], pair.shape)), mine[-16:]

    early, early_sums = reduced(keep, send)

    def backward_with(d_mixed):
        d_query, d_kv = attend_back(starts, core, qkv, (other_kv, prev_own, prev_other), d_mixed, mixed, log_total)
        d_prev = d_kv[2].astype(f32) + from_other_core(d_kv[3]).astype(f32)
        d_prev = lax.ppermute(d_prev.astype(bf16), "ctx", [(i + group, i) for i in range(ctx_size - group)])
        return d_query, d_kv[0], d_kv[1], d_prev

    def backward_without(d_mixed):
        d_query, d_kv = attend_back(starts, core, qkv, (other_kv,), d_mixed, mixed, log_total)
        return d_query, d_kv[0], d_kv[1], jnp.zeros(other_kv.shape, bf16)

    d_query, d_own, d_other, d_prev = lax.cond(straddles, backward_with, backward_without, d_mixed)
    d_kv = d_own.astype(f32) + from_other_core(d_other).astype(f32) + d_prev.astype(f32)
    d_heads = exchange(jnp.concatenate([d_query, d_kv.astype(bf16)], 1))
    d_raw, keep, send = first_back(group, core, d_heads, inputs, vectors, d_hidden, w_qkv, other_qkv)
    late, late_sums = reduced(keep, send)

    count_scale = total_rows / jnp.sum(early_sums[8, :128])
    half = width // 2
    raw_gains = jnp.stack([late_sums[0, :half], early_sums[0, :half]])
    raw_biases = jnp.concatenate([late_sums[1:4, :half], early_sums[1:8, :half]], 0)
    local_squares = (
        jnp.sum(jnp.square(early[:, :-16].astype(f32)))
        + jnp.sum(jnp.square(late[:, :-16].astype(f32)))
        + jnp.sum(raw_gains * raw_gains)
        + jnp.sum(raw_biases * raw_biases)
    )
    squares = jnp.full((8, 128), local_squares, f32)
    total_squares = (squares + from_other_core(squares))[0, 0]
    grad_norm = jnp.sqrt(total_squares) * count_scale / total_rows
    clip_factor = jnp.minimum(1.0, clip_limit / grad_norm)
    scale_back = clip_factor / total_rows
    weights_here = [w_qkv, w_out, w_up, w_down]
    results = update(
        group,
        jnp.stack([count_scale, scale_back]),
        early,
        late,
        d_raw,
        weights_here,
        [first_qkv, first_out, first_up, first_down],
        [second_qkv, second_out, second_up, second_down],
    )
    grad_gains = raw_gains * count_scale
    grad_biases = raw_biases * count_scale
    gains = adam_step(norm_gains, grad_gains, first_gains, second_gains, scale_back, 0.0)
    offsets = adam_step(biases, grad_biases, first_biases, second_biases, scale_back, 0.0)
    matrices = [tuple(results[1 + 4 * kind : 5 + 4 * kind]) for kind in range(4)]
    return (
        (outputs, results[0])
        + matrices[0]
        + (grad_gains, grad_biases, grad_norm)
        + matrices[1]
        + (gains[0], offsets[0])
        + matrices[2]
        + (gains[1], offsets[1])
        + matrices[3]
        + (gains[2], offsets[2])
    )


def solution(mesh):
    tokens = P(("ctx", "fsdp"), None)
    weight = P("fsdp", None)
    vector = P(None, "fsdp")
    params = (weight, weight, weight, weight, vector, vector)
    in_specs = (tokens, tokens, P(("ctx", "fsdp")), P()) + params * 3
    out_specs = (tokens, tokens) + params + (P(),) + params * 3
    return jax.shard_map(per_device, mesh=mesh, in_specs=in_specs, out_specs=out_specs, check_vma=False)
```

```python
import functools
import math

import jax
import jax.numpy as jnp
from jax import lax
from jax.experimental import pallas as pl
from jax.experimental.pallas import tpu as pltpu
from jax.sharding import PartitionSpec as P

HD = 64
STEP = 10

very_low = -1e30
norm_floor = 1e-05
first_decay = 0.9
second_decay = 0.95
adam_floor = 1e-08
learn_rate = 0.02
weight_decay = 0.1
clip_limit = 0.01
gelu_scale = (2.0 / math.pi) ** 0.5
gelu_cubic = 0.044715

BASE_LIMIT = 1e20
ONES = 16

bf16 = jnp.bfloat16
f32 = jnp.float32
NN = (((1,), (0,)), ((), ()))
NT = (((1,), (1,)), ((), ()))
TN = (((0,), (0,)), ((), ()))


def mxu(left, right, dims):
    return lax.dot_general(left, right, dims, preferred_element_type=f32)


def below_diagonal(scores):
    key_pos = lax.broadcasted_iota(jnp.int32, scores.shape, 0)
    query_pos = lax.broadcasted_iota(jnp.int32, scores.shape, 1)
    return jnp.where(key_pos <= query_pos, scores, very_low)


def column_sum(values):
    return jnp.sum(values, axis=0, keepdims=True)


def column_max(values):
    return jnp.max(values, axis=0, keepdims=True)


def normalize(rows):
    center = rows - jnp.mean(rows, axis=1, keepdims=True)
    inverse = lax.rsqrt(jnp.mean(center * center, axis=1, keepdims=True) + norm_floor)
    return center * inverse, inverse


def span(start, size):
    return pl.ds(pl.multiple_of(start, size), size)


def attend_kernel(starts, place_of, qkv, kv, other_kv, *refs, group, own, final):
    if own:
        acc_in = base_in = None
    else:
        acc_in, base_in = refs[:2]
        refs = refs[2:]
    if final:
        out, log_total = refs[:2]
        pieces = refs[2 : 2 + group]
        low, kv_rows, v_ones, q_pad, acc, high = refs[2 + group :]
    else:
        acc_out, base_out, kv_rows, v_ones, q_pad, acc, high = refs
    tokens = q_pad.shape[1]
    count = kv.shape[0]
    ones = jnp.ones((ONES, tokens), bf16)
    for place in range(count):
        for kind, source in ((0, kv), (1, other_kv)):
            here = source[place, source.shape[1] - 2 * HD :, :]
            kv_rows[kind, place] = here.T
            v_ones[kind, place, :HD, :] = here[HD:]
            v_ones[kind, place, HD:, :] = ones
    q_pad[HD:, :] = jnp.zeros((HD, tokens), bf16)

    def score(kind, place):
        return mxu(kv_rows[kind, place], q_pad[...], NN)

    def weigh(kind, place, scores, base):
        return mxu(v_ones[kind, place], jnp.exp(scores - base).astype(bf16), NN)

    def finish(place):
        if final:
            total = acc[HD : HD + 1, :]
            mixed = acc[:HD, :] * (1.0 / total)
            out[place] = mixed
            low[place] = mixed.astype(bf16)
            log_total[place] = high[...] + jnp.log(total)
        else:
            acc_out[place] = acc[...]
            base_out[place] = high[...]

    def begin(place):
        q_pad[:HD, :] = qkv[place, :HD, :] * bf16(HD**-0.5)
        if not own:
            high[...] = base_in[place]
            acc[...] = acc_in[place]
        return jnp.maximum(starts[place] - (group if own else group - count), 0)

    def quick(place, largest):
        first = begin(place)
        if own:
            scores = below_diagonal(score(0, place))
            base = column_max(scores)
            high[...] = base
            acc[...] = weigh(0, place, scores, base)

        def loop(kinds, first, last):
            def body(key_place, nothing):
                base = high[...]
                acc[...] += sum(weigh(kind, key_place, score(kind, key_place), base) for kind in kinds)
                return nothing

            lax.fori_loop(first, last, body, 0)

        if own:
            loop((1,), place, place + place_of[0])
        loop((0, 1), first, place if own else count)
        finish(place)
        return jnp.maximum(largest, acc[HD : HD + 1, :])

    largest = lax.fori_loop(0, group, quick, jnp.zeros((1, tokens), f32))

    @pl.when(jnp.logical_not(jnp.max(largest) < BASE_LIMIT))
    def _():
        rows = 128

        def careful(place, nothing):
            first = begin(place)
            if own:
                high[...] = jnp.full(high.shape, very_low, f32)
                acc[...] = jnp.zeros(acc.shape, f32)

            def by_kind(kind, nothing):
                def by_place(key_place, nothing):
                    def by_rows(index, nothing):
                        here = span(index * rows, rows)
                        scores = mxu(kv_rows[kind, key_place, here, :], q_pad[...], NN)
                        if own:
                            key_pos = index * rows + lax.broadcasted_iota(jnp.int32, scores.shape, 0)
                            query_pos = lax.broadcasted_iota(jnp.int32, scores.shape, 1)
                            query_pos = query_pos + jnp.where((kind == 0) & (key_place == place), 0, tokens)
                            scores = jnp.where(key_pos <= query_pos, scores, very_low)
                        old = high[...]
                        new = jnp.maximum(old, column_max(scores))
                        probs = jnp.exp(scores - new).astype(bf16)
                        acc[...] = acc[...] * jnp.exp(old - new) + mxu(v_ones[kind, key_place, :, here], probs, NN)
                        high[...] = new
                        return nothing

                    return lax.fori_loop(0, tokens // rows, by_rows, nothing)

                last = place + jnp.where(kind == 0, 1, place_of[0]) if own else count
                return lax.fori_loop(first, last, by_place, nothing)

            lax.fori_loop(0, 2, by_kind, 0)
            finish(place)
            return nothing

        lax.fori_loop(0, group, careful, 0)

    if final:
        for step, piece in enumerate(pieces):
            piece[...] = low[place_of[1] ^ step]


def attend_back_kernel(starts, place_of, qkv, kv, other_kv, out, log_total, *refs, group, own, low, final, resumed):
    pieces = refs[:group]
    d_query_in = refs[group] if resumed else None
    d_query, d_kv, d_other_kv, d_out, kv_rows, q_pad, d_pad, d_kv_sum, d_query_sum = refs[group + 1 + resumed :]
    for step, piece in enumerate(pieces):
        d_out[place_of[1] ^ step] = piece[...]
    tokens = q_pad.shape[1]
    count = d_kv.shape[0]
    sources = (kv, other_kv)
    for place in range(count):
        for kind in (0, 1):
            source = sources[kind]
            kv_rows[kind, place] = source[low + place, source.shape[1] - 2 * HD :, :].T
    q_pad[HD:, :] = jnp.zeros((HD, tokens), bf16)
    d_pad[:HD, :] = jnp.zeros((HD, tokens), bf16)
    d_kv_sum[...] = jnp.zeros(d_kv_sum.shape, f32)

    def tile(kind, place, masked, delta, log_row):
        source = sources[kind]
        rows = kv_rows[kind, place]
        scores = mxu(rows, q_pad[...], NN)
        if masked:
            scores = below_diagonal(scores)
        probs = jnp.exp(scores - log_row)
        d_probs = mxu(rows, d_pad[...], NN)
        d_scores = (probs * (d_probs - delta)).astype(bf16)
        d_kv_sum[kind, place] += mxu(q_pad[...], d_scores, NT) + mxu(d_pad[...], probs.astype(bf16), NT)
        first = source.shape[1] - 2 * HD
        return mxu(source[low + place, first : first + HD, :], d_scores, NN)

    def chunk(place, nothing):
        q_pad[:HD, :] = qkv[place, :HD, :] * bf16(HD**-0.5)
        d_here = d_out[place]
        d_pad[HD:, :] = d_here
        delta = column_sum(d_here.astype(f32) * out[place])
        log_row = log_total[place]
        d_query_sum[...] = d_query_in[place] if resumed else jnp.zeros(d_query_sum.shape, f32)

        def loop(kinds, first, last):
            def body(key_place, nothing):
                d_query_sum[...] += sum(tile(kind, key_place, False, delta, log_row) for kind in kinds)
                return nothing

            lax.fori_loop(first, last, body, 0)

        if own:
            here = place - low

            @pl.when(jnp.logical_and(here >= 0, here < count))
            def _():
                d_query_sum[...] += tile(0, here, True, delta, log_row)
                loop((1,), here, here + place_of[0])

            loop((0, 1), jnp.maximum(starts[place] - group - low, 0), jnp.minimum(here, count))
        else:
            loop((0, 1), jnp.maximum(starts[place] - (group - count), 0), count)
        if final:
            d_query[place] = (d_query_sum[...] * HD**-0.5).astype(bf16)
        else:
            d_query[place] = d_query_sum[...]
        return nothing

    lax.fori_loop(0, group, chunk, 0)
    d_kv[...] = d_kv_sum[0].astype(bf16)
    d_other_kv[...] = d_kv_sum[1].astype(bf16)


def first_kernel(core, inputs, vectors, own, other, by_head):
    width = inputs.shape[1]
    half = width // 2
    unit, _ = normalize(inputs[...].astype(f32))
    normed = (unit * vectors[0:1, :] + vectors[2:3, :]).astype(bf16)
    swap = core[0] == 1
    low, high = normed[:, :half], normed[:, half:]
    mine, rest = jnp.where(swap, high, low), jnp.where(swap, low, high)
    for part in range(3):
        columns = slice(part * width, (part + 1) * width)
        rows = mxu(mine, own[:, columns], NN) + mxu(rest, other[:, columns], NN)
        if part != 1:
            row = 3 + part // 2
            rows = rows + vectors[row : row + 1, :]
        turned = rows.astype(bf16).T
        for head in range(width // HD):
            by_head[head, part * HD : (part + 1) * HD, :] = turned[head * HD : (head + 1) * HD]


in_vmem = pl.BlockSpec(memory_space=pltpu.VMEM)
in_smem = pl.BlockSpec(memory_space=pltpu.SMEM)


def norm_back(d_rows, unit, inverse, gain):
    scaled = d_rows * gain
    first = jnp.mean(scaled, axis=1, keepdims=True)
    second = jnp.mean(scaled * unit, axis=1, keepdims=True)
    return inverse * (scaled - first - unit * second)


def feed_kernel(
    core,
    inputs,
    targets,
    valid,
    vectors,
    out_own,
    out_other,
    up_own,
    up_other,
    down_own,
    down_other,
    *refs,
):
    group = inputs.shape[1] // HD
    mixed, refs = refs[:group], refs[group:]
    outputs, d_hidden, d_hidden_low, attended, active, d_lifted, normed, d_out_low, small = refs[:9]
    pieces, refs = refs[9 : 9 + group], refs[9 + group :]
    d_attended, hidden, unit, slope, acc, up_sum = refs
    for index, piece in enumerate(mixed):
        attended[span((core[1] ^ index) * HD, HD), :] = piece[...]
    tokens, width = inputs.shape
    half = width // 2
    f_half = down_own.shape[0]
    step = 512
    place = core[0]
    halves = ((place, out_own, up_own, down_own), (1 - place, out_other, up_other, down_other))
    hidden[...] = inputs[...].astype(f32) + vectors[5:6, :]
    for where, w_out, _, _ in halves:
        hidden[...] += mxu(attended[span(where * half, half), :], w_out[...], TN)
    unit_here, inverse = normalize(hidden[...])
    unit[...] = unit_here
    normed[...] = (unit_here * vectors[1:2, :] + vectors[6:7, :]).astype(bf16)
    for row in range(4):
        up_sum[:, row * width : (row + 1) * width] = vectors[8 + row : 9 + row, :]
    acc[...] = hidden[...] + vectors[7:8, :]
    for where, _, _, w_down in halves:

        def lift(index, nothing):
            columns = span(where * f_half + index * step, step)
            u = up_sum[:, columns]
            for other, _, w_up, _ in halves:
                u = u + mxu(normed[:, span(other * half, half)], w_up[:, columns], NN)
            square = u * u
            tanh = jnp.tanh(gelu_scale * (u + gelu_cubic * (square * u)))
            side = 0.5 * (1.0 + tanh)
            act = (u * side).astype(bf16)
            active[:, columns] = act
            slope[:, columns] = side + (0.5 * gelu_scale) * u * (1.0 - tanh * tanh) * (
                1.0 + (3.0 * gelu_cubic) * square
            )
            acc[...] += mxu(act, w_down[span(index * step, step), :], NN)
            return nothing

        lax.fori_loop(0, f_half // step, lift, 0)
    out_f32 = acc[...]
    outputs[...] = out_f32.astype(bf16)
    d_out = valid[...] * (out_f32 - targets[...].astype(f32))
    d_hidden[...] = d_out
    d_out_low[...] = d_out.astype(bf16)
    small[...] = jnp.zeros(small.shape, f32)
    small[3:4, :] = column_sum(d_out)
    acc[...] = jnp.zeros(acc.shape, f32)
    for where, _, _, w_down in halves:

        def lower(index, nothing):
            columns = span(where * f_half + index * step, step)
            d_active = mxu(d_out_low[...], w_down[span(index * step, step), :], NT)
            low = (d_active * slope[:, columns]).astype(bf16)
            d_lifted[:, columns] = low
            up_sum[:, columns] = column_sum(low.astype(f32))
            for other, _, w_up, _ in halves:
                acc[:, span(other * half, half)] += mxu(low, w_up[:, columns], NT)
            return nothing

        lax.fori_loop(0, f_half // step, lower, 0)
    for row in range(4):
        small[4 + row : 5 + row, :] = up_sum[:, row * width : (row + 1) * width]
    d_normed = acc[...]
    unit_here = unit[...]
    small[0:1, :] = column_sum(d_normed * unit_here)
    small[2:3, :] = column_sum(d_normed)
    d_rows = d_hidden[...] + norm_back(d_normed, unit_here, inverse, vectors[1:2, :])
    d_hidden[...] = d_rows
    small[1:2, :] = column_sum(d_rows)
    low = d_rows.astype(bf16)
    d_hidden_low[...] = low
    for where, w_out, _, _ in halves:
        d_attended[span(where * half, half), :] = mxu(w_out[...], low, NT).astype(bf16)
    for index, piece in enumerate(pieces):
        piece[...] = d_attended[span((core[1] ^ index) * HD, HD), :]
    lanes = lax.broadcasted_iota(jnp.int32, (tokens, 128), 1)
    rows = lax.broadcasted_iota(jnp.int32, (tokens, 128), 0)
    counts = column_sum(jnp.where(rows % 128 == lanes, valid[...], 0.0))
    small[8:9, :128] = counts
    small[8:9, half : half + 128] = counts


def spread_rows(target, gradient, first, rows, me):
    low = gradient.astype(bf16)
    for member in range(target.shape[0]):
        target[member ^ me, first : first + rows, :] = low[member * rows : (member + 1) * rows]


def feed_grads_kernel(core, active, d_out_low, normed, d_lifted, attended, d_hidden_low, small, keep, send):
    width = attended.shape[0]
    half = width // 2
    members = keep.shape[0]
    f_half = active.shape[1] // 2
    rows = f_half // members
    for target, where in ((keep, core[0]), (send, 1 - core[0])):

        def down(index, nothing):
            low = mxu(active[:, span(where * f_half + index * 2 * rows, 2 * rows)], d_out_low[...], TN).astype(bf16)
            target[2 * index, :rows, :] = low[:rows]
            target[2 * index + 1, :rows, :] = low[rows:]
            return nothing

        lax.fori_loop(0, members // 2, down, 0)
        here = span(where * half, half)
        first = rows
        for column in range(0, 2 * f_half, width):
            spread_rows(target, mxu(normed[:, here], d_lifted[:, column : column + width], TN), first, half // members, 0)
            first += half // members
        spread_rows(target, mxu(attended[here, :], d_hidden_low[...], NN), first, half // members, 0)
        first += half // members
        sums = jnp.concatenate([small[:, here], jnp.zeros(small[:, here].shape, f32)], 1).astype(bf16)
        for member in range(members):
            target[member, first:, :] = sums


def first_back_kernel(core, d_heads, inputs, vectors, d_hidden, own, other, d_inputs, keep, send, d_proj, d_normed):
    width = inputs.shape[1]
    half = width // 2
    members = keep.shape[0]
    place = core[0]
    for head in range(width // HD):
        for part in range(3):
            d_proj[part * width + head * HD : part * width + (head + 1) * HD, :] = d_heads[
                head, part * HD : (part + 1) * HD, :
            ]
    unit, inverse = normalize(inputs[...].astype(f32))
    normed = (unit * vectors[0:1, :] + vectors[2:3, :]).astype(bf16).T
    for where, weight in ((place, own), (1 - place, other)):
        d_normed[span(where * half, half), :] = mxu(weight[...], d_proj[...], NN)
    d_rows = d_normed[:width, :].T
    d_inputs[...] = d_hidden[...] + norm_back(d_rows, unit, inverse, vectors[0:1, :])
    gain_sum = column_sum(d_rows * unit)
    offset_sum = column_sum(d_rows)
    ones = jnp.ones((ONES, inputs.shape[0]), bf16)
    query_sum = mxu(ones, d_proj[:width], NT)[:1]
    value_sum = mxu(ones, d_proj[2 * width :], NT)[:1]
    sums = jnp.concatenate([gain_sum, offset_sum, query_sum, value_sum, jnp.zeros((ONES - 4, width), f32)], 0)
    rows = half // members
    d_normed[:ONES, :] = sums
    for part in range(3):
        gradient = mxu(normed, d_proj[part * width : (part + 1) * width], NT)
        d_normed[ONES : ONES + width, :] = gradient
        for target, where in ((keep, place), (send, 1 - place)):
            low = d_normed[pl.ds(pl.multiple_of(ONES + where * half, ONES), half), :]
            spread_rows(target, low, part * rows, rows, core[1])
    for target, where in ((keep, place), (send, 1 - place)):
        low = d_normed[:ONES, span(where * half, half)]
        low = jnp.concatenate([low, jnp.zeros(low.shape, f32)], 1).astype(bf16)
        for member in range(members):
            target[member, 3 * rows :, :] = low


def squares_kernel(sums_early, sums_late, *refs):
    pieces, squares = refs[:-1], refs[-1]
    group = len(pieces) // 2
    half = sums_early.shape[1] // 2

    def square_sum(values):
        values = values.astype(f32)
        return jnp.sum(column_sum(values * values), axis=1, keepdims=True)

    parts = [square_sum(early[...]) + square_sum(late[...]) for early, late in zip(pieces[:group], pieces[group:])]
    total = paired_sum(parts) + (square_sum(sums_early[:8, :half]) + square_sum(sums_late[:4, :half]))
    squares[...] = jnp.broadcast_to(total, squares.shape)


def paired_sum(parts):
    while len(parts) > 1:
        parts = [parts[i] + parts[i + 1] for i in range(0, len(parts), 2)]
    return parts[0]


def update_kernel(me, squares, other_squares, sums_early, sums_late, d_raw, *refs, group, total_rows):
    del me
    early_pieces, late_pieces, refs = refs[:group], refs[group : 2 * group], refs[2 * group :]
    weights, firsts, seconds, refs = refs[0:6], refs[6:12], refs[12:18], refs[18:]
    grad_inputs, norm = refs[:2]
    grads, new_firsts, new_seconds, steps = refs[2:8], refs[8:14], refs[14:20], refs[20:26]
    early, late = refs[26:]
    step = pl.program_id(0)
    for index in range(group):

        @pl.when(step == index)
        def _():
            early[...] = early_pieces[index][...]
            late[...] = late_pieces[index][...]

    count_scale = total_rows / jnp.sum(sums_early[8:9, :128], axis=1, keepdims=True)
    total = squares[:1, :1] + other_squares[:1, :1]
    grad_norm = jnp.sqrt(total) * count_scale / total_rows
    scale_back = jnp.minimum(1.0, clip_limit / grad_norm) / total_rows
    width = d_raw.shape[1]
    grad_inputs[...] = d_raw[...] * count_scale

    def change(index, rows, columns, raw, decay):
        where = (rows, columns)
        gradient = raw * count_scale
        grads[index][where] = gradient
        results = adam_step(
            weights[index][where], gradient, firsts[index][where], seconds[index][where], scale_back, decay
        )
        new_firsts[index][where], new_seconds[index][where], steps[index][where] = results

    everything = slice(None)
    down_rows = weights[3].shape[0]
    after_up = down_rows + weights[2].shape[0] * (weights[2].shape[1] // width)
    for index, (source, first) in enumerate(((late, 0), (early, after_up), (early, down_rows), (early, 0))):
        rows = weights[index].shape[0]
        for block in range(weights[index].shape[1] // width):
            raw = source[first + block * rows : first + (block + 1) * rows, :].astype(f32)
            change(index, everything, slice(block * width, (block + 1) * width), raw, weight_decay)

    @pl.when(step == 0)
    def _():
        half = width // 2
        norm[...] = jnp.broadcast_to(grad_norm, norm.shape)
        change(4, slice(0, 1), everything, sums_late[0:1, :half], 0.0)
        change(4, slice(1, 2), everything, sums_early[0:1, :half], 0.0)
        for row in range(3):
            change(5, slice(row, row + 1), everything, sums_late[1 + row : 2 + row, :half], 0.0)
        for row in range(3, 10):
            change(5, slice(row, row + 1), everything, sums_early[row - 2 : row - 1, :half], 0.0)


def adam_step(weight, gradient, first_old, second_old, scale_back, decay_rate):
    weight32 = weight.astype(f32)
    clipped = gradient * scale_back
    new_first = first_decay * first_old + (1.0 - first_decay) * clipped
    new_second = second_decay * second_old + (1.0 - second_decay) * clipped * clipped
    first_hat = new_first / (1.0 - first_decay**STEP)
    second_hat = new_second / (1.0 - second_decay**STEP)
    update = -learn_rate * (first_hat / (jnp.sqrt(second_hat) + adam_floor) + decay_rate * weight32)
    return (new_first, new_second, update)


roomy = pltpu.CompilerParams(vmem_limit_bytes=56 * 2**20)


def shaped(shape, kind):
    return jax.ShapeDtypeStruct(shape, kind)


in_place = pl.BlockSpec(memory_space=pl.ANY)


def attend(starts, core, qkv, kv, other_kv, state=None, final=True):
    group, _, tokens = qkv.shape
    count = kv.shape[0]
    row = shaped((group, 1, tokens), f32)
    if final:
        out_shape = (shaped((group, HD, tokens), f32), row) + (shaped((HD, tokens), bf16),) * group
    else:
        out_shape = (shaped((group, HD + ONES, tokens), f32), row)
    state = state or ()
    return pl.pallas_call(
        functools.partial(attend_kernel, group=group, own=not state, final=final),
        out_shape=out_shape,
        in_specs=[in_smem, in_smem] + [in_vmem] * (3 + len(state)),
        out_specs=(in_vmem,) * len(out_shape),
        scratch_shapes=([pltpu.VMEM((group, HD, tokens), bf16)] if final else [])
        + [
            pltpu.VMEM((2, count, tokens, 2 * HD), bf16),
            pltpu.VMEM((2, count, HD + ONES, tokens), bf16),
            pltpu.VMEM((2 * HD, tokens), bf16),
            pltpu.VMEM((HD + ONES, tokens), f32),
            pltpu.VMEM((1, tokens), f32),
        ],
        cost_estimate=pl.CostEstimate(flops=30 * 2**30, bytes_accessed=5 * 2**20, transcendentals=2**24),
        compiler_params=roomy,
        name="attend",
    )(starts, core, qkv, kv, other_kv, *state)


def attend_back(starts, core, qkv, kv, other_kv, d_out, out, log_total, after, d_query=None, own=True, low=0, count=0, final=False):
    group, _, tokens = qkv.shape
    resumed = d_query is not None
    return pl.pallas_call(
        functools.partial(attend_back_kernel, group=group, own=own, low=low, final=final, resumed=resumed),
        out_shape=(
            shaped((group, HD, tokens), bf16 if final else f32),
            shaped((count, 2 * HD, tokens), bf16),
            shaped((count, 2 * HD, tokens), bf16),
        ),
        in_specs=[in_smem, in_smem] + [in_vmem] * (5 + group + resumed) + [in_place],
        out_specs=(in_vmem,) * 3,
        scratch_shapes=[
            pltpu.VMEM((group, HD, tokens), bf16),
            pltpu.VMEM((2, count, tokens, 2 * HD), bf16),
            pltpu.VMEM((2 * HD, tokens), bf16),
            pltpu.VMEM((2 * HD, tokens), bf16),
            pltpu.VMEM((2, count, 2 * HD, tokens), f32),
            pltpu.VMEM((HD, tokens), f32),
        ],
        cost_estimate=pl.CostEstimate(flops=count * 8 * 2**30, bytes_accessed=8 * 2**20, transcendentals=2**24),
        compiler_params=roomy,
        name="attend_back",
    )(starts, core, qkv, kv, other_kv, out, log_total, *d_out, *((d_query,) if resumed else ()), after)


def project(core, inputs, vectors, own, other):
    tokens, width = inputs.shape
    return pl.pallas_call(
        first_kernel,
        out_shape=shaped((width // HD, 3 * HD, tokens), bf16),
        in_specs=[in_smem] + [in_vmem] * 4,
        out_specs=in_vmem,
        cost_estimate=pl.CostEstimate(flops=2**30, bytes_accessed=4 * 2**20, transcendentals=0),
        compiler_params=roomy,
        name="project",
    )(core, inputs, vectors, own, other)


def feed(core, mixed, inputs, targets, valid, vectors, *weights):
    tokens, width = inputs.shape
    group = width // HD
    hidden_units = weights[2].shape[1]
    return pl.pallas_call(
        feed_kernel,
        out_shape=(
            shaped((tokens, width), bf16),
            shaped((tokens, width), f32),
            shaped((tokens, width), bf16),
            shaped((width, tokens), bf16),
            shaped((tokens, hidden_units), bf16),
            shaped((tokens, hidden_units), bf16),
            shaped((tokens, width), bf16),
            shaped((tokens, width), bf16),
            shaped((16, width), f32),
        )
        + (shaped((HD, tokens), bf16),) * group,
        in_specs=[in_smem] + [in_vmem] * (10 + group),
        out_specs=(in_vmem,) * (9 + group),
        scratch_shapes=[
            pltpu.VMEM((width, tokens), bf16),
            pltpu.VMEM((tokens, width), f32),
            pltpu.VMEM((tokens, width), f32),
            pltpu.VMEM((tokens, hidden_units), f32),
            pltpu.VMEM((tokens, width), f32),
            pltpu.VMEM((1, hidden_units), f32),
        ],
        cost_estimate=pl.CostEstimate(flops=10 * 2**30, bytes_accessed=14 * 2**20, transcendentals=2**20),
        compiler_params=roomy,
        name="feed",
    )(core, inputs, targets, valid, vectors, *weights, *mixed)


def feed_grads(group, core, *arrays):
    tokens, hidden_units = arrays[0].shape
    width = arrays[1].shape[1]
    rows = (hidden_units + width) // 2 // group + hidden_units // 2 // group + 16
    return pl.pallas_call(
        feed_grads_kernel,
        out_shape=(shaped((group, rows, width), bf16),) * 2,
        in_specs=[in_smem] + [in_vmem] * 7,
        out_specs=(in_vmem,) * 2,
        cost_estimate=pl.CostEstimate(flops=5 * 2**30, bytes_accessed=12 * 2**20, transcendentals=0),
        compiler_params=roomy,
        name="feed_grads",
    )(core, *arrays)


def first_back(group, core, d_heads, inputs, vectors, d_hidden, own, other):
    tokens, width = inputs.shape
    rows = own.shape[0] // group * 3 + 16
    return pl.pallas_call(
        first_back_kernel,
        out_shape=(shaped((tokens, width), f32),) + (shaped((group, rows, width), bf16),) * 2,
        in_specs=[in_smem] + [in_vmem] * 6,
        out_specs=(in_vmem,) * 3,
        scratch_shapes=[pltpu.VMEM((3 * width, tokens), bf16), pltpu.VMEM((width + 16, tokens), f32)],
        cost_estimate=pl.CostEstimate(flops=4 * 2**30, bytes_accessed=8 * 2**20, transcendentals=0),
        compiler_params=roomy,
        name="first_back",
    )(core, d_heads, inputs, vectors, d_hidden, own, other)


def sum_squares(sums_early, sums_late, early, late):
    return pl.pallas_call(
        squares_kernel,
        out_shape=shaped((8, 128), f32),
        in_specs=[in_vmem] * (2 + 2 * len(early)),
        out_specs=in_vmem,
        cost_estimate=pl.CostEstimate(flops=2**22, bytes_accessed=4 * 2**20, transcendentals=0),
        compiler_params=pltpu.CompilerParams(vmem_limit_bytes=16 * 2**20),
        name="sum_squares",
    )(sums_early, sums_late, *early, *late)


def update(group, me, total_rows, squares, other_squares, sums_early, sums_late, d_raw, early, late, *state):
    def whole(array):
        return pl.BlockSpec(array.shape, lambda i, me: (0,) * array.ndim)

    def rows_of(array):
        return pl.BlockSpec((array.shape[0] // group, array.shape[1]), lambda i, me: (i ^ me[0], 0))

    weights = state[0]
    specs = [rows_of(weight) for weight in weights[:4]] + [whole(weight) for weight in weights[4:]]
    like = [shaped(weight.shape, f32) for weight in weights]
    norm = shaped((8, 128), f32)
    inputs = [squares, other_squares, sums_early, sums_late]
    return pl.pallas_call(
        functools.partial(update_kernel, group=group, total_rows=total_rows),
        grid_spec=pltpu.PrefetchScalarGridSpec(
            num_scalar_prefetch=1,
            grid=(group,),
            in_specs=[whole(array) for array in inputs]
            + [rows_of(d_raw)]
            + [whole(array) for array in early + late]
            + specs * 3,
            out_specs=[rows_of(d_raw), whole(norm)] + specs * 4,
            scratch_shapes=[pltpu.VMEM(early[0].shape, bf16), pltpu.VMEM(late[0].shape, bf16)],
        ),
        out_shape=[shaped(d_raw.shape, f32), norm] + like * 4,
        cost_estimate=pl.CostEstimate(flops=2**26, bytes_accessed=44 * 2**20, transcendentals=2**22),
        compiler_params=pltpu.CompilerParams(vmem_limit_bytes=32 * 2**20),
        name="update",
    )(me, *inputs, d_raw, *early, *late, *state[0], *state[1], *state[2])


def from_other_core(value):
    return lax.ppermute(value, "fsdp", [(0, 1), (1, 0)])


def whole_of(value, axis):
    other = from_other_core(value)
    first = lax.axis_index("fsdp") == 0
    return jnp.concatenate([jnp.where(first, value, other), jnp.where(first, other, value)], axis)


def swap_ctx(value, bit):
    size = lax.axis_size("ctx")
    return lax.ppermute(value, "ctx", [(i, i ^ bit) for i in range(size)])


def across_groups(value, group, step_type):
    bit = group
    while bit < lax.axis_size("ctx"):
        sent = value.astype(step_type)
        value = sent.astype(f32) + swap_ctx(sent, bit).astype(f32)
        bit *= 2
    return value


def per_device(
    inputs,
    targets,
    valid_mask,
    block_seq,
    w_qkv,
    w_out,
    w_up,
    w_down,
    norm_gains,
    biases,
    first_qkv,
    first_out,
    first_up,
    first_down,
    first_gains,
    first_biases,
    second_qkv,
    second_out,
    second_up,
    second_down,
    second_gains,
    second_biases,
):
    rows_here, width = inputs.shape
    group = width // HD
    ctx_size = lax.axis_size("ctx")
    block_rows = rows_here * 2
    total_rows = float(block_rows * ctx_size)
    ctx_place = lax.axis_index("ctx")
    core_place = lax.axis_index("fsdp")
    members = [[first + i for i in range(group)] for first in range(0, ctx_size, group)]

    def exchange(value):
        return lax.all_to_all(value, "ctx", 0, 0, axis_index_groups=members, tiled=True)

    core = jnp.stack([core_place, ctx_place % group]).astype(jnp.int32)
    vectors = whole_of(jnp.concatenate([norm_gains, biases], 0), 1).astype(f32)
    other_qkv = from_other_core(w_qkv)
    other_out, other_up, other_down = (from_other_core(w_out), from_other_core(w_up), from_other_core(w_down))
    valid_rows = valid_mask.astype(f32)
    qkv = exchange(project(core, inputs, vectors, w_qkv, other_qkv))
    own_kv = qkv[:, HD:]
    other_kv = from_other_core(own_kv)

    first_block = (ctx_place // group) * group
    own_seq = lax.dynamic_slice_in_dim(block_seq, first_block, group, 0)
    starts = jnp.sum((block_seq[None, :] < own_seq[:, None]).astype(jnp.int32), axis=1)
    starts = jnp.maximum(starts - first_block + group, 0)
    behind = jnp.zeros((), jnp.int32)
    for edge in range(group, ctx_size, group):
        same = (block_seq[edge - group : edge] == block_seq[edge]).astype(jnp.int32)
        behind = jnp.maximum(behind, jnp.sum(same))
    most_behind = group - 1
    few_behind = group // 2
    branch = (behind > 0).astype(jnp.int32) + (behind > few_behind).astype(jnp.int32)
    counts = (0, few_behind, most_behind)

    def forward(count, own, other):
        if count == 0:
            nothing = jnp.zeros((most_behind, 2 * HD, rows_here), bf16)
            return tuple(attend(starts, core, qkv, qkv, other)) + (nothing, nothing)
        prev_own = lax.ppermute(own[group - count :], "ctx", [(i, i + group) for i in range(ctx_size - group)])
        state = attend(starts, core, qkv, qkv, other, final=False)
        prev_own, state = lax.optimization_barrier((prev_own, state))
        prev_other = from_other_core(prev_own)
        mixed = attend(starts, core, qkv, prev_own, prev_other, state=state)
        short = ((most_behind - count, 0), (0, 0), (0, 0))
        return tuple(mixed) + (jnp.pad(prev_own, short), jnp.pad(prev_other, short))

    results = lax.switch(branch, [functools.partial(forward, count) for count in counts], own_kv, other_kv)
    mixed, log_total = results[:2]
    prev = results[2 + group :]

    def deal(pieces):
        moved = []
        for step in range(1, group):
            moved.append(lax.ppermute(pieces[step], "ctx", [(i, i ^ step) for i in range(ctx_size)]))
        return [pieces[0]] + moved

    results = feed(
        core,
        deal(results[2 : 2 + group]),
        inputs,
        targets,
        valid_rows[:, None],
        vectors,
        w_out,
        other_out,
        w_up,
        other_up,
        w_down,
        other_down,
    )
    outputs, d_hidden, d_hidden_low, attended, active, d_lifted, normed_two, d_out_low, small = results[:9]
    d_mixed = deal(results[9:])
    keep, send = feed_grads(group, core, active, d_out_low, normed_two, d_lifted, attended, d_hidden_low, small)

    d_query, d_first, d_first_other = attend_back(
        starts, core, qkv, qkv, other_kv, d_mixed, mixed, log_total, send, low=0, count=1
    )

    def paired(keep, received):
        return [(keep[i].astype(f32) + received[i].astype(f32)).astype(bf16) for i in range(group)]

    def gathered(pairs):
        return paired_sum([piece.astype(f32) for piece in deal(pairs)])

    def finished(mine):
        mine = across_groups(mine, group, bf16)
        return mine[:-16].astype(bf16), mine[-16:]

    received, d_query = lax.optimization_barrier((from_other_core(send), d_query))
    pair = (keep.astype(f32) + received.astype(f32)).astype(bf16)
    early_mine = jnp.sum(exchange(pair).astype(f32), axis=0)

    def backward(count, d_query, d_mixed, pair, prev):
        d_prev = None
        if count:
            prev_own, prev_other = prev
            d_query, d_behind, d_behind_other = attend_back(
                starts,
                core,
                qkv,
                prev_own,
                prev_other,
                d_mixed,
                mixed,
                log_total,
                pair,
                d_query=d_query,
                own=False,
                low=most_behind - count,
                count=count,
            )
            d_prev = (d_behind.astype(f32) + from_other_core(d_behind_other).astype(f32)).astype(bf16)
            d_prev = lax.ppermute(d_prev, "ctx", [(i + group, i) for i in range(ctx_size - group)])
        d_query, d_own, d_other = attend_back(
            starts,
            core,
            qkv,
            qkv,
            other_kv,
            d_mixed,
            mixed,
            log_total,
            pair,
            d_query=d_query,
            low=1,
            count=group - 1,
            final=True,
        )
        if count:
            last = group - 1 - count
            d_last = (d_own[last:].astype(f32) + d_prev.astype(f32)).astype(bf16)
            d_own = jnp.concatenate([d_own[:last], d_last], 0) if last else d_last
        return d_query, d_own, d_other

    d_query, d_own, d_other = lax.switch(
        branch, [functools.partial(backward, count) for count in counts], d_query, d_mixed, pair, prev
    )
    early_mine, d_own, d_other = lax.optimization_barrier((early_mine, d_own, d_other))
    early_low, early_sums = finished(early_mine)
    d_other = jnp.concatenate([from_other_core(d_first_other), from_other_core(d_other)], 0)
    d_own = jnp.concatenate([d_first, d_own], 0)
    d_kv = (d_own.astype(f32) + d_other.astype(f32)).astype(bf16)
    d_heads = exchange(jnp.concatenate([d_query, d_kv], 1))
    early_low, d_heads = lax.optimization_barrier((early_low, d_heads))
    early = deal([early_low] * group)
    d_raw, keep, send = first_back(group, core, d_heads, inputs, vectors, d_hidden, w_qkv, other_qkv)
    late_low, late_sums = finished(gathered(paired(keep, from_other_core(send))))
    late = deal([late_low] * group)
    squares = sum_squares(early_sums, late_sums, early, late)
    results = update(
        group,
        core[1:],
        total_rows,
        squares,
        from_other_core(squares),
        early_sums,
        late_sums,
        d_raw,
        early,
        late,
        [w_qkv, w_out, w_up, w_down, norm_gains, biases],
        [first_qkv, first_out, first_up, first_down, first_gains, first_biases],
        [second_qkv, second_out, second_up, second_down, second_gains, second_biases],
    )
    grad_inputs, norm = results[:2]
    return (outputs, grad_inputs) + tuple(results[2:8]) + (norm[0, 0],) + tuple(results[8:])


def solution(mesh):
    tokens = P(("ctx", "fsdp"), None)
    weight = P("fsdp", None)
    vector = P(None, "fsdp")
    params = (weight, weight, weight, weight, vector, vector)
    in_specs = (tokens, tokens, P(("ctx", "fsdp")), P()) + params * 3
    out_specs = (tokens, tokens) + params + (P(),) + params * 3
    return jax.shard_map(per_device, mesh=mesh, in_specs=in_specs, out_specs=out_specs, check_vma=False)
```

```python
import functools
import math

import jax
import jax.numpy as jnp
from jax import lax
from jax.experimental import pallas as pl
from jax.experimental.pallas import tpu as pltpu
from jax.sharding import PartitionSpec as P

HD = 64
STEP = 10

very_low = -1e30
norm_floor = 1e-05
first_decay = 0.9
second_decay = 0.95
adam_floor = 1e-08
learn_rate = 0.02
weight_decay = 0.1
clip_limit = 0.01
gelu_scale = (2.0 / math.pi) ** 0.5
gelu_cubic = 0.044715

BASE_LIMIT = 1e20
ONES = 16

bf16 = jnp.bfloat16
f32 = jnp.float32
NN = (((1,), (0,)), ((), ()))
NT = (((1,), (1,)), ((), ()))
TN = (((0,), (0,)), ((), ()))


def mxu(left, right, dims):
    return lax.dot_general(left, right, dims, preferred_element_type=f32)


def below_diagonal(scores):
    key_pos = lax.broadcasted_iota(jnp.int32, scores.shape, 0)
    query_pos = lax.broadcasted_iota(jnp.int32, scores.shape, 1)
    return jnp.where(key_pos <= query_pos, scores, very_low)


def column_sum(values):
    return jnp.sum(values, axis=0, keepdims=True)


def column_max(values):
    return jnp.max(values, axis=0, keepdims=True)


def normalize(rows):
    center = rows - jnp.mean(rows, axis=1, keepdims=True)
    inverse = lax.rsqrt(jnp.mean(center * center, axis=1, keepdims=True) + norm_floor)
    return center * inverse, inverse


def span(start, size):
    return pl.ds(pl.multiple_of(start, size), size)


def attend_kernel(starts, place_of, qkv, kv, other_kv, *refs, group, own, final):
    if own:
        acc_in = base_in = None
    else:
        acc_in, base_in = refs[:2]
        refs = refs[2:]
    if final:
        out, log_total = refs[:2]
        pieces = refs[2 : 2 + group]
        low, kv_rows, v_ones, q_pad, acc, high = refs[2 + group :]
    else:
        acc_out, base_out, kv_rows, v_ones, q_pad, acc, high = refs
    tokens = q_pad.shape[1]
    count = kv.shape[0]
    ones = jnp.ones((ONES, tokens), bf16)
    for place in range(count):
        for kind, source in ((0, kv), (1, other_kv)):
            here = source[place, source.shape[1] - 2 * HD :, :]
            kv_rows[kind, place] = here.T
            v_ones[kind, place, :HD, :] = here[HD:]
            v_ones[kind, place, HD:, :] = ones
    q_pad[HD:, :] = jnp.zeros((HD, tokens), bf16)

    def score(kind, place):
        return mxu(kv_rows[kind, place], q_pad[...], NN)

    def weigh(kind, place, scores, base):
        return mxu(v_ones[kind, place], jnp.exp(scores - base).astype(bf16), NN)

    def finish(place):
        if final:
            total = acc[HD : HD + 1, :]
            mixed = acc[:HD, :] * (1.0 / total)
            out[place] = mixed
            low[place] = mixed.astype(bf16)
            log_total[place] = high[...] + jnp.log(total)
        else:
            acc_out[place] = acc[...]
            base_out[place] = high[...]

    def begin(place):
        q_pad[:HD, :] = qkv[place, :HD, :] * bf16(HD**-0.5)
        if not own:
            high[...] = base_in[place]
            acc[...] = acc_in[place]
        return jnp.maximum(starts[place] - (group if own else group - count), 0)

    def quick(place, largest):
        first = begin(place)
        if own:
            scores = below_diagonal(score(0, place))
            base = column_max(scores)
            high[...] = base
            acc[...] = weigh(0, place, scores, base)

        def loop(kinds, first, last):
            def body(key_place, nothing):
                base = high[...]
                acc[...] += sum(weigh(kind, key_place, score(kind, key_place), base) for kind in kinds)
                return nothing

            lax.fori_loop(first, last, body, 0)

        if own:
            loop((1,), place, place + place_of[0])
        loop((0, 1), first, place if own else count)
        finish(place)
        return jnp.maximum(largest, acc[HD : HD + 1, :])

    largest = lax.fori_loop(0, group, quick, jnp.zeros((1, tokens), f32))

    @pl.when(jnp.logical_not(jnp.max(largest) < BASE_LIMIT))
    def _():
        rows = 128

        def careful(place, nothing):
            first = begin(place)
            if own:
                high[...] = jnp.full(high.shape, very_low, f32)
                acc[...] = jnp.zeros(acc.shape, f32)

            def by_kind(kind, nothing):
                def by_place(key_place, nothing):
                    def by_rows(index, nothing):
                        here = span(index * rows, rows)
                        scores = mxu(kv_rows[kind, key_place, here, :], q_pad[...], NN)
                        if own:
                            key_pos = index * rows + lax.broadcasted_iota(jnp.int32, scores.shape, 0)
                            query_pos = lax.broadcasted_iota(jnp.int32, scores.shape, 1)
                            query_pos = query_pos + jnp.where((kind == 0) & (key_place == place), 0, tokens)
                            scores = jnp.where(key_pos <= query_pos, scores, very_low)
                        old = high[...]
                        new = jnp.maximum(old, column_max(scores))
                        probs = jnp.exp(scores - new).astype(bf16)
                        acc[...] = acc[...] * jnp.exp(old - new) + mxu(v_ones[kind, key_place, :, here], probs, NN)
                        high[...] = new
                        return nothing

                    return lax.fori_loop(0, tokens // rows, by_rows, nothing)

                last = place + jnp.where(kind == 0, 1, place_of[0]) if own else count
                return lax.fori_loop(first, last, by_place, nothing)

            lax.fori_loop(0, 2, by_kind, 0)
            finish(place)
            return nothing

        lax.fori_loop(0, group, careful, 0)

    if final:
        for step, piece in enumerate(pieces):
            piece[...] = low[place_of[1] ^ step]


def attend_back_kernel(starts, place_of, qkv, kv, other_kv, out, log_total, *refs, group, own, low, final, resumed):
    pieces = refs[:group]
    d_query_in = refs[group] if resumed else None
    d_query, d_kv, d_other_kv, d_out, kv_rows, q_pad, d_pad, d_kv_sum, d_query_sum = refs[-9:]
    for step, piece in enumerate(pieces):
        d_out[place_of[1] ^ step] = piece[...]
    tokens = q_pad.shape[1]
    count = d_kv.shape[0]
    sources = (kv, other_kv)
    for place in range(count):
        for kind in (0, 1):
            source = sources[kind]
            kv_rows[kind, place] = source[low + place, source.shape[1] - 2 * HD :, :].T
    q_pad[HD:, :] = jnp.zeros((HD, tokens), bf16)
    d_pad[:HD, :] = jnp.zeros((HD, tokens), bf16)
    d_kv_sum[...] = jnp.zeros(d_kv_sum.shape, f32)

    def tile(kind, place, masked, delta, log_row):
        source = sources[kind]
        rows = kv_rows[kind, place]
        scores = mxu(rows, q_pad[...], NN)
        if masked:
            scores = below_diagonal(scores)
        probs = jnp.exp(scores - log_row)
        d_probs = mxu(rows, d_pad[...], NN)
        d_scores = (probs * (d_probs - delta)).astype(bf16)
        d_kv_sum[kind, place] += mxu(q_pad[...], d_scores, NT) + mxu(d_pad[...], probs.astype(bf16), NT)
        first = source.shape[1] - 2 * HD
        return mxu(source[low + place, first : first + HD, :], d_scores, NN)

    def chunk(place, nothing):
        q_pad[:HD, :] = qkv[place, :HD, :] * bf16(HD**-0.5)
        d_here = d_out[place]
        d_pad[HD:, :] = d_here
        delta = column_sum(d_here.astype(f32) * out[place])
        log_row = log_total[place]
        d_query_sum[...] = d_query_in[place] if resumed else jnp.zeros(d_query_sum.shape, f32)

        def loop(kinds, first, last):
            def body(key_place, nothing):
                d_query_sum[...] += sum(tile(kind, key_place, False, delta, log_row) for kind in kinds)
                return nothing

            lax.fori_loop(first, last, body, 0)

        if own:
            here = place - low

            @pl.when(jnp.logical_and(here >= 0, here < count))
            def _():
                d_query_sum[...] += tile(0, here, True, delta, log_row)
                loop((1,), here, here + place_of[0])

            loop((0, 1), jnp.maximum(starts[place] - group - low, 0), jnp.minimum(here, count))
        else:
            loop((0, 1), jnp.maximum(starts[place] - (group - count), 0), count)
        if final:
            d_query[place] = (d_query_sum[...] * HD**-0.5).astype(bf16)
        else:
            d_query[place] = d_query_sum[...]
        return nothing

    lax.fori_loop(0, group, chunk, 0)
    d_kv[...] = d_kv_sum[0].astype(bf16)
    d_other_kv[...] = d_kv_sum[1].astype(bf16)


def first_kernel(core, inputs, vectors, own, other, by_head):
    width = inputs.shape[1]
    half = width // 2
    unit, _ = normalize(inputs[...].astype(f32))
    normed = (unit * vectors[0:1, :] + vectors[2:3, :]).astype(bf16)
    swap = core[0] == 1
    low, high = normed[:, :half], normed[:, half:]
    mine, rest = jnp.where(swap, high, low), jnp.where(swap, low, high)
    for part in range(3):
        columns = slice(part * width, (part + 1) * width)
        rows = mxu(mine, own[:, columns], NN) + mxu(rest, other[:, columns], NN)
        if part != 1:
            row = 3 + part // 2
            rows = rows + vectors[row : row + 1, :]
        turned = rows.astype(bf16).T
        for head in range(width // HD):
            by_head[head, part * HD : (part + 1) * HD, :] = turned[head * HD : (head + 1) * HD]


in_vmem = pl.BlockSpec(memory_space=pltpu.VMEM)
in_smem = pl.BlockSpec(memory_space=pltpu.SMEM)


def norm_back(d_rows, unit, inverse, gain):
    scaled = d_rows * gain
    first = jnp.mean(scaled, axis=1, keepdims=True)
    second = jnp.mean(scaled * unit, axis=1, keepdims=True)
    return inverse * (scaled - first - unit * second)


def feed_kernel(
    core,
    inputs,
    targets,
    valid,
    vectors,
    out_own,
    out_other,
    up_own,
    up_other,
    down_own,
    down_other,
    *refs,
):
    group = inputs.shape[1] // HD
    mixed, refs = refs[:group], refs[group:]
    outputs, d_hidden, d_hidden_low, attended, active, d_lifted, normed, d_out_low, small = refs[:9]
    pieces, refs = refs[9 : 9 + group], refs[9 + group :]
    d_attended, hidden, unit, slope, acc, up_sum = refs
    for index, piece in enumerate(mixed):
        attended[span((core[1] ^ index) * HD, HD), :] = piece[...]
    tokens, width = inputs.shape
    half = width // 2
    f_half = down_own.shape[0]
    step = 512
    place = core[0]
    halves = ((place, out_own, up_own, down_own), (1 - place, out_other, up_other, down_other))
    hidden[...] = inputs[...].astype(f32) + vectors[5:6, :]
    for where, w_out, _, _ in halves:
        hidden[...] += mxu(attended[span(where * half, half), :], w_out[...], TN)
    unit_here, inverse = normalize(hidden[...])
    unit[...] = unit_here
    normed[...] = (unit_here * vectors[1:2, :] + vectors[6:7, :]).astype(bf16)
    for row in range(4):
        up_sum[:, row * width : (row + 1) * width] = vectors[8 + row : 9 + row, :]
    acc[...] = hidden[...] + vectors[7:8, :]
    for where, _, _, w_down in halves:

        def lift(index, nothing):
            columns = span(where * f_half + index * step, step)
            u = up_sum[:, columns]
            for other, _, w_up, _ in halves:
                u = u + mxu(normed[:, span(other * half, half)], w_up[:, columns], NN)
            square = u * u
            tanh = jnp.tanh(gelu_scale * (u + gelu_cubic * (square * u)))
            side = 0.5 * (1.0 + tanh)
            act = (u * side).astype(bf16)
            active[:, columns] = act
            slope[:, columns] = side + (0.5 * gelu_scale) * u * (1.0 - tanh * tanh) * (
                1.0 + (3.0 * gelu_cubic) * square
            )
            acc[...] += mxu(act, w_down[span(index * step, step), :], NN)
            return nothing

        lax.fori_loop(0, f_half // step, lift, 0)
    out_f32 = acc[...]
    outputs[...] = out_f32.astype(bf16)
    d_out = valid[...] * (out_f32 - targets[...].astype(f32))
    d_hidden[...] = d_out
    d_out_low[...] = d_out.astype(bf16)
    small[...] = jnp.zeros(small.shape, f32)
    small[3:4, :] = column_sum(d_out)
    acc[...] = jnp.zeros(acc.shape, f32)
    for where, _, _, w_down in halves:

        def lower(index, nothing):
            columns = span(where * f_half + index * step, step)
            d_active = mxu(d_out_low[...], w_down[span(index * step, step), :], NT)
            low = (d_active * slope[:, columns]).astype(bf16)
            d_lifted[:, columns] = low
            up_sum[:, columns] = column_sum(low.astype(f32))
            for other, _, w_up, _ in halves:
                acc[:, span(other * half, half)] += mxu(low, w_up[:, columns], NT)
            return nothing

        lax.fori_loop(0, f_half // step, lower, 0)
    for row in range(4):
        small[4 + row : 5 + row, :] = up_sum[:, row * width : (row + 1) * width]
    d_normed = acc[...]
    unit_here = unit[...]
    small[0:1, :] = column_sum(d_normed * unit_here)
    small[2:3, :] = column_sum(d_normed)
    d_rows = d_hidden[...] + norm_back(d_normed, unit_here, inverse, vectors[1:2, :])
    d_hidden[...] = d_rows
    small[1:2, :] = column_sum(d_rows)
    low = d_rows.astype(bf16)
    d_hidden_low[...] = low
    for where, w_out, _, _ in halves:
        d_attended[span(where * half, half), :] = mxu(w_out[...], low, NT).astype(bf16)
    for index, piece in enumerate(pieces):
        piece[...] = d_attended[span((core[1] ^ index) * HD, HD), :]
    lanes = lax.broadcasted_iota(jnp.int32, (tokens, 128), 1)
    rows = lax.broadcasted_iota(jnp.int32, (tokens, 128), 0)
    counts = column_sum(jnp.where(rows % 128 == lanes, valid[...], 0.0))
    small[8:9, :128] = counts
    small[8:9, half : half + 128] = counts


def spread_rows(target, gradient, first, rows, me):
    low = gradient.astype(bf16)
    for member in range(target.shape[0]):
        target[member ^ me, first : first + rows, :] = low[member * rows : (member + 1) * rows]


def feed_grads_kernel(core, active, d_out_low, normed, d_lifted, attended, d_hidden_low, small, keep, send):
    width = attended.shape[0]
    half = width // 2
    members = keep.shape[0]
    f_half = active.shape[1] // 2
    rows = f_half // members
    for target, where in ((keep, core[0]), (send, 1 - core[0])):

        def down(index, nothing):
            low = mxu(active[:, span(where * f_half + index * 2 * rows, 2 * rows)], d_out_low[...], TN).astype(bf16)
            target[2 * index, :rows, :] = low[:rows]
            target[2 * index + 1, :rows, :] = low[rows:]
            return nothing

        lax.fori_loop(0, members // 2, down, 0)
        here = span(where * half, half)
        first = rows
        for column in range(0, 2 * f_half, width):
            spread_rows(target, mxu(normed[:, here], d_lifted[:, column : column + width], TN), first, half // members, 0)
            first += half // members
        spread_rows(target, mxu(attended[here, :], d_hidden_low[...], NN), first, half // members, 0)
        first += half // members
        sums = jnp.concatenate([small[:, here], jnp.zeros(small[:, here].shape, f32)], 1).astype(bf16)
        for member in range(members):
            target[member, first:, :] = sums


def first_back_kernel(core, d_heads, inputs, vectors, d_hidden, own, other, d_inputs, keep, send, d_proj, d_normed):
    width = inputs.shape[1]
    half = width // 2
    members = keep.shape[0]
    place = core[0]
    for head in range(width // HD):
        for part in range(3):
            d_proj[part * width + head * HD : part * width + (head + 1) * HD, :] = d_heads[
                head, part * HD : (part + 1) * HD, :
            ]
    unit, inverse = normalize(inputs[...].astype(f32))
    normed = (unit * vectors[0:1, :] + vectors[2:3, :]).astype(bf16).T
    for where, weight in ((place, own), (1 - place, other)):
        d_normed[span(where * half, half), :] = mxu(weight[...], d_proj[...], NN)
    d_rows = d_normed[:width, :].T
    d_inputs[...] = d_hidden[...] + norm_back(d_rows, unit, inverse, vectors[0:1, :])
    gain_sum = column_sum(d_rows * unit)
    offset_sum = column_sum(d_rows)
    ones = jnp.ones((ONES, inputs.shape[0]), bf16)
    query_sum = mxu(ones, d_proj[:width], NT)[:1]
    value_sum = mxu(ones, d_proj[2 * width :], NT)[:1]
    sums = jnp.concatenate([gain_sum, offset_sum, query_sum, value_sum, jnp.zeros((ONES - 4, width), f32)], 0)
    rows = half // members
    d_normed[:ONES, :] = sums
    for part in range(3):
        gradient = mxu(normed, d_proj[part * width : (part + 1) * width], NT)
        d_normed[ONES : ONES + width, :] = gradient
        for target, where in ((keep, place), (send, 1 - place)):
            low = d_normed[pl.ds(pl.multiple_of(ONES + where * half, ONES), half), :]
            spread_rows(target, low, part * rows, rows, core[1])
    for target, where in ((keep, place), (send, 1 - place)):
        low = d_normed[:ONES, span(where * half, half)]
        low = jnp.concatenate([low, jnp.zeros(low.shape, f32)], 1).astype(bf16)
        for member in range(members):
            target[member, 3 * rows :, :] = low


def squares_kernel(sums_early, sums_late, *refs):
    pieces, squares = refs[:-1], refs[-1]
    group = len(pieces) // 2
    half = sums_early.shape[1] // 2

    def square_sum(values):
        values = values.astype(f32)
        return jnp.sum(column_sum(values * values), axis=1, keepdims=True)

    parts = [square_sum(early[...]) + square_sum(late[...]) for early, late in zip(pieces[:group], pieces[group:])]
    total = paired_sum(parts) + (square_sum(sums_early[:8, :half]) + square_sum(sums_late[:4, :half]))
    squares[...] = jnp.broadcast_to(total, squares.shape)


def paired_sum(parts):
    while len(parts) > 1:
        parts = [parts[i] + parts[i + 1] for i in range(0, len(parts), 2)]
    return parts[0]


def update_kernel(me, squares, other_squares, sums_early, sums_late, d_raw, *refs, group, total_rows):
    del me
    early_pieces, late_pieces, refs = refs[:group], refs[group : 2 * group], refs[2 * group :]
    weights, firsts, seconds, refs = refs[0:6], refs[6:12], refs[12:18], refs[18:]
    grad_inputs, norm = refs[:2]
    grads, new_firsts, new_seconds, steps = refs[2:8], refs[8:14], refs[14:20], refs[20:26]
    early, late = refs[26:]
    step = pl.program_id(0)
    for index in range(group):

        @pl.when(step == index)
        def _():
            early[...] = early_pieces[index][...]
            late[...] = late_pieces[index][...]

    count_scale = total_rows / jnp.sum(sums_early[8:9, :128], axis=1, keepdims=True)
    total = squares[:1, :1] + other_squares[:1, :1]
    grad_norm = jnp.sqrt(total) * count_scale / total_rows
    scale_back = jnp.minimum(1.0, clip_limit / grad_norm) / total_rows
    width = d_raw.shape[1]
    grad_inputs[...] = d_raw[...] * count_scale

    def change(index, rows, columns, raw, decay):
        where = (rows, columns)
        gradient = raw * count_scale
        grads[index][where] = gradient
        results = adam_step(
            weights[index][where], gradient, firsts[index][where], seconds[index][where], scale_back, decay
        )
        new_firsts[index][where], new_seconds[index][where], steps[index][where] = results

    everything = slice(None)
    down_rows = weights[3].shape[0]
    after_up = down_rows + weights[2].shape[0] * (weights[2].shape[1] // width)
    for index, (source, first) in enumerate(((late, 0), (early, after_up), (early, down_rows), (early, 0))):
        rows = weights[index].shape[0]
        for block in range(weights[index].shape[1] // width):
            raw = source[first + block * rows : first + (block + 1) * rows, :].astype(f32)
            change(index, everything, slice(block * width, (block + 1) * width), raw, weight_decay)

    @pl.when(step == 0)
    def _():
        half = width // 2
        norm[...] = jnp.broadcast_to(grad_norm, norm.shape)
        change(4, slice(0, 1), everything, sums_late[0:1, :half], 0.0)
        change(4, slice(1, 2), everything, sums_early[0:1, :half], 0.0)
        for row in range(3):
            change(5, slice(row, row + 1), everything, sums_late[1 + row : 2 + row, :half], 0.0)
        for row in range(3, 10):
            change(5, slice(row, row + 1), everything, sums_early[row - 2 : row - 1, :half], 0.0)


def adam_step(weight, gradient, first_old, second_old, scale_back, decay_rate):
    weight32 = weight.astype(f32)
    clipped = gradient * scale_back
    new_first = first_decay * first_old + (1.0 - first_decay) * clipped
    new_second = second_decay * second_old + (1.0 - second_decay) * clipped * clipped
    first_hat = new_first / (1.0 - first_decay**STEP)
    second_hat = new_second / (1.0 - second_decay**STEP)
    update = -learn_rate * (first_hat / (jnp.sqrt(second_hat) + adam_floor) + decay_rate * weight32)
    return (new_first, new_second, update)


roomy = pltpu.CompilerParams(vmem_limit_bytes=56 * 2**20)


def shaped(shape, kind):
    return jax.ShapeDtypeStruct(shape, kind)


in_place = pl.BlockSpec(memory_space=pl.ANY)


def attend(starts, core, qkv, kv, other_kv, state=None, final=True):
    group, _, tokens = qkv.shape
    count = kv.shape[0]
    row = shaped((group, 1, tokens), f32)
    if final:
        out_shape = (shaped((group, HD, tokens), f32), row) + (shaped((HD, tokens), bf16),) * group
    else:
        out_shape = (shaped((group, HD + ONES, tokens), f32), row)
    state = state or ()
    return pl.pallas_call(
        functools.partial(attend_kernel, group=group, own=not state, final=final),
        out_shape=out_shape,
        in_specs=[in_smem, in_smem] + [in_vmem] * (3 + len(state)),
        out_specs=(in_vmem,) * len(out_shape),
        scratch_shapes=([pltpu.VMEM((group, HD, tokens), bf16)] if final else [])
        + [
            pltpu.VMEM((2, count, tokens, 2 * HD), bf16),
            pltpu.VMEM((2, count, HD + ONES, tokens), bf16),
            pltpu.VMEM((2 * HD, tokens), bf16),
            pltpu.VMEM((HD + ONES, tokens), f32),
            pltpu.VMEM((1, tokens), f32),
        ],
        cost_estimate=pl.CostEstimate(flops=30 * 2**30, bytes_accessed=5 * 2**20, transcendentals=2**24),
        compiler_params=roomy,
        name="attend",
    )(starts, core, qkv, kv, other_kv, *state)


def attend_back(starts, core, qkv, kv, other_kv, d_out, out, log_total, after, d_query=None, own=True, low=0, count=0, final=False):
    group, _, tokens = qkv.shape
    resumed = d_query is not None
    return pl.pallas_call(
        functools.partial(attend_back_kernel, group=group, own=own, low=low, final=final, resumed=resumed),
        out_shape=(
            shaped((group, HD, tokens), bf16 if final else f32),
            shaped((count, 2 * HD, tokens), bf16),
            shaped((count, 2 * HD, tokens), bf16),
        ),
        in_specs=[in_smem, in_smem] + [in_vmem] * (5 + group + resumed) + [in_place] * len(after),
        out_specs=(in_vmem,) * 3,
        scratch_shapes=[
            pltpu.VMEM((group, HD, tokens), bf16),
            pltpu.VMEM((2, count, tokens, 2 * HD), bf16),
            pltpu.VMEM((2 * HD, tokens), bf16),
            pltpu.VMEM((2 * HD, tokens), bf16),
            pltpu.VMEM((2, count, 2 * HD, tokens), f32),
            pltpu.VMEM((HD, tokens), f32),
        ],
        cost_estimate=pl.CostEstimate(flops=count * 8 * 2**30, bytes_accessed=8 * 2**20, transcendentals=2**24),
        compiler_params=roomy,
        name="attend_back",
    )(starts, core, qkv, kv, other_kv, out, log_total, *d_out, *((d_query,) if resumed else ()), *after)


def project(core, inputs, vectors, own, other):
    tokens, width = inputs.shape
    return pl.pallas_call(
        first_kernel,
        out_shape=shaped((width // HD, 3 * HD, tokens), bf16),
        in_specs=[in_smem] + [in_vmem] * 4,
        out_specs=in_vmem,
        cost_estimate=pl.CostEstimate(flops=2**30, bytes_accessed=4 * 2**20, transcendentals=0),
        compiler_params=roomy,
        name="project",
    )(core, inputs, vectors, own, other)


def feed(core, mixed, inputs, targets, valid, vectors, *weights):
    tokens, width = inputs.shape
    group = width // HD
    hidden_units = weights[2].shape[1]
    return pl.pallas_call(
        feed_kernel,
        out_shape=(
            shaped((tokens, width), bf16),
            shaped((tokens, width), f32),
            shaped((tokens, width), bf16),
            shaped((width, tokens), bf16),
            shaped((tokens, hidden_units), bf16),
            shaped((tokens, hidden_units), bf16),
            shaped((tokens, width), bf16),
            shaped((tokens, width), bf16),
            shaped((16, width), f32),
        )
        + (shaped((HD, tokens), bf16),) * group,
        in_specs=[in_smem] + [in_vmem] * (10 + group),
        out_specs=(in_vmem,) * (9 + group),
        scratch_shapes=[
            pltpu.VMEM((width, tokens), bf16),
            pltpu.VMEM((tokens, width), f32),
            pltpu.VMEM((tokens, width), f32),
            pltpu.VMEM((tokens, hidden_units), f32),
            pltpu.VMEM((tokens, width), f32),
            pltpu.VMEM((1, hidden_units), f32),
        ],
        cost_estimate=pl.CostEstimate(flops=10 * 2**30, bytes_accessed=14 * 2**20, transcendentals=2**20),
        compiler_params=roomy,
        name="feed",
    )(core, inputs, targets, valid, vectors, *weights, *mixed)


def feed_grads(group, core, *arrays):
    tokens, hidden_units = arrays[0].shape
    width = arrays[1].shape[1]
    rows = (hidden_units + width) // 2 // group + hidden_units // 2 // group + 16
    return pl.pallas_call(
        feed_grads_kernel,
        out_shape=(shaped((group, rows, width), bf16),) * 2,
        in_specs=[in_smem] + [in_vmem] * 7,
        out_specs=(in_vmem,) * 2,
        cost_estimate=pl.CostEstimate(flops=5 * 2**30, bytes_accessed=12 * 2**20, transcendentals=0),
        compiler_params=roomy,
        name="feed_grads",
    )(core, *arrays)


def first_back(group, core, d_heads, inputs, vectors, d_hidden, own, other):
    tokens, width = inputs.shape
    rows = own.shape[0] // group * 3 + 16
    return pl.pallas_call(
        first_back_kernel,
        out_shape=(shaped((tokens, width), f32),) + (shaped((group, rows, width), bf16),) * 2,
        in_specs=[in_smem] + [in_vmem] * 6,
        out_specs=(in_vmem,) * 3,
        scratch_shapes=[pltpu.VMEM((3 * width, tokens), bf16), pltpu.VMEM((width + 16, tokens), f32)],
        cost_estimate=pl.CostEstimate(flops=4 * 2**30, bytes_accessed=8 * 2**20, transcendentals=0),
        compiler_params=roomy,
        name="first_back",
    )(core, d_heads, inputs, vectors, d_hidden, own, other)


def sum_squares(sums_early, sums_late, early, late):
    return pl.pallas_call(
        squares_kernel,
        out_shape=shaped((8, 128), f32),
        in_specs=[in_vmem] * (2 + 2 * len(early)),
        out_specs=in_vmem,
        cost_estimate=pl.CostEstimate(flops=2**22, bytes_accessed=4 * 2**20, transcendentals=0),
        compiler_params=pltpu.CompilerParams(vmem_limit_bytes=16 * 2**20),
        name="sum_squares",
    )(sums_early, sums_late, *early, *late)


def update(group, me, total_rows, squares, other_squares, sums_early, sums_late, d_raw, early, late, *state):
    def whole(array):
        return pl.BlockSpec(array.shape, lambda i, me: (0,) * array.ndim)

    def rows_of(array):
        return pl.BlockSpec((array.shape[0] // group, array.shape[1]), lambda i, me: (i ^ me[0], 0))

    weights = state[0]
    specs = [rows_of(weight) for weight in weights[:4]] + [whole(weight) for weight in weights[4:]]
    like = [shaped(weight.shape, f32) for weight in weights]
    norm = shaped((8, 128), f32)
    inputs = [squares, other_squares, sums_early, sums_late]
    return pl.pallas_call(
        functools.partial(update_kernel, group=group, total_rows=total_rows),
        grid_spec=pltpu.PrefetchScalarGridSpec(
            num_scalar_prefetch=1,
            grid=(group,),
            in_specs=[whole(array) for array in inputs]
            + [rows_of(d_raw)]
            + [whole(array) for array in early + late]
            + specs * 3,
            out_specs=[rows_of(d_raw), whole(norm)] + specs * 4,
            scratch_shapes=[pltpu.VMEM(early[0].shape, bf16), pltpu.VMEM(late[0].shape, bf16)],
        ),
        out_shape=[shaped(d_raw.shape, f32), norm] + like * 4,
        cost_estimate=pl.CostEstimate(flops=2**26, bytes_accessed=44 * 2**20, transcendentals=2**22),
        compiler_params=pltpu.CompilerParams(vmem_limit_bytes=32 * 2**20),
        name="update",
    )(me, *inputs, d_raw, *early, *late, *state[0], *state[1], *state[2])


def from_other_core(value):
    return lax.ppermute(value, "fsdp", [(0, 1), (1, 0)])


def whole_of(value, axis):
    other = from_other_core(value)
    first = lax.axis_index("fsdp") == 0
    return jnp.concatenate([jnp.where(first, value, other), jnp.where(first, other, value)], axis)


def swap_ctx(value, bit):
    size = lax.axis_size("ctx")
    return lax.ppermute(value, "ctx", [(i, i ^ bit) for i in range(size)])


def across_groups(value, group, step_type):
    bit = group
    while bit < lax.axis_size("ctx"):
        sent = value.astype(step_type)
        value = sent.astype(f32) + swap_ctx(sent, bit).astype(f32)
        bit *= 2
    return value


def per_device(
    inputs,
    targets,
    valid_mask,
    block_seq,
    w_qkv,
    w_out,
    w_up,
    w_down,
    norm_gains,
    biases,
    first_qkv,
    first_out,
    first_up,
    first_down,
    first_gains,
    first_biases,
    second_qkv,
    second_out,
    second_up,
    second_down,
    second_gains,
    second_biases,
):
    rows_here, width = inputs.shape
    group = width // HD
    ctx_size = lax.axis_size("ctx")
    block_rows = rows_here * 2
    total_rows = float(block_rows * ctx_size)
    ctx_place = lax.axis_index("ctx")
    core_place = lax.axis_index("fsdp")
    members = [[first + i for i in range(group)] for first in range(0, ctx_size, group)]

    def exchange(value):
        return lax.all_to_all(value, "ctx", 0, 0, axis_index_groups=members, tiled=True)

    core = jnp.stack([core_place, ctx_place % group]).astype(jnp.int32)
    vectors = whole_of(jnp.concatenate([norm_gains, biases], 0), 1).astype(f32)
    other_qkv = from_other_core(w_qkv)
    other_out, other_up, other_down = (from_other_core(w_out), from_other_core(w_up), from_other_core(w_down))
    valid_rows = valid_mask.astype(f32)
    qkv = exchange(project(core, inputs, vectors, w_qkv, other_qkv))
    own_kv = qkv[:, HD:]
    other_kv = from_other_core(own_kv)

    first_block = (ctx_place // group) * group
    own_seq = lax.dynamic_slice_in_dim(block_seq, first_block, group, 0)
    starts = jnp.sum((block_seq[None, :] < own_seq[:, None]).astype(jnp.int32), axis=1)
    starts = jnp.maximum(starts - first_block + group, 0)
    behind = jnp.zeros((), jnp.int32)
    for edge in range(group, ctx_size, group):
        same = (block_seq[edge - group : edge] == block_seq[edge]).astype(jnp.int32)
        behind = jnp.maximum(behind, jnp.sum(same))
    most_behind = group - 1
    few_behind = group // 2
    branch = (behind > 0).astype(jnp.int32) + (behind > few_behind).astype(jnp.int32)
    counts = (0, few_behind, most_behind)

    def forward(count, own, other):
        if count == 0:
            nothing = jnp.zeros((most_behind, 2 * HD, rows_here), bf16)
            return tuple(attend(starts, core, qkv, qkv, other)) + (nothing, nothing)
        prev_own = lax.ppermute(own[group - count :], "ctx", [(i, i + group) for i in range(ctx_size - group)])
        state = attend(starts, core, qkv, qkv, other, final=False)
        prev_own, state = lax.optimization_barrier((prev_own, state))
        prev_other = from_other_core(prev_own)
        mixed = attend(starts, core, qkv, prev_own, prev_other, state=state)
        short = ((most_behind - count, 0), (0, 0), (0, 0))
        return tuple(mixed) + (jnp.pad(prev_own, short), jnp.pad(prev_other, short))

    results = lax.switch(branch, [functools.partial(forward, count) for count in counts], own_kv, other_kv)
    mixed, log_total = results[:2]
    prev = results[2 + group :]

    def deal(pieces):
        moved = []
        for step in range(1, group):
            moved.append(lax.ppermute(pieces[step], "ctx", [(i, i ^ step) for i in range(ctx_size)]))
        return [pieces[0]] + moved

    results = feed(
        core,
        deal(results[2 : 2 + group]),
        inputs,
        targets,
        valid_rows[:, None],
        vectors,
        w_out,
        other_out,
        w_up,
        other_up,
        w_down,
        other_down,
    )
    outputs, d_hidden, d_hidden_low, attended, active, d_lifted, normed_two, d_out_low, small = results[:9]
    d_mixed = deal(results[9:])
    keep, send = feed_grads(group, core, active, d_out_low, normed_two, d_lifted, attended, d_hidden_low, small)

    def paired(keep, received):
        return [(keep[i].astype(f32) + received[i].astype(f32)).astype(bf16) for i in range(group)]

    def gathered(pairs):
        return paired_sum([piece.astype(f32) for piece in deal(pairs)])

    def finished(mine):
        mine = across_groups(mine, group, bf16)
        return mine[:-16].astype(bf16), mine[-16:]

    received, d_mixed = lax.optimization_barrier((from_other_core(send), d_mixed))
    pair = (keep.astype(f32) + received.astype(f32)).astype(bf16)
    early_mine = jnp.sum(exchange(pair).astype(f32), axis=0)
    cuts = (0, 3, 5, group)

    def back(part, after, d_query, d_mixed):
        low, high = cuts[part], cuts[part + 1]
        return attend_back(
            starts,
            core,
            qkv,
            qkv,
            other_kv,
            d_mixed,
            mixed,
            log_total,
            after,
            d_query=d_query,
            low=low,
            count=high - low,
            final=high == group,
        )

    def backward(count, d_mixed, pair, prev):
        if count == 0:
            nothing = jnp.zeros((most_behind, 2 * HD, rows_here), bf16)
            return tuple(back(0, (pair,), None, d_mixed)) + (nothing,)
        prev_own, prev_other = prev
        d_query, d_behind, d_behind_other = attend_back(
            starts,
            core,
            qkv,
            prev_own,
            prev_other,
            d_mixed,
            mixed,
            log_total,
            (pair,),
            own=False,
            low=most_behind - count,
            count=count,
        )
        d_prev = (d_behind.astype(f32) + from_other_core(d_behind_other).astype(f32)).astype(bf16)
        d_prev = lax.ppermute(d_prev, "ctx", [(i + group, i) for i in range(ctx_size - group)])
        results = tuple(back(0, (pair,), d_query, d_mixed))
        results, d_prev = lax.optimization_barrier((results, d_prev))
        return results + (jnp.pad(d_prev, ((most_behind - count, 0), (0, 0), (0, 0))),)

    def summed(part, d_own, d_other):
        low, high = cuts[part], cuts[part + 1]
        total = d_own.astype(f32) + from_other_core(d_other).astype(f32)
        behind = d_prev[max(low - 1, 0) : high - 1].astype(f32)
        if low == 0:
            behind = jnp.pad(behind, ((1, 0), (0, 0), (0, 0)))
        return (total + behind).astype(bf16)

    d_query, d_own, d_other, d_prev = lax.switch(
        branch, [functools.partial(backward, count) for count in counts], d_mixed, pair, prev
    )
    first_sum = (d_own, d_other)
    d_query, d_own, d_other = back(1, (early_mine,), d_query, d_mixed)
    d_kv = [summed(0, *first_sum)]
    second_sum = (d_own, d_other)
    early_low, early_sums = finished(early_mine)
    d_query, d_own, d_other = back(2, (early_low, d_kv[0]), d_query, d_mixed)

    def forward_piece(piece, step):
        return lax.ppermute(piece, "ctx", [(i, i ^ step) for i in range(ctx_size)])

    early = [early_low] + [forward_piece(early_low, step) if step in (1, 2, 4) else None for step in range(1, group)]
    (early[1], early[2], early[4]), d_own, d_other = lax.optimization_barrier(
        ((early[1], early[2], early[4]), d_own, d_other)
    )
    d_kv += [summed(1, *second_sum), summed(2, d_own, d_other)]
    d_heads = exchange(jnp.concatenate([d_query, jnp.concatenate(d_kv, 0)], 1))
    early[3] = forward_piece(early[2], 1)
    early[5] = forward_piece(early[1], 4)
    early[6] = forward_piece(early[4], 2)
    early[7] = forward_piece(early[6], 1)
    d_raw, keep, send = first_back(group, core, d_heads, inputs, vectors, d_hidden, w_qkv, other_qkv)
    (early[3], early[5], early[6]), keep, send = lax.optimization_barrier(((early[3], early[5], early[6]), keep, send))
    late_low, late_sums = finished(gathered(paired(keep, from_other_core(send))))
    late = deal([late_low] * group)
    squares = sum_squares(early_sums, late_sums, early, late)
    results = update(
        group,
        core[1:],
        total_rows,
        squares,
        from_other_core(squares),
        early_sums,
        late_sums,
        d_raw,
        early,
        late,
        [w_qkv, w_out, w_up, w_down, norm_gains, biases],
        [first_qkv, first_out, first_up, first_down, first_gains, first_biases],
        [second_qkv, second_out, second_up, second_down, second_gains, second_biases],
    )
    grad_inputs, norm = results[:2]
    return (outputs, grad_inputs) + tuple(results[2:8]) + (norm[0, 0],) + tuple(results[8:])


def solution(mesh):
    tokens = P(("ctx", "fsdp"), None)
    weight = P("fsdp", None)
    vector = P(None, "fsdp")
    params = (weight, weight, weight, weight, vector, vector)
    in_specs = (tokens, tokens, P(("ctx", "fsdp")), P()) + params * 3
    out_specs = (tokens, tokens) + params + (P(),) + params * 3
    return jax.shard_map(per_device, mesh=mesh, in_specs=in_specs, out_specs=out_specs, check_vma=False)
```

```python
import functools
import math

import jax
import jax.numpy as jnp
from jax import lax
from jax.experimental import pallas as pl
from jax.experimental.pallas import tpu as pltpu
from jax.sharding import PartitionSpec as P

HD = 64
STEP = 10

very_low = -1e30
norm_floor = 1e-05
first_decay = 0.9
second_decay = 0.95
adam_floor = 1e-08
learn_rate = 0.02
weight_decay = 0.1
clip_limit = 0.01
gelu_scale = (2.0 / math.pi) ** 0.5
gelu_cubic = 0.044715

BASE_LIMIT = 1e20
ONES = 16

bf16 = jnp.bfloat16
f32 = jnp.float32
NN = (((1,), (0,)), ((), ()))
NT = (((1,), (1,)), ((), ()))
TN = (((0,), (0,)), ((), ()))


def mxu(left, right, dims):
    return lax.dot_general(left, right, dims, preferred_element_type=f32)


def below_diagonal(scores):
    key_pos = lax.broadcasted_iota(jnp.int32, scores.shape, 0)
    query_pos = lax.broadcasted_iota(jnp.int32, scores.shape, 1)
    return jnp.where(key_pos <= query_pos, scores, very_low)


def column_sum(values):
    return jnp.sum(values, axis=0, keepdims=True)


def column_max(values):
    return jnp.max(values, axis=0, keepdims=True)


def normalize(rows):
    center = rows - jnp.mean(rows, axis=1, keepdims=True)
    inverse = lax.rsqrt(jnp.mean(center * center, axis=1, keepdims=True) + norm_floor)
    return center * inverse, inverse


def span(start, size):
    return pl.ds(pl.multiple_of(start, size), size)


def attend_kernel(starts, place_of, qkv, kv, other_kv, *refs, group, own, final):
    if own:
        acc_in = base_in = None
    else:
        acc_in, base_in = refs[:2]
        refs = refs[2:]
    if final:
        out, log_total = refs[:2]
        pieces = refs[2 : 2 + group]
        low, kv_rows, v_ones, q_pad, acc, high = refs[2 + group :]
    else:
        acc_out, base_out, kv_rows, v_ones, q_pad, acc, high = refs
    tokens = q_pad.shape[1]
    count = kv.shape[0]
    ones = jnp.ones((ONES, tokens), bf16)
    for place in range(count):
        for kind, source in ((0, kv), (1, other_kv)):
            here = source[place, source.shape[1] - 2 * HD :, :]
            kv_rows[kind, place] = here.T
            v_ones[kind, place, :HD, :] = here[HD:]
            v_ones[kind, place, HD:, :] = ones
    q_pad[HD:, :] = jnp.zeros((HD, tokens), bf16)

    def score(kind, place):
        return mxu(kv_rows[kind, place], q_pad[...], NN)

    def weigh(kind, place, scores, base):
        return mxu(v_ones[kind, place], jnp.exp(scores - base).astype(bf16), NN)

    def finish(place):
        if final:
            total = acc[HD : HD + 1, :]
            mixed = acc[:HD, :] * (1.0 / total)
            out[place] = mixed
            low[place] = mixed.astype(bf16)
            log_total[place] = high[...] + jnp.log(total)
        else:
            acc_out[place] = acc[...]
            base_out[place] = high[...]

    def begin(place):
        q_pad[:HD, :] = qkv[place, :HD, :] * bf16(HD**-0.5)
        if not own:
            high[...] = base_in[place]
            acc[...] = acc_in[place]
        return jnp.maximum(starts[place] - (group if own else group - count), 0)

    def quick(place, largest):
        first = begin(place)
        if own:
            scores = below_diagonal(score(0, place))
            base = column_max(scores)
            high[...] = base
            acc[...] = weigh(0, place, scores, base)

        def loop(kinds, first, last):
            def body(key_place, nothing):
                base = high[...]
                acc[...] += sum(weigh(kind, key_place, score(kind, key_place), base) for kind in kinds)
                return nothing

            lax.fori_loop(first, last, body, 0)

        if own:
            loop((1,), place, place + place_of[0])
        loop((0, 1), first, place if own else count)
        finish(place)
        return jnp.maximum(largest, acc[HD : HD + 1, :])

    largest = lax.fori_loop(0, group, quick, jnp.zeros((1, tokens), f32))

    @pl.when(jnp.logical_not(jnp.max(largest) < BASE_LIMIT))
    def _():
        rows = 128

        def careful(place, nothing):
            first = begin(place)
            if own:
                high[...] = jnp.full(high.shape, very_low, f32)
                acc[...] = jnp.zeros(acc.shape, f32)

            def by_kind(kind, nothing):
                def by_place(key_place, nothing):
                    def by_rows(index, nothing):
                        here = span(index * rows, rows)
                        scores = mxu(kv_rows[kind, key_place, here, :], q_pad[...], NN)
                        if own:
                            key_pos = index * rows + lax.broadcasted_iota(jnp.int32, scores.shape, 0)
                            query_pos = lax.broadcasted_iota(jnp.int32, scores.shape, 1)
                            query_pos = query_pos + jnp.where((kind == 0) & (key_place == place), 0, tokens)
                            scores = jnp.where(key_pos <= query_pos, scores, very_low)
                        old = high[...]
                        new = jnp.maximum(old, column_max(scores))
                        probs = jnp.exp(scores - new).astype(bf16)
                        acc[...] = acc[...] * jnp.exp(old - new) + mxu(v_ones[kind, key_place, :, here], probs, NN)
                        high[...] = new
                        return nothing

                    return lax.fori_loop(0, tokens // rows, by_rows, nothing)

                last = place + jnp.where(kind == 0, 1, place_of[0]) if own else count
                return lax.fori_loop(first, last, by_place, nothing)

            lax.fori_loop(0, 2, by_kind, 0)
            finish(place)
            return nothing

        lax.fori_loop(0, group, careful, 0)

    if final:
        for step, piece in enumerate(pieces):
            piece[...] = low[place_of[1] ^ step]


def attend_back_kernel(starts, place_of, qkv, kv, other_kv, out, log_total, *refs, group, own, low, final, resumed):
    pieces = refs[:group]
    d_query_in = refs[group] if resumed else None
    d_query, d_kv, d_other_kv, d_out, kv_rows, q_pad, d_pad, d_kv_sum, d_query_sum = refs[-9:]
    for step, piece in enumerate(pieces):
        d_out[place_of[1] ^ step] = piece[...]
    tokens = q_pad.shape[1]
    count = d_kv.shape[0]
    sources = (kv, other_kv)
    for place in range(count):
        for kind in (0, 1):
            source = sources[kind]
            kv_rows[kind, place] = source[low + place, source.shape[1] - 2 * HD :, :].T
    q_pad[HD:, :] = jnp.zeros((HD, tokens), bf16)
    d_pad[:HD, :] = jnp.zeros((HD, tokens), bf16)
    d_kv_sum[...] = jnp.zeros(d_kv_sum.shape, f32)

    def tile(kind, place, masked, delta, log_row):
        source = sources[kind]
        rows = kv_rows[kind, place]
        scores = mxu(rows, q_pad[...], NN)
        if masked:
            scores = below_diagonal(scores)
        probs = jnp.exp(scores - log_row)
        d_probs = mxu(rows, d_pad[...], NN)
        d_scores = (probs * (d_probs - delta)).astype(bf16)
        d_kv_sum[kind, place] += mxu(q_pad[...], d_scores, NT) + mxu(d_pad[...], probs.astype(bf16), NT)
        first = source.shape[1] - 2 * HD
        return mxu(source[low + place, first : first + HD, :], d_scores, NN)

    def chunk(place, nothing):
        q_pad[:HD, :] = qkv[place, :HD, :] * bf16(HD**-0.5)
        d_here = d_out[place]
        d_pad[HD:, :] = d_here
        delta = column_sum(d_here.astype(f32) * out[place])
        log_row = log_total[place]
        d_query_sum[...] = d_query_in[place] if resumed else jnp.zeros(d_query_sum.shape, f32)

        def loop(kinds, first, last):
            def body(key_place, nothing):
                d_query_sum[...] += sum(tile(kind, key_place, False, delta, log_row) for kind in kinds)
                return nothing

            lax.fori_loop(first, last, body, 0)

        if own:
            here = place - low

            @pl.when(jnp.logical_and(here >= 0, here < count))
            def _():
                d_query_sum[...] += tile(0, here, True, delta, log_row)
                loop((1,), here, here + place_of[0])

            loop((0, 1), jnp.maximum(starts[place] - group - low, 0), jnp.minimum(here, count))
        else:
            loop((0, 1), jnp.maximum(starts[place] - (group - count), 0), count)
        if final:
            d_query[place] = (d_query_sum[...] * HD**-0.5).astype(bf16)
        else:
            d_query[place] = d_query_sum[...]
        return nothing

    lax.fori_loop(0, group, chunk, 0)
    d_kv[...] = d_kv_sum[0].astype(bf16)
    d_other_kv[...] = d_kv_sum[1].astype(bf16)


def first_kernel(core, inputs, vectors, own, other, by_head):
    width = inputs.shape[1]
    half = width // 2
    unit, _ = normalize(inputs[...].astype(f32))
    normed = (unit * vectors[0:1, :] + vectors[2:3, :]).astype(bf16)
    swap = core[0] == 1
    low, high = normed[:, :half], normed[:, half:]
    mine, rest = jnp.where(swap, high, low), jnp.where(swap, low, high)
    for part in range(3):
        columns = slice(part * width, (part + 1) * width)
        rows = mxu(mine, own[:, columns], NN) + mxu(rest, other[:, columns], NN)
        if part != 1:
            row = 3 + part // 2
            rows = rows + vectors[row : row + 1, :]
        turned = rows.astype(bf16).T
        for head in range(width // HD):
            by_head[head, part * HD : (part + 1) * HD, :] = turned[head * HD : (head + 1) * HD]


in_vmem = pl.BlockSpec(memory_space=pltpu.VMEM)
in_smem = pl.BlockSpec(memory_space=pltpu.SMEM)


def norm_back(d_rows, unit, inverse, gain):
    scaled = d_rows * gain
    first = jnp.mean(scaled, axis=1, keepdims=True)
    second = jnp.mean(scaled * unit, axis=1, keepdims=True)
    return inverse * (scaled - first - unit * second)


def feed_kernel(
    core,
    inputs,
    targets,
    valid,
    vectors,
    out_own,
    out_other,
    up_own,
    up_other,
    down_own,
    down_other,
    *refs,
):
    group = inputs.shape[1] // HD
    mixed, refs = refs[:group], refs[group:]
    outputs, d_hidden, keep, send = refs[:4]
    pieces, refs = refs[4 : 4 + group], refs[4 + group :]
    attended, active, normed, normed_turned, d_out_low, small, d_attended, hidden, unit, slope, acc, up_sum = refs
    for index, piece in enumerate(mixed):
        attended[span((core[1] ^ index) * HD, HD), :] = piece[...]
    tokens, width = inputs.shape
    half = width // 2
    f_half = down_own.shape[0]
    step = 512
    rows = f_half // group
    up_rows = half // group
    place = core[0]
    halves = ((place, out_own, up_own, down_own), (1 - place, out_other, up_other, down_other))
    hidden[...] = inputs[...].astype(f32) + vectors[5:6, :]
    for where, w_out, _, _ in halves:
        hidden[...] += mxu(attended[span(where * half, half), :], w_out[...], TN)
    unit_here, inverse = normalize(hidden[...])
    unit[...] = unit_here
    normed_here = (unit_here * vectors[1:2, :] + vectors[6:7, :]).astype(bf16)
    normed[...] = normed_here
    normed_turned[...] = normed_here.T
    for row in range(4):
        up_sum[:, row * width : (row + 1) * width] = vectors[8 + row : 9 + row, :]
    acc[...] = hidden[...] + vectors[7:8, :]
    for where, _, _, w_down in halves:

        def lift(index, nothing):
            columns = span(where * f_half + index * step, step)
            u = up_sum[:, columns]
            for other, _, w_up, _ in halves:
                u = u + mxu(normed[:, span(other * half, half)], w_up[:, columns], NN)
            square = u * u
            tanh = jnp.tanh(gelu_scale * (u + gelu_cubic * (square * u)))
            side = 0.5 * (1.0 + tanh)
            act = (u * side).astype(bf16)
            active[:, columns] = act
            slope[:, columns] = side + (0.5 * gelu_scale) * u * (1.0 - tanh * tanh) * (
                1.0 + (3.0 * gelu_cubic) * square
            )
            acc[...] += mxu(act, w_down[span(index * step, step), :], NN)
            return nothing

        lax.fori_loop(0, f_half // step, lift, 0)
    out_f32 = acc[...]
    outputs[...] = out_f32.astype(bf16)
    d_out = valid[...] * (out_f32 - targets[...].astype(f32))
    d_hidden[...] = d_out
    d_out_low[...] = d_out.astype(bf16)
    small[...] = jnp.zeros(small.shape, f32)
    small[3:4, :] = column_sum(d_out)
    acc[...] = jnp.zeros(acc.shape, f32)
    for target, (where, _, _, w_down) in zip((keep, send), halves):

        def lower(index, nothing):
            columns = span(where * f_half + index * step, step)
            d_active = mxu(d_out_low[...], w_down[span(index * step, step), :], NT)
            low = (d_active * slope[:, columns]).astype(bf16)
            up_sum[:, columns] = column_sum(low.astype(f32))
            for side, (other, _, w_up, _) in zip((keep, send), halves):
                acc[:, span(other * half, half)] += mxu(low, w_up[:, columns], NT)
                gradient = mxu(normed_turned[span(other * half, half), :], low, NN).astype(bf16)
                first = pl.multiple_of(rows + (where * (f_half // step) + index) * up_rows, up_rows)
                for member in range(group):
                    side[member, pl.ds(first, up_rows), :] = gradient[member * up_rows : (member + 1) * up_rows]
            gradient = mxu(active[:, columns], d_out_low[...], TN).astype(bf16)
            for part in range(step // rows):
                target[index * (step // rows) + part, :rows, :] = gradient[part * rows : (part + 1) * rows]
            return nothing

        lax.fori_loop(0, f_half // step, lower, 0)
    for row in range(4):
        small[4 + row : 5 + row, :] = up_sum[:, row * width : (row + 1) * width]
    d_normed = acc[...]
    unit_here = unit[...]
    small[0:1, :] = column_sum(d_normed * unit_here)
    small[2:3, :] = column_sum(d_normed)
    d_rows = d_hidden[...] + norm_back(d_normed, unit_here, inverse, vectors[1:2, :])
    d_hidden[...] = d_rows
    small[1:2, :] = column_sum(d_rows)
    low = d_rows.astype(bf16)
    for where, w_out, _, _ in halves:
        d_attended[span(where * half, half), :] = mxu(w_out[...], low, NT).astype(bf16)
    for index, piece in enumerate(pieces):
        piece[...] = d_attended[span((core[1] ^ index) * HD, HD), :]
    lanes = lax.broadcasted_iota(jnp.int32, (tokens, 128), 1)
    token = lax.broadcasted_iota(jnp.int32, (tokens, 128), 0)
    counts = column_sum(jnp.where(token % 128 == lanes, valid[...], 0.0))
    small[8:9, :128] = counts
    small[8:9, half : half + 128] = counts
    first = rows + up_rows * (2 * f_half // width)
    for target, (where, _, _, _) in zip((keep, send), halves):
        here = span(where * half, half)
        spread_rows(target, mxu(attended[here, :], low, NN), first, up_rows, 0)
        sums = jnp.concatenate([small[:, here], jnp.zeros(small[:, here].shape, f32)], 1).astype(bf16)
        for member in range(group):
            target[member, first + up_rows :, :] = sums


def spread_rows(target, gradient, first, rows, me):
    low = gradient.astype(bf16)
    for member in range(target.shape[0]):
        target[member ^ me, first : first + rows, :] = low[member * rows : (member + 1) * rows]


def first_back_kernel(core, d_heads, inputs, vectors, d_hidden, own, other, d_inputs, keep, send, d_proj, d_normed):
    width = inputs.shape[1]
    half = width // 2
    members = keep.shape[0]
    place = core[0]
    for head in range(width // HD):
        for part in range(3):
            d_proj[part * width + head * HD : part * width + (head + 1) * HD, :] = d_heads[
                head, part * HD : (part + 1) * HD, :
            ]
    unit, inverse = normalize(inputs[...].astype(f32))
    normed = (unit * vectors[0:1, :] + vectors[2:3, :]).astype(bf16).T
    for where, weight in ((place, own), (1 - place, other)):
        d_normed[span(where * half, half), :] = mxu(weight[...], d_proj[...], NN)
    d_rows = d_normed[:width, :].T
    d_inputs[...] = d_hidden[...] + norm_back(d_rows, unit, inverse, vectors[0:1, :])
    gain_sum = column_sum(d_rows * unit)
    offset_sum = column_sum(d_rows)
    ones = jnp.ones((ONES, inputs.shape[0]), bf16)
    query_sum = mxu(ones, d_proj[:width], NT)[:1]
    value_sum = mxu(ones, d_proj[2 * width :], NT)[:1]
    sums = jnp.concatenate([gain_sum, offset_sum, query_sum, value_sum, jnp.zeros((ONES - 4, width), f32)], 0)
    rows = half // members
    d_normed[:ONES, :] = sums
    for part in range(3):
        gradient = mxu(normed, d_proj[part * width : (part + 1) * width], NT)
        d_normed[ONES : ONES + width, :] = gradient
        for target, where in ((keep, place), (send, 1 - place)):
            low = d_normed[pl.ds(pl.multiple_of(ONES + where * half, ONES), half), :]
            spread_rows(target, low, part * rows, rows, core[1])
    for target, where in ((keep, place), (send, 1 - place)):
        low = d_normed[:ONES, span(where * half, half)]
        low = jnp.concatenate([low, jnp.zeros(low.shape, f32)], 1).astype(bf16)
        for member in range(members):
            target[member, 3 * rows :, :] = low


def squares_kernel(sums_early, sums_late, *refs):
    pieces, squares = refs[:-1], refs[-1]
    group = len(pieces) // 2
    half = sums_early.shape[1] // 2

    def square_sum(values):
        values = values.astype(f32)
        return jnp.sum(column_sum(values * values), axis=1, keepdims=True)

    parts = [square_sum(early[...]) + square_sum(late[...]) for early, late in zip(pieces[:group], pieces[group:])]
    total = paired_sum(parts) + (square_sum(sums_early[:8, :half]) + square_sum(sums_late[:4, :half]))
    squares[...] = jnp.broadcast_to(total, squares.shape)


def paired_sum(parts):
    while len(parts) > 1:
        parts = [parts[i] + parts[i + 1] for i in range(0, len(parts), 2)]
    return parts[0]


def update_kernel(me, squares, other_squares, sums_early, sums_late, d_raw, *refs, group, total_rows):
    early_pieces, late_pieces, refs = refs[:group], refs[group : 2 * group], refs[2 * group :]
    weights, firsts, seconds, refs = refs[0:6], refs[6:12], refs[12:18], refs[18:]
    grad_inputs, norm = refs[:2]
    grads, new_firsts, new_seconds, steps = refs[2:8], refs[8:14], refs[14:20], refs[20:26]
    early, late, raw_out = refs[26:29]
    buffers, sems = refs[29:33], refs[33]
    for index in range(group):
        early[index] = early_pieces[index][...]
        late[index] = late_pieces[index][...]

    count_scale = total_rows / jnp.sum(sums_early[8:9, :128], axis=1, keepdims=True)
    total = squares[:1, :1] + other_squares[:1, :1]
    grad_norm = jnp.sqrt(total) * count_scale / total_rows
    scale_back = jnp.minimum(1.0, clip_limit / grad_norm) / total_rows
    width = d_raw.shape[1]
    raw_rows = d_raw.shape[0] // group
    down_rows = weights[3].shape[0] // group
    after_up = down_rows + weights[2].shape[0] // group * (weights[2].shape[1] // width)

    def copies(slot, member):
        moves = [pltpu.make_async_copy(raw_out.at[slot], grad_inputs.at[span(member * raw_rows, raw_rows)], sems.at[slot, 0])]
        for index in range(4):
            rows = weights[index].shape[0] // group
            for kind, target in enumerate((grads, new_firsts, new_seconds, steps)):
                moves.append(
                    pltpu.make_async_copy(
                        buffers[index].at[slot, kind],
                        target[index].at[span(member * rows, rows)],
                        sems.at[slot, 1 + 4 * index + kind],
                    )
                )
        return moves

    def step(number, nothing):
        slot = number & 1
        member = me[0] ^ number

        @pl.when(number >= 2)
        def _():
            for move in copies(slot, member):
                move.wait()

        raw_out[slot] = d_raw[span(member * raw_rows, raw_rows), :] * count_scale
        for index, (source, first) in enumerate(((late, 0), (early, after_up), (early, down_rows), (early, 0))):
            rows = weights[index].shape[0] // group
            here = span(member * rows, rows)
            for block in range(weights[index].shape[1] // width):
                columns = slice(block * width, (block + 1) * width)
                gradient = source[number, first + block * rows : first + (block + 1) * rows, :].astype(f32) * count_scale
                results = adam_step(
                    weights[index][here, columns],
                    gradient,
                    firsts[index][here, columns],
                    seconds[index][here, columns],
                    scale_back,
                    weight_decay,
                )
                for kind, result in enumerate((gradient,) + results):
                    buffers[index][slot, kind, :, columns] = result
        for move in copies(slot, member):
            move.start()
        return nothing

    lax.fori_loop(0, group, step, 0)
    half = width // 2
    norm[...] = jnp.broadcast_to(grad_norm, norm.shape)

    def change(index, row, raw):
        where = (slice(row, row + 1), slice(None))
        gradient = raw * count_scale
        grads[index][where] = gradient
        results = adam_step(
            weights[index][where], gradient, firsts[index][where], seconds[index][where], scale_back, 0.0
        )
        new_firsts[index][where], new_seconds[index][where], steps[index][where] = results

    change(4, 0, sums_late[0:1, :half])
    change(4, 1, sums_early[0:1, :half])
    for row in range(3):
        change(5, row, sums_late[1 + row : 2 + row, :half])
    for row in range(3, 10):
        change(5, row, sums_early[row - 2 : row - 1, :half])
    for slot in (0, 1):
        for move in copies(slot, me[0] ^ slot):
            move.wait()


def adam_step(weight, gradient, first_old, second_old, scale_back, decay_rate):
    clipped = gradient * scale_back
    new_first = first_decay * first_old + (1.0 - first_decay) * clipped
    new_second = second_decay * second_old + ((1.0 - second_decay) * clipped) * clipped
    second_hat = new_second * (1.0 / (1.0 - second_decay**STEP))
    below = second_hat * lax.rsqrt(second_hat) + adam_floor
    inverse = pl.reciprocal(below, approx=True)
    inverse = inverse * (2.0 - below * inverse)
    inverse = inverse * (2.0 - below * inverse)
    update = (new_first * (-learn_rate / (1.0 - first_decay**STEP))) * inverse
    if decay_rate:
        update = update - (learn_rate * decay_rate) * weight.astype(f32)
    return (new_first, new_second, update)


def shaped(shape, kind):
    return jax.ShapeDtypeStruct(shape, kind)


in_place = pl.BlockSpec(memory_space=pl.ANY)


def attend(starts, core, qkv, kv, other_kv, state=None, final=True):
    group, _, tokens = qkv.shape
    count = kv.shape[0]
    row = shaped((group, 1, tokens), f32)
    if final:
        out_shape = (shaped((group, HD, tokens), f32), row) + (shaped((HD, tokens), bf16),) * group
    else:
        out_shape = (shaped((group, HD + ONES, tokens), f32), row)
    state = state or ()
    return pl.pallas_call(
        functools.partial(attend_kernel, group=group, own=not state, final=final),
        out_shape=out_shape,
        in_specs=[in_smem, in_smem] + [in_vmem] * (3 + len(state)),
        out_specs=(in_vmem,) * len(out_shape),
        scratch_shapes=([pltpu.VMEM((group, HD, tokens), bf16)] if final else [])
        + [
            pltpu.VMEM((2, count, tokens, 2 * HD), bf16),
            pltpu.VMEM((2, count, HD + ONES, tokens), bf16),
            pltpu.VMEM((2 * HD, tokens), bf16),
            pltpu.VMEM((HD + ONES, tokens), f32),
            pltpu.VMEM((1, tokens), f32),
        ],
        cost_estimate=pl.CostEstimate(flops=30 * 2**30, bytes_accessed=5 * 2**20, transcendentals=2**24),
        compiler_params=pltpu.CompilerParams(vmem_limit_bytes=24 * 2**20),
        name="attend",
    )(starts, core, qkv, kv, other_kv, *state)


def attend_back(starts, core, qkv, kv, other_kv, d_out, out, log_total, after, d_query=None, own=True, low=0, count=0, final=False):
    group, _, tokens = qkv.shape
    resumed = d_query is not None
    return pl.pallas_call(
        functools.partial(attend_back_kernel, group=group, own=own, low=low, final=final, resumed=resumed),
        out_shape=(
            shaped((group, HD, tokens), bf16 if final else f32),
            shaped((count, 2 * HD, tokens), bf16),
            shaped((count, 2 * HD, tokens), bf16),
        ),
        in_specs=[in_smem, in_smem] + [in_vmem] * (5 + group + resumed) + [in_place] * len(after),
        out_specs=(in_vmem,) * 3,
        scratch_shapes=[
            pltpu.VMEM((group, HD, tokens), bf16),
            pltpu.VMEM((2, count, tokens, 2 * HD), bf16),
            pltpu.VMEM((2 * HD, tokens), bf16),
            pltpu.VMEM((2 * HD, tokens), bf16),
            pltpu.VMEM((2, count, 2 * HD, tokens), f32),
            pltpu.VMEM((HD, tokens), f32),
        ],
        cost_estimate=pl.CostEstimate(flops=count * 8 * 2**30, bytes_accessed=8 * 2**20, transcendentals=2**24),
        compiler_params=pltpu.CompilerParams(vmem_limit_bytes=32 * 2**20),
        name="attend_back",
    )(starts, core, qkv, kv, other_kv, out, log_total, *d_out, *((d_query,) if resumed else ()), *after)


def project(core, inputs, vectors, own, other):
    tokens, width = inputs.shape
    return pl.pallas_call(
        first_kernel,
        out_shape=shaped((width // HD, 3 * HD, tokens), bf16),
        in_specs=[in_smem] + [in_vmem] * 4,
        out_specs=in_vmem,
        cost_estimate=pl.CostEstimate(flops=2**30, bytes_accessed=4 * 2**20, transcendentals=0),
        compiler_params=pltpu.CompilerParams(vmem_limit_bytes=16 * 2**20),
        name="project",
    )(core, inputs, vectors, own, other)


def feed(core, mixed, inputs, targets, valid, vectors, *weights):
    tokens, width = inputs.shape
    group = width // HD
    hidden_units = weights[2].shape[1]
    rows = (2 * hidden_units + width) // 2 // group + 16
    return pl.pallas_call(
        feed_kernel,
        out_shape=(shaped((tokens, width), bf16), shaped((tokens, width), f32))
        + (shaped((group, rows, width), bf16),) * 2
        + (shaped((HD, tokens), bf16),) * group,
        in_specs=[in_smem] + [in_vmem] * (10 + group),
        out_specs=(in_vmem,) * (4 + group),
        scratch_shapes=[
            pltpu.VMEM((width, tokens), bf16),
            pltpu.VMEM((tokens, hidden_units), bf16),
            pltpu.VMEM((tokens, width), bf16),
            pltpu.VMEM((width, tokens), bf16),
            pltpu.VMEM((tokens, width), bf16),
            pltpu.VMEM((16, width), f32),
            pltpu.VMEM((width, tokens), bf16),
            pltpu.VMEM((tokens, width), f32),
            pltpu.VMEM((tokens, width), f32),
            pltpu.VMEM((tokens, hidden_units), f32),
            pltpu.VMEM((tokens, width), f32),
            pltpu.VMEM((1, hidden_units), f32),
        ],
        cost_estimate=pl.CostEstimate(flops=10 * 2**30, bytes_accessed=14 * 2**20, transcendentals=2**20),
        compiler_params=pltpu.CompilerParams(vmem_limit_bytes=34 * 2**20),
        name="feed",
    )(core, inputs, targets, valid, vectors, *weights, *mixed)


def first_back(group, core, d_heads, inputs, vectors, d_hidden, own, other):
    tokens, width = inputs.shape
    rows = own.shape[0] // group * 3 + 16
    return pl.pallas_call(
        first_back_kernel,
        out_shape=(shaped((tokens, width), f32),) + (shaped((group, rows, width), bf16),) * 2,
        in_specs=[in_smem] + [in_vmem] * 6,
        out_specs=(in_vmem,) * 3,
        scratch_shapes=[pltpu.VMEM((3 * width, tokens), bf16), pltpu.VMEM((width + 16, tokens), f32)],
        cost_estimate=pl.CostEstimate(flops=4 * 2**30, bytes_accessed=8 * 2**20, transcendentals=0),
        compiler_params=pltpu.CompilerParams(vmem_limit_bytes=24 * 2**20),
        name="first_back",
    )(core, d_heads, inputs, vectors, d_hidden, own, other)


def sum_squares(sums_early, sums_late, early, late):
    return pl.pallas_call(
        squares_kernel,
        out_shape=shaped((8, 128), f32),
        in_specs=[in_vmem] * (2 + 2 * len(early)),
        out_specs=in_vmem,
        cost_estimate=pl.CostEstimate(flops=2**22, bytes_accessed=4 * 2**20, transcendentals=0),
        compiler_params=pltpu.CompilerParams(vmem_limit_bytes=16 * 2**20),
        name="sum_squares",
    )(sums_early, sums_late, *early, *late)


def update(group, me, total_rows, squares, other_squares, sums_early, sums_late, d_raw, early, late, *state):
    weights = state[0]
    like = [shaped(weight.shape, f32) for weight in weights]
    out_specs = [in_place] * 4 + [in_vmem] * 2
    return pl.pallas_call(
        functools.partial(update_kernel, group=group, total_rows=total_rows),
        out_shape=[shaped(d_raw.shape, f32), shaped((8, 128), f32)] + like * 4,
        in_specs=[in_smem] + [in_vmem] * (5 + 2 * group + 18),
        out_specs=[in_place, in_vmem] + out_specs * 4,
        scratch_shapes=[
            pltpu.VMEM((group,) + early[0].shape, bf16),
            pltpu.VMEM((group,) + late[0].shape, bf16),
            pltpu.VMEM((2, d_raw.shape[0] // group, d_raw.shape[1]), f32),
        ]
        + [pltpu.VMEM((2, 4, weight.shape[0] // group, weight.shape[1]), f32) for weight in weights[:4]]
        + [pltpu.SemaphoreType.DMA((2, 17))],
        cost_estimate=pl.CostEstimate(flops=2**26, bytes_accessed=44 * 2**20, transcendentals=2**22),
        compiler_params=pltpu.CompilerParams(vmem_limit_bytes=31 * 2**20),
        name="update",
    )(me, squares, other_squares, sums_early, sums_late, d_raw, *early, *late, *state[0], *state[1], *state[2])


def from_other_core(value):
    return lax.ppermute(value, "fsdp", [(0, 1), (1, 0)])


def whole_of(value, axis):
    other = from_other_core(value)
    first = lax.axis_index("fsdp") == 0
    return jnp.concatenate([jnp.where(first, value, other), jnp.where(first, other, value)], axis)


def swap_ctx(value, bit):
    size = lax.axis_size("ctx")
    return lax.ppermute(value, "ctx", [(i, i ^ bit) for i in range(size)])


def across_groups(value, group):
    low, sums = value[:-16].astype(bf16), value[-16:]
    bit = group
    while bit < lax.axis_size("ctx"):
        sent = value.astype(bf16)
        received = swap_ctx(sent, bit)
        low = (sent[:-16].astype(f32) + received[:-16].astype(f32)).astype(bf16)
        sums = sent[-16:].astype(f32) + received[-16:].astype(f32)
        value = jnp.concatenate([low.astype(f32), sums], 0) if 2 * bit < lax.axis_size("ctx") else None
        bit *= 2
    return low, sums


def per_device(
    inputs,
    targets,
    valid_mask,
    block_seq,
    w_qkv,
    w_out,
    w_up,
    w_down,
    norm_gains,
    biases,
    first_qkv,
    first_out,
    first_up,
    first_down,
    first_gains,
    first_biases,
    second_qkv,
    second_out,
    second_up,
    second_down,
    second_gains,
    second_biases,
):
    rows_here, width = inputs.shape
    group = width // HD
    ctx_size = lax.axis_size("ctx")
    block_rows = rows_here * 2
    total_rows = float(block_rows * ctx_size)
    ctx_place = lax.axis_index("ctx")
    core_place = lax.axis_index("fsdp")
    members = [[first + i for i in range(group)] for first in range(0, ctx_size, group)]

    def exchange(value):
        return lax.all_to_all(value, "ctx", 0, 0, axis_index_groups=members, tiled=True)

    core = jnp.stack([core_place, ctx_place % group]).astype(jnp.int32)
    vectors = whole_of(jnp.concatenate([norm_gains, biases], 0), 1).astype(f32)
    other_qkv = from_other_core(w_qkv)
    other_out, other_up, other_down = (from_other_core(w_out), from_other_core(w_up), from_other_core(w_down))
    valid_rows = valid_mask.astype(f32)
    qkv = exchange(project(core, inputs, vectors, w_qkv, other_qkv))
    own_kv = qkv[:, HD:]
    other_kv = from_other_core(own_kv)

    first_block = (ctx_place // group) * group
    own_seq = lax.dynamic_slice_in_dim(block_seq, first_block, group, 0)
    starts = jnp.sum((block_seq[None, :] < own_seq[:, None]).astype(jnp.int32), axis=1)
    starts = jnp.maximum(starts - first_block + group, 0)
    behind = jnp.zeros((), jnp.int32)
    for edge in range(group, ctx_size, group):
        same = (block_seq[edge - group : edge] == block_seq[edge]).astype(jnp.int32)
        behind = jnp.maximum(behind, jnp.sum(same))
    most_behind = group - 1
    few_behind = group // 2
    branch = (behind > 0).astype(jnp.int32) + (behind > few_behind).astype(jnp.int32)
    counts = (0, few_behind, most_behind)

    def forward(count, own, other):
        if count == 0:
            nothing = jnp.zeros((most_behind, 2 * HD, rows_here), bf16)
            return tuple(attend(starts, core, qkv, qkv, other)) + (nothing, nothing)
        prev_own = lax.ppermute(own[group - count :], "ctx", [(i, i + group) for i in range(ctx_size - group)])
        state = attend(starts, core, qkv, qkv, other, final=False)
        prev_own, state = lax.optimization_barrier((prev_own, state))
        prev_other = from_other_core(prev_own)
        mixed = attend(starts, core, qkv, prev_own, prev_other, state=state)
        short = ((most_behind - count, 0), (0, 0), (0, 0))
        return tuple(mixed) + (jnp.pad(prev_own, short), jnp.pad(prev_other, short))

    results = lax.switch(branch, [functools.partial(forward, count) for count in counts], own_kv, other_kv)
    mixed, log_total = results[:2]
    prev = results[2 + group :]

    def deal(pieces):
        moved = []
        for step in range(1, group):
            moved.append(lax.ppermute(pieces[step], "ctx", [(i, i ^ step) for i in range(ctx_size)]))
        return [pieces[0]] + moved

    results = feed(
        core,
        deal(results[2 : 2 + group]),
        inputs,
        targets,
        valid_rows[:, None],
        vectors,
        w_out,
        other_out,
        w_up,
        other_up,
        w_down,
        other_down,
    )
    outputs, d_hidden, keep, send = results[:4]
    d_mixed = deal(results[4:])

    def paired(keep, received):
        return [(keep[i].astype(f32) + received[i].astype(f32)).astype(bf16) for i in range(group)]

    def gathered(pairs):
        return paired_sum([piece.astype(f32) for piece in deal(pairs)])

    def finished(mine):
        return across_groups(mine, group)

    received, d_mixed = lax.optimization_barrier((from_other_core(send), d_mixed))
    pair = (keep.astype(f32) + received.astype(f32)).astype(bf16)
    early_mine = jnp.sum(exchange(pair).astype(f32), axis=0)
    cuts = (0, 3, 5, group)

    def back(part, after, d_query, d_mixed):
        low, high = cuts[part], cuts[part + 1]
        return attend_back(
            starts,
            core,
            qkv,
            qkv,
            other_kv,
            d_mixed,
            mixed,
            log_total,
            after,
            d_query=d_query,
            low=low,
            count=high - low,
            final=high == group,
        )

    def backward(count, d_mixed, pair, prev):
        if count == 0:
            return tuple(back(0, (pair,), None, d_mixed)) + tuple(
                jnp.zeros((high - low, 2 * HD, rows_here), bf16) for low, high in zip(cuts[1:-1], cuts[2:])
            )
        prev_own, prev_other = prev
        d_query, d_behind, d_behind_other = attend_back(
            starts,
            core,
            qkv,
            prev_own,
            prev_other,
            d_mixed,
            mixed,
            log_total,
            (pair,),
            own=False,
            low=most_behind - count,
            count=count,
        )
        d_prev = (d_behind.astype(f32) + from_other_core(d_behind_other).astype(f32)).astype(bf16)
        d_prev = lax.ppermute(d_prev, "ctx", [(i + group, i) for i in range(ctx_size - group)])
        results = tuple(back(0, (pair,), d_query, d_mixed))
        (d_query, d_own, d_other), d_prev = lax.optimization_barrier((results, d_prev))
        d_prev = jnp.pad(d_prev, ((group - count, 0), (0, 0), (0, 0)))
        d_own = (d_own.astype(f32) + d_prev[: cuts[1]].astype(f32)).astype(bf16)
        return (d_query, d_own, d_other) + tuple(d_prev[low:high] for low, high in zip(cuts[1:-1], cuts[2:]))

    def summed(d_own, d_other, *more):
        return sum((one.astype(f32) for one in more), d_own.astype(f32) + from_other_core(d_other).astype(f32)).astype(bf16)

    d_query, d_own, d_other, *d_prev = lax.switch(
        branch, [functools.partial(backward, count) for count in counts], d_mixed, pair, prev
    )
    first_sum = (d_own, d_other)
    d_query, d_own, d_other = back(1, (early_mine,), d_query, d_mixed)
    d_kv = [summed(*first_sum)]
    second_sum = (d_own, d_other)
    early_low, early_sums = finished(early_mine)
    d_query, d_own, d_other = back(2, (early_low, d_kv[0]), d_query, d_mixed)

    def forward_piece(piece, step):
        return lax.ppermute(piece, "ctx", [(i, i ^ step) for i in range(ctx_size)])

    early = [early_low] + [forward_piece(early_low, step) if step in (1, 2, 4) else None for step in range(1, group)]
    (early[1], early[2], early[4]), d_own, d_other = lax.optimization_barrier(
        ((early[1], early[2], early[4]), d_own, d_other)
    )
    d_kv += [summed(*second_sum, d_prev[0]), summed(d_own, d_other, d_prev[1])]
    d_heads = exchange(jnp.concatenate([d_query, jnp.concatenate(d_kv, 0)], 1))
    early[3] = forward_piece(early[2], 1)
    early[5] = forward_piece(early[1], 4)
    early[6] = forward_piece(early[4], 2)
    early[7] = forward_piece(early[6], 1)
    d_raw, keep, send = first_back(group, core, d_heads, inputs, vectors, d_hidden, w_qkv, other_qkv)
    (early[3], early[5], early[6]), keep, send = lax.optimization_barrier(((early[3], early[5], early[6]), keep, send))
    late_low, late_sums = finished(gathered(paired(keep, from_other_core(send))))
    late = deal([late_low] * group)
    squares = sum_squares(early_sums, late_sums, early, late)
    results = update(
        group,
        core[1:],
        total_rows,
        squares,
        from_other_core(squares),
        early_sums,
        late_sums,
        d_raw,
        early,
        late,
        [w_qkv, w_out, w_up, w_down, norm_gains, biases],
        [first_qkv, first_out, first_up, first_down, first_gains, first_biases],
        [second_qkv, second_out, second_up, second_down, second_gains, second_biases],
    )
    grad_inputs, norm = results[:2]
    return (outputs, grad_inputs) + tuple(results[2:8]) + (norm[0, 0],) + tuple(results[8:])


def solution(mesh):
    tokens = P(("ctx", "fsdp"), None)
    weight = P("fsdp", None)
    vector = P(None, "fsdp")
    params = (weight, weight, weight, weight, vector, vector)
    in_specs = (tokens, tokens, P(("ctx", "fsdp")), P()) + params * 3
    out_specs = (tokens, tokens) + params + (P(),) + params * 3
    return jax.shard_map(per_device, mesh=mesh, in_specs=in_specs, out_specs=out_specs, check_vma=False)
```

```python
import functools
import math

import jax
import jax.numpy as jnp
from jax import lax
from jax.experimental import pallas as pl
from jax.experimental.pallas import tpu as pltpu
from jax.sharding import PartitionSpec as P

HD = 64
STEP = 10

very_low = -1e30
norm_floor = 1e-05
first_decay = 0.9
second_decay = 0.95
adam_floor = 1e-08
learn_rate = 0.02
weight_decay = 0.1
clip_limit = 0.01
gelu_scale = (2.0 / math.pi) ** 0.5
gelu_cubic = 0.044715

BASE_LIMIT = 1e20
ONES = 16

bf16 = jnp.bfloat16
f32 = jnp.float32
NN = (((1,), (0,)), ((), ()))
NT = (((1,), (1,)), ((), ()))
TN = (((0,), (0,)), ((), ()))


def mxu(left, right, dims):
    return lax.dot_general(left, right, dims, preferred_element_type=f32)


def below_diagonal(scores):
    key_pos = lax.broadcasted_iota(jnp.int32, scores.shape, 0)
    query_pos = lax.broadcasted_iota(jnp.int32, scores.shape, 1)
    return jnp.where(key_pos <= query_pos, scores, very_low)


def column_sum(values):
    return jnp.sum(values, axis=0, keepdims=True)


def column_max(values):
    return jnp.max(values, axis=0, keepdims=True)


def normalize(rows):
    center = rows - jnp.mean(rows, axis=1, keepdims=True)
    inverse = lax.rsqrt(jnp.mean(center * center, axis=1, keepdims=True) + norm_floor)
    return center * inverse, inverse


def span(start, size):
    return pl.ds(pl.multiple_of(start, size), size)


def attend_kernel(starts, place_of, qkv, kv, other_kv, *refs, group, own, final, spare):
    if own:
        acc_in = base_in = None
    else:
        acc_in, base_in = refs[:2]
        refs = refs[2:]
    if final:
        out, log_total = refs[:2]
        pieces = refs[2 : 2 + group]
        low, kv_rows, v_ones, q_pad, acc, high = refs[2 + group + spare :]
    else:
        acc_out, base_out, kv_rows, v_ones, q_pad, acc, high = refs
    tokens = q_pad.shape[1]
    count = kv.shape[0]
    ones = jnp.ones((ONES, tokens), bf16)
    for place in range(count):
        for kind, source in ((0, kv), (1, other_kv)):
            here = source[place, source.shape[1] - 2 * HD :, :]
            kv_rows[kind, place] = here.T
            v_ones[kind, place, :HD, :] = here[HD:]
            v_ones[kind, place, HD:, :] = ones
    q_pad[HD:, :] = jnp.zeros((HD, tokens), bf16)

    def score(kind, place):
        return mxu(kv_rows[kind, place], q_pad[...], NN)

    def weigh(kind, place, scores, base):
        return mxu(v_ones[kind, place], jnp.exp(scores - base).astype(bf16), NN)

    def finish(place):
        if final:
            total = acc[HD : HD + 1, :]
            mixed = acc[:HD, :] * (1.0 / total)
            out[place] = mixed
            low[place] = mixed.astype(bf16)
            log_total[place] = high[...] + jnp.log(total)
        else:
            acc_out[place] = acc[...]
            base_out[place] = high[...]

    def begin(place):
        q_pad[:HD, :] = qkv[place, :HD, :] * bf16(HD**-0.5)
        if not own:
            high[...] = base_in[place]
            acc[...] = acc_in[place]
        return jnp.maximum(starts[place] - (group if own else group - count), 0)

    def quick(place, largest):
        first = begin(place)
        if own:
            scores = below_diagonal(score(0, place))
            base = column_max(scores)
            high[...] = base
            acc[...] = weigh(0, place, scores, base)

        def loop(kinds, first, last):
            def body(key_place, nothing):
                base = high[...]
                acc[...] += sum(weigh(kind, key_place, score(kind, key_place), base) for kind in kinds)
                return nothing

            lax.fori_loop(first, last, body, 0)

        if own:
            loop((1,), place, place + place_of[0])
        loop((0, 1), first, place if own else count)
        finish(place)
        return jnp.maximum(largest, acc[HD : HD + 1, :])

    largest = lax.fori_loop(0, group, quick, jnp.zeros((1, tokens), f32))

    @pl.when(jnp.logical_not(jnp.max(largest) < BASE_LIMIT))
    def _():
        rows = 128

        def careful(place, nothing):
            first = begin(place)
            if own:
                high[...] = jnp.full(high.shape, very_low, f32)
                acc[...] = jnp.zeros(acc.shape, f32)

            def by_kind(kind, nothing):
                def by_place(key_place, nothing):
                    def by_rows(index, nothing):
                        here = span(index * rows, rows)
                        scores = mxu(kv_rows[kind, key_place, here, :], q_pad[...], NN)
                        if own:
                            key_pos = index * rows + lax.broadcasted_iota(jnp.int32, scores.shape, 0)
                            query_pos = lax.broadcasted_iota(jnp.int32, scores.shape, 1)
                            query_pos = query_pos + jnp.where((kind == 0) & (key_place == place), 0, tokens)
                            scores = jnp.where(key_pos <= query_pos, scores, very_low)
                        old = high[...]
                        new = jnp.maximum(old, column_max(scores))
                        probs = jnp.exp(scores - new).astype(bf16)
                        acc[...] = acc[...] * jnp.exp(old - new) + mxu(v_ones[kind, key_place, :, here], probs, NN)
                        high[...] = new
                        return nothing

                    return lax.fori_loop(0, tokens // rows, by_rows, nothing)

                last = place + jnp.where(kind == 0, 1, place_of[0]) if own else count
                return lax.fori_loop(first, last, by_place, nothing)

            lax.fori_loop(0, 2, by_kind, 0)
            finish(place)
            return nothing

        lax.fori_loop(0, group, careful, 0)

    if final:
        for step, piece in enumerate(pieces):
            piece[...] = low[place_of[1] ^ step]


def attend_back_kernel(starts, place_of, qkv, kv, other_kv, out, log_total, *refs, group, own, low, final, resumed):
    pieces = refs[:group]
    d_query_in = refs[group] if resumed else None
    d_query, d_kv, d_other_kv, d_out, kv_rows, q_pad, d_pad, d_kv_sum, d_query_sum = refs[-9:]
    for step, piece in enumerate(pieces):
        d_out[place_of[1] ^ step] = piece[...]
    tokens = q_pad.shape[1]
    count = d_kv.shape[0]
    sources = (kv, other_kv)
    for place in range(count):
        for kind in (0, 1):
            source = sources[kind]
            kv_rows[kind, place] = source[low + place, source.shape[1] - 2 * HD :, :].T
    q_pad[HD:, :] = jnp.zeros((HD, tokens), bf16)
    d_pad[:HD, :] = jnp.zeros((HD, tokens), bf16)
    d_kv_sum[...] = jnp.zeros(d_kv_sum.shape, f32)

    def tile(kind, place, masked, delta, log_row):
        source = sources[kind]
        rows = kv_rows[kind, place]
        scores = mxu(rows, q_pad[...], NN)
        if masked:
            scores = below_diagonal(scores)
        probs = jnp.exp(scores - log_row)
        d_probs = mxu(rows, d_pad[...], NN)
        d_scores = (probs * (d_probs - delta)).astype(bf16)
        d_kv_sum[kind, place] += mxu(q_pad[...], d_scores, NT) + mxu(d_pad[...], probs.astype(bf16), NT)
        first = source.shape[1] - 2 * HD
        return mxu(source[low + place, first : first + HD, :], d_scores, NN)

    def chunk(place, nothing):
        q_pad[:HD, :] = qkv[place, :HD, :] * bf16(HD**-0.5)
        d_here = d_out[place]
        d_pad[HD:, :] = d_here
        delta = column_sum(d_here.astype(f32) * out[place])
        log_row = log_total[place]
        d_query_sum[...] = d_query_in[place] if resumed else jnp.zeros(d_query_sum.shape, f32)

        def loop(kinds, first, last):
            def body(key_place, nothing):
                d_query_sum[...] += sum(tile(kind, key_place, False, delta, log_row) for kind in kinds)
                return nothing

            lax.fori_loop(first, last, body, 0)

        if own:
            here = place - low

            @pl.when(jnp.logical_and(here >= 0, here < count))
            def _():
                d_query_sum[...] += tile(0, here, True, delta, log_row)
                loop((1,), here, here + place_of[0])

            loop((0, 1), jnp.maximum(starts[place] - group - low, 0), jnp.minimum(here, count))
        else:
            loop((0, 1), jnp.maximum(starts[place] - (group - count), 0), count)
        if final:
            d_query[place] = (d_query_sum[...] * HD**-0.5).astype(bf16)
        else:
            d_query[place] = d_query_sum[...]
        return nothing

    lax.fori_loop(0, group, chunk, 0)
    d_kv[...] = d_kv_sum[0].astype(bf16)
    d_other_kv[...] = d_kv_sum[1].astype(bf16)


def first_kernel(core, inputs, vectors, own, other, by_head):
    width = inputs.shape[1]
    half = width // 2
    unit, _ = normalize(inputs[...].astype(f32))
    normed = (unit * vectors[0:1, :] + vectors[2:3, :]).astype(bf16)
    swap = core[0] == 1
    low, high = normed[:, :half], normed[:, half:]
    mine, rest = jnp.where(swap, high, low), jnp.where(swap, low, high)
    for part in range(3):
        columns = slice(part * width, (part + 1) * width)
        rows = mxu(mine, own[:, columns], NN) + mxu(rest, other[:, columns], NN)
        if part != 1:
            row = 3 + part // 2
            rows = rows + vectors[row : row + 1, :]
        turned = rows.astype(bf16).T
        for head in range(width // HD):
            by_head[head, part * HD : (part + 1) * HD, :] = turned[head * HD : (head + 1) * HD]


in_vmem = pl.BlockSpec(memory_space=pltpu.VMEM)
in_smem = pl.BlockSpec(memory_space=pltpu.SMEM)


def norm_back(d_rows, unit, inverse, gain):
    scaled = d_rows * gain
    first = jnp.mean(scaled, axis=1, keepdims=True)
    second = jnp.mean(scaled * unit, axis=1, keepdims=True)
    return inverse * (scaled - first - unit * second)


def feed_kernel(
    core,
    inputs,
    targets,
    valid,
    vectors,
    out_own,
    out_other,
    up_own,
    up_other,
    down_own,
    down_other,
    *refs,
):
    group = inputs.shape[1] // HD
    mixed, refs = refs[:group], refs[group:]
    outputs, d_hidden, keep, send = refs[:4]
    pieces, refs = refs[4 : 4 + group], refs[4 + group :]
    attended, active, normed, normed_turned, d_out_low, small, d_attended, hidden, unit, slope, acc, up_sum = refs
    for index, piece in enumerate(mixed):
        attended[span((core[1] ^ index) * HD, HD), :] = piece[...]
    tokens, width = inputs.shape
    half = width // 2
    f_half = down_own.shape[0]
    step = 512
    wide = 1024
    rows = f_half // group
    up_rows = half // group
    place = core[0]
    halves = ((place, out_own, up_own, down_own), (1 - place, out_other, up_other, down_other))
    hidden[...] = inputs[...].astype(f32) + vectors[5:6, :]
    for where, w_out, _, _ in halves:
        hidden[...] += mxu(attended[span(where * half, half), :], w_out[...], TN)
    unit_here, inverse = normalize(hidden[...])
    unit[...] = unit_here
    normed_here = (unit_here * vectors[1:2, :] + vectors[6:7, :]).astype(bf16)
    normed[...] = normed_here
    normed_turned[...] = normed_here.T
    for row in range(4):
        up_sum[:, row * width : (row + 1) * width] = vectors[8 + row : 9 + row, :]
    acc[...] = hidden[...] + vectors[7:8, :]
    for where, _, _, w_down in halves:

        def lift(index, nothing):
            columns = span(where * f_half + index * wide, wide)
            u = up_sum[:, columns]
            for other, _, w_up, _ in halves:
                u = u + mxu(normed[:, span(other * half, half)], w_up[:, columns], NN)
            square = u * u
            tanh = jnp.tanh(gelu_scale * (u + gelu_cubic * (square * u)))
            side = 0.5 * (1.0 + tanh)
            act = (u * side).astype(bf16)
            active[:, columns] = act
            slope[:, columns] = side + (0.5 * gelu_scale) * u * (1.0 - tanh * tanh) * (
                1.0 + (3.0 * gelu_cubic) * square
            )
            acc[...] += mxu(act, w_down[span(index * wide, wide), :], NN)
            return nothing

        lax.fori_loop(0, f_half // wide, lift, 0)
    out_f32 = acc[...]
    outputs[...] = out_f32.astype(bf16)
    d_out = valid[...] * (out_f32 - targets[...].astype(f32))
    d_hidden[...] = d_out
    d_out_low[...] = d_out.astype(bf16)
    small[...] = jnp.zeros(small.shape, f32)
    small[3:4, :] = column_sum(d_out)
    acc[...] = jnp.zeros(acc.shape, f32)
    for target, (where, _, _, w_down) in zip((keep, send), halves):

        def lower(index, nothing):
            columns = span(where * f_half + index * step, step)
            d_active = mxu(d_out_low[...], w_down[span(index * step, step), :], NT)
            low = (d_active * slope[:, columns]).astype(bf16)
            up_sum[:, columns] = column_sum(low.astype(f32))
            for side, (other, _, w_up, _) in zip((keep, send), halves):
                acc[:, span(other * half, half)] += mxu(low, w_up[:, columns], NT)
                gradient = mxu(normed_turned[span(other * half, half), :], low, NN).astype(bf16)
                first = pl.multiple_of(rows + (where * (f_half // step) + index) * up_rows, up_rows)
                for member in range(group):
                    side[member, pl.ds(first, up_rows), :] = gradient[member * up_rows : (member + 1) * up_rows]
            gradient = mxu(active[:, columns], d_out_low[...], TN).astype(bf16)
            for part in range(step // rows):
                target[index * (step // rows) + part, :rows, :] = gradient[part * rows : (part + 1) * rows]
            return nothing

        lax.fori_loop(0, f_half // step, lower, 0)
    for row in range(4):
        small[4 + row : 5 + row, :] = up_sum[:, row * width : (row + 1) * width]
    d_normed = acc[...]
    unit_here = unit[...]
    small[0:1, :] = column_sum(d_normed * unit_here)
    small[2:3, :] = column_sum(d_normed)
    d_rows = d_hidden[...] + norm_back(d_normed, unit_here, inverse, vectors[1:2, :])
    d_hidden[...] = d_rows
    small[1:2, :] = column_sum(d_rows)
    low = d_rows.astype(bf16)
    for where, w_out, _, _ in halves:
        d_attended[span(where * half, half), :] = mxu(w_out[...], low, NT).astype(bf16)
    for index, piece in enumerate(pieces):
        piece[...] = d_attended[span((core[1] ^ index) * HD, HD), :]
    lanes = lax.broadcasted_iota(jnp.int32, (tokens, 128), 1)
    token = lax.broadcasted_iota(jnp.int32, (tokens, 128), 0)
    counts = column_sum(jnp.where(token % 128 == lanes, valid[...], 0.0))
    small[8:9, :128] = counts
    small[8:9, half : half + 128] = counts
    first = rows + up_rows * (2 * f_half // width)
    for target, (where, _, _, _) in zip((keep, send), halves):
        here = span(where * half, half)
        spread_rows(target, mxu(attended[here, :], low, NN), first, up_rows, 0)
        sums = jnp.concatenate([small[:, here], jnp.zeros(small[:, here].shape, f32)], 1).astype(bf16)
        for member in range(group):
            target[member, first + up_rows :, :] = sums


def spread_rows(target, gradient, first, rows, me):
    low = gradient.astype(bf16)
    for member in range(target.shape[0]):
        target[member ^ me, first : first + rows, :] = low[member * rows : (member + 1) * rows]


def first_back_kernel(core, d_heads, inputs, vectors, d_hidden, own, other, d_inputs, keep, send, d_proj, d_normed):
    width = inputs.shape[1]
    half = width // 2
    members = keep.shape[0]
    place = core[0]
    for head in range(width // HD):
        for part in range(3):
            d_proj[part * width + head * HD : part * width + (head + 1) * HD, :] = d_heads[
                head, part * HD : (part + 1) * HD, :
            ]
    unit, inverse = normalize(inputs[...].astype(f32))
    normed = (unit * vectors[0:1, :] + vectors[2:3, :]).astype(bf16).T
    for where, weight in ((place, own), (1 - place, other)):
        d_normed[span(where * half, half), :] = mxu(weight[...], d_proj[...], NN)
    d_rows = d_normed[:width, :].T
    d_inputs[...] = d_hidden[...] + norm_back(d_rows, unit, inverse, vectors[0:1, :])
    gain_sum = column_sum(d_rows * unit)
    offset_sum = column_sum(d_rows)
    ones = jnp.ones((ONES, inputs.shape[0]), bf16)
    query_sum = mxu(ones, d_proj[:width], NT)[:1]
    value_sum = mxu(ones, d_proj[2 * width :], NT)[:1]
    sums = jnp.concatenate([gain_sum, offset_sum, query_sum, value_sum, jnp.zeros((ONES - 4, width), f32)], 0)
    rows = half // members
    d_normed[:ONES, :] = sums
    for part in range(3):
        gradient = mxu(normed, d_proj[part * width : (part + 1) * width], NT)
        d_normed[ONES : ONES + width, :] = gradient
        for target, where in ((keep, place), (send, 1 - place)):
            low = d_normed[pl.ds(pl.multiple_of(ONES + where * half, ONES), half), :]
            spread_rows(target, low, part * rows, rows, core[1])
    for target, where in ((keep, place), (send, 1 - place)):
        low = d_normed[:ONES, span(where * half, half)]
        low = jnp.concatenate([low, jnp.zeros(low.shape, f32)], 1).astype(bf16)
        for member in range(members):
            target[member, 3 * rows :, :] = low


def squares_kernel(sums_early, sums_late, *refs):
    pieces, squares = refs[:-1], refs[-1]
    group = len(pieces) // 2
    half = sums_early.shape[1] // 2

    def square_sum(values):
        values = values.astype(f32)
        return jnp.sum(column_sum(values * values), axis=1, keepdims=True)

    parts = [square_sum(early[...]) + square_sum(late[...]) for early, late in zip(pieces[:group], pieces[group:])]
    total = paired_sum(parts) + (square_sum(sums_early[:8, :half]) + square_sum(sums_late[:4, :half]))
    squares[...] = jnp.broadcast_to(total, squares.shape)


def paired_sum(parts):
    while len(parts) > 1:
        parts = [parts[i] + parts[i + 1] for i in range(0, len(parts), 2)]
    return parts[0]


def update_kernel(me, squares, other_squares, sums_early, sums_late, d_raw, *refs, group, total_rows):
    early_pieces, late_pieces, refs = refs[:group], refs[group : 2 * group], refs[2 * group :]
    weights, firsts, seconds, refs = refs[0:6], refs[6:12], refs[12:18], refs[18:]
    grad_inputs, norm = refs[:2]
    grads, new_firsts, new_seconds, steps = refs[2:8], refs[8:14], refs[14:20], refs[20:26]
    early, late, raw_out = refs[26:29]
    buffers, sems = refs[29:33], refs[33]
    for index in range(group):
        early[index] = early_pieces[index][...]
        late[index] = late_pieces[index][...]

    count_scale = total_rows / jnp.sum(sums_early[8:9, :128], axis=1, keepdims=True)
    total = squares[:1, :1] + other_squares[:1, :1]
    grad_norm = jnp.sqrt(total) * count_scale / total_rows
    scale_back = jnp.minimum(1.0, clip_limit / grad_norm) / total_rows
    width = d_raw.shape[1]
    raw_rows = d_raw.shape[0] // group
    down_rows = weights[3].shape[0] // group
    after_up = down_rows + weights[2].shape[0] // group * (weights[2].shape[1] // width)

    def copies(slot, member):
        moves = [pltpu.make_async_copy(raw_out.at[slot], grad_inputs.at[span(member * raw_rows, raw_rows)], sems.at[slot, 0])]
        for index in range(4):
            rows = weights[index].shape[0] // group
            for kind, target in enumerate((grads, new_firsts, new_seconds, steps)):
                moves.append(
                    pltpu.make_async_copy(
                        buffers[index].at[slot, kind],
                        target[index].at[span(member * rows, rows)],
                        sems.at[slot, 1 + 4 * index + kind],
                    )
                )
        return moves

    def step(number, nothing):
        slot = number & 1
        member = me[0] ^ number

        @pl.when(number >= 2)
        def _():
            for move in copies(slot, member):
                move.wait()

        raw_out[slot] = d_raw[span(member * raw_rows, raw_rows), :] * count_scale
        for index, (source, first) in enumerate(((late, 0), (early, after_up), (early, down_rows), (early, 0))):
            rows = weights[index].shape[0] // group
            here = span(member * rows, rows)
            for block in range(weights[index].shape[1] // width):
                columns = slice(block * width, (block + 1) * width)
                gradient = source[number, first + block * rows : first + (block + 1) * rows, :].astype(f32) * count_scale
                results = adam_step(
                    weights[index][here, columns],
                    gradient,
                    firsts[index][here, columns],
                    seconds[index][here, columns],
                    scale_back,
                    weight_decay,
                )
                for kind, result in enumerate((gradient,) + results):
                    buffers[index][slot, kind, :, columns] = result
        for move in copies(slot, member):
            move.start()
        return nothing

    lax.fori_loop(0, group, step, 0)
    half = width // 2
    norm[...] = jnp.broadcast_to(grad_norm, norm.shape)

    def change(index, row, raw):
        where = (slice(row, row + 1), slice(None))
        gradient = raw * count_scale
        grads[index][where] = gradient
        results = adam_step(
            weights[index][where], gradient, firsts[index][where], seconds[index][where], scale_back, 0.0
        )
        new_firsts[index][where], new_seconds[index][where], steps[index][where] = results

    change(4, 0, sums_late[0:1, :half])
    change(4, 1, sums_early[0:1, :half])
    for row in range(3):
        change(5, row, sums_late[1 + row : 2 + row, :half])
    for row in range(3, 10):
        change(5, row, sums_early[row - 2 : row - 1, :half])
    for slot in (0, 1):
        for move in copies(slot, me[0] ^ slot):
            move.wait()


def adam_step(weight, gradient, first_old, second_old, scale_back, decay_rate):
    clipped = gradient * scale_back
    new_first = first_decay * first_old + (1.0 - first_decay) * clipped
    new_second = second_decay * second_old + ((1.0 - second_decay) * clipped) * clipped
    second_hat = new_second * (1.0 / (1.0 - second_decay**STEP))
    below = second_hat * lax.rsqrt(second_hat) + adam_floor
    inverse = pl.reciprocal(below, approx=True)
    inverse = inverse * (2.0 - below * inverse)
    inverse = inverse * (2.0 - below * inverse)
    update = (new_first * (-learn_rate / (1.0 - first_decay**STEP))) * inverse
    if decay_rate:
        update = update - (learn_rate * decay_rate) * weight.astype(f32)
    return (new_first, new_second, update)


def shaped(shape, kind):
    return jax.ShapeDtypeStruct(shape, kind)


in_place = pl.BlockSpec(memory_space=pl.ANY)


def attend(starts, core, qkv, kv, other_kv, state=None, final=True, spare=()):
    group, _, tokens = qkv.shape
    count = kv.shape[0]
    row = shaped((group, 1, tokens), f32)
    if final:
        out_shape = (shaped((group, HD, tokens), f32), row) + (shaped((HD, tokens), bf16),) * group
    else:
        out_shape = (shaped((group, HD + ONES, tokens), f32), row)
    state = state or ()
    return pl.pallas_call(
        functools.partial(attend_kernel, group=group, own=not state, final=final, spare=len(spare)),
        out_shape=out_shape + tuple(shaped(shape, bf16) for shape in spare),
        in_specs=[in_smem, in_smem] + [in_vmem] * (3 + len(state)),
        out_specs=(in_vmem,) * len(out_shape) + (in_place,) * len(spare),
        scratch_shapes=([pltpu.VMEM((group, HD, tokens), bf16)] if final else [])
        + [
            pltpu.VMEM((2, count, tokens, 2 * HD), bf16),
            pltpu.VMEM((2, count, HD + ONES, tokens), bf16),
            pltpu.VMEM((2 * HD, tokens), bf16),
            pltpu.VMEM((HD + ONES, tokens), f32),
            pltpu.VMEM((1, tokens), f32),
        ],
        cost_estimate=pl.CostEstimate(flops=30 * 2**30, bytes_accessed=5 * 2**20, transcendentals=2**24),
        compiler_params=pltpu.CompilerParams(vmem_limit_bytes=24 * 2**20),
        name="attend",
    )(starts, core, qkv, kv, other_kv, *state)


def attend_back(starts, core, qkv, kv, other_kv, d_out, out, log_total, after, d_query=None, own=True, low=0, count=0, final=False):
    group, _, tokens = qkv.shape
    resumed = d_query is not None
    return pl.pallas_call(
        functools.partial(attend_back_kernel, group=group, own=own, low=low, final=final, resumed=resumed),
        out_shape=(
            shaped((group, HD, tokens), bf16 if final else f32),
            shaped((count, 2 * HD, tokens), bf16),
            shaped((count, 2 * HD, tokens), bf16),
        ),
        in_specs=[in_smem, in_smem] + [in_vmem] * (5 + group + resumed) + [in_place] * len(after),
        out_specs=(in_vmem,) * 3,
        scratch_shapes=[
            pltpu.VMEM((group, HD, tokens), bf16),
            pltpu.VMEM((2, count, tokens, 2 * HD), bf16),
            pltpu.VMEM((2 * HD, tokens), bf16),
            pltpu.VMEM((2 * HD, tokens), bf16),
            pltpu.VMEM((2, count, 2 * HD, tokens), f32),
            pltpu.VMEM((HD, tokens), f32),
        ],
        cost_estimate=pl.CostEstimate(flops=count * 8 * 2**30, bytes_accessed=8 * 2**20, transcendentals=2**24),
        compiler_params=pltpu.CompilerParams(vmem_limit_bytes=32 * 2**20),
        name="attend_back",
    )(starts, core, qkv, kv, other_kv, out, log_total, *d_out, *((d_query,) if resumed else ()), *after)


def project(core, inputs, vectors, own, other):
    tokens, width = inputs.shape
    return pl.pallas_call(
        first_kernel,
        out_shape=shaped((width // HD, 3 * HD, tokens), bf16),
        in_specs=[in_smem] + [in_vmem] * 4,
        out_specs=in_vmem,
        cost_estimate=pl.CostEstimate(flops=2**30, bytes_accessed=4 * 2**20, transcendentals=0),
        compiler_params=pltpu.CompilerParams(vmem_limit_bytes=16 * 2**20),
        name="project",
    )(core, inputs, vectors, own, other)


def feed(core, mixed, inputs, targets, valid, vectors, *weights):
    tokens, width = inputs.shape
    group = width // HD
    hidden_units = weights[2].shape[1]
    rows = (2 * hidden_units + width) // 2 // group + 16
    return pl.pallas_call(
        feed_kernel,
        out_shape=(shaped((tokens, width), bf16), shaped((tokens, width), f32))
        + (shaped((group, rows, width), bf16),) * 2
        + (shaped((HD, tokens), bf16),) * group,
        in_specs=[in_smem] + [in_vmem] * (10 + group),
        out_specs=(in_vmem,) * (4 + group),
        scratch_shapes=[
            pltpu.VMEM((width, tokens), bf16),
            pltpu.VMEM((tokens, hidden_units), bf16),
            pltpu.VMEM((tokens, width), bf16),
            pltpu.VMEM((width, tokens), bf16),
            pltpu.VMEM((tokens, width), bf16),
            pltpu.VMEM((16, width), f32),
            pltpu.VMEM((width, tokens), bf16),
            pltpu.VMEM((tokens, width), f32),
            pltpu.VMEM((tokens, width), f32),
            pltpu.VMEM((tokens, hidden_units), f32),
            pltpu.VMEM((tokens, width), f32),
            pltpu.VMEM((1, hidden_units), f32),
        ],
        cost_estimate=pl.CostEstimate(flops=10 * 2**30, bytes_accessed=14 * 2**20, transcendentals=2**20),
        compiler_params=pltpu.CompilerParams(vmem_limit_bytes=34 * 2**20),
        name="feed",
    )(core, inputs, targets, valid, vectors, *weights, *mixed)


def first_back(group, core, d_heads, inputs, vectors, d_hidden, own, other):
    tokens, width = inputs.shape
    rows = own.shape[0] // group * 3 + 16
    return pl.pallas_call(
        first_back_kernel,
        out_shape=(shaped((tokens, width), f32),) + (shaped((group, rows, width), bf16),) * 2,
        in_specs=[in_smem] + [in_vmem] * 6,
        out_specs=(in_vmem,) * 3,
        scratch_shapes=[pltpu.VMEM((3 * width, tokens), bf16), pltpu.VMEM((width + 16, tokens), f32)],
        cost_estimate=pl.CostEstimate(flops=4 * 2**30, bytes_accessed=8 * 2**20, transcendentals=0),
        compiler_params=pltpu.CompilerParams(vmem_limit_bytes=24 * 2**20),
        name="first_back",
    )(core, d_heads, inputs, vectors, d_hidden, own, other)


def sum_squares(sums_early, sums_late, early, late):
    return pl.pallas_call(
        squares_kernel,
        out_shape=shaped((8, 128), f32),
        in_specs=[in_vmem] * (2 + 2 * len(early)),
        out_specs=in_vmem,
        cost_estimate=pl.CostEstimate(flops=2**22, bytes_accessed=4 * 2**20, transcendentals=0),
        compiler_params=pltpu.CompilerParams(vmem_limit_bytes=16 * 2**20),
        name="sum_squares",
    )(sums_early, sums_late, *early, *late)


def update(group, me, total_rows, squares, other_squares, sums_early, sums_late, d_raw, early, late, *state):
    weights = state[0]
    like = [shaped(weight.shape, f32) for weight in weights]
    out_specs = [in_place] * 4 + [in_vmem] * 2
    return pl.pallas_call(
        functools.partial(update_kernel, group=group, total_rows=total_rows),
        out_shape=[shaped(d_raw.shape, f32), shaped((8, 128), f32)] + like * 4,
        in_specs=[in_smem] + [in_vmem] * (5 + 2 * group + 18),
        out_specs=[in_place, in_vmem] + out_specs * 4,
        scratch_shapes=[
            pltpu.VMEM((group,) + early[0].shape, bf16),
            pltpu.VMEM((group,) + late[0].shape, bf16),
            pltpu.VMEM((2, d_raw.shape[0] // group, d_raw.shape[1]), f32),
        ]
        + [pltpu.VMEM((2, 4, weight.shape[0] // group, weight.shape[1]), f32) for weight in weights[:4]]
        + [pltpu.SemaphoreType.DMA((2, 17))],
        cost_estimate=pl.CostEstimate(flops=2**26, bytes_accessed=44 * 2**20, transcendentals=2**22),
        compiler_params=pltpu.CompilerParams(vmem_limit_bytes=31 * 2**20),
        name="update",
    )(me, squares, other_squares, sums_early, sums_late, d_raw, *early, *late, *state[0], *state[1], *state[2])


def from_other_core(value):
    return lax.ppermute(value, "fsdp", [(0, 1), (1, 0)])


def whole_of(value, axis):
    other = from_other_core(value)
    first = lax.axis_index("fsdp") == 0
    return jnp.concatenate([jnp.where(first, value, other), jnp.where(first, other, value)], axis)


def swap_ctx(value, bit):
    size = lax.axis_size("ctx")
    return lax.ppermute(value, "ctx", [(i, i ^ bit) for i in range(size)])


def across_groups(value, group):
    low, sums = value[:-16].astype(bf16), value[-16:]
    bit = group
    while bit < lax.axis_size("ctx"):
        sent = value.astype(bf16)
        received = swap_ctx(sent, bit)
        low = (sent[:-16].astype(f32) + received[:-16].astype(f32)).astype(bf16)
        sums = sent[-16:].astype(f32) + received[-16:].astype(f32)
        value = jnp.concatenate([low.astype(f32), sums], 0) if 2 * bit < lax.axis_size("ctx") else None
        bit *= 2
    return low, sums


def per_device(
    inputs,
    targets,
    valid_mask,
    block_seq,
    w_qkv,
    w_out,
    w_up,
    w_down,
    norm_gains,
    biases,
    first_qkv,
    first_out,
    first_up,
    first_down,
    first_gains,
    first_biases,
    second_qkv,
    second_out,
    second_up,
    second_down,
    second_gains,
    second_biases,
):
    rows_here, width = inputs.shape
    group = width // HD
    ctx_size = lax.axis_size("ctx")
    block_rows = rows_here * 2
    total_rows = float(block_rows * ctx_size)
    ctx_place = lax.axis_index("ctx")
    core_place = lax.axis_index("fsdp")
    members = [[first + i for i in range(group)] for first in range(0, ctx_size, group)]

    def exchange(value):
        return lax.all_to_all(value, "ctx", 0, 0, axis_index_groups=members, tiled=True)

    core = jnp.stack([core_place, ctx_place % group]).astype(jnp.int32)
    vectors = whole_of(jnp.concatenate([norm_gains, biases], 0), 1).astype(f32)
    other_qkv = from_other_core(w_qkv)
    other_out, other_up, other_down = (from_other_core(w_out), from_other_core(w_up), from_other_core(w_down))
    valid_rows = valid_mask.astype(f32)
    qkv = exchange(project(core, inputs, vectors, w_qkv, other_qkv))
    own_kv = qkv[:, HD:]
    other_kv = from_other_core(own_kv)

    first_block = (ctx_place // group) * group
    own_seq = lax.dynamic_slice_in_dim(block_seq, first_block, group, 0)
    starts = jnp.sum((block_seq[None, :] < own_seq[:, None]).astype(jnp.int32), axis=1)
    starts = jnp.maximum(starts - first_block + group, 0)
    behind = jnp.zeros((), jnp.int32)
    for edge in range(group, ctx_size, group):
        same = (block_seq[edge - group : edge] == block_seq[edge]).astype(jnp.int32)
        behind = jnp.maximum(behind, jnp.sum(same))
    most_behind = group - 1
    few_behind = group // 2
    branch = (behind > 0).astype(jnp.int32) + (behind > few_behind).astype(jnp.int32)
    counts = (0, few_behind, most_behind)

    def forward(count, own, other):
        if count == 0:
            return tuple(attend(starts, core, qkv, qkv, other, spare=[(most_behind, 2 * HD, rows_here)] * 2))
        prev_own = lax.ppermute(own[group - count :], "ctx", [(i, i + group) for i in range(ctx_size - group)])
        state = attend(starts, core, qkv, qkv, other, final=False)
        prev_own, state = lax.optimization_barrier((prev_own, state))
        prev_other = from_other_core(prev_own)
        mixed = attend(starts, core, qkv, prev_own, prev_other, state=state)
        short = ((most_behind - count, 0), (0, 0), (0, 0))
        return tuple(mixed) + (jnp.pad(prev_own, short), jnp.pad(prev_other, short))

    results = lax.switch(branch, [functools.partial(forward, count) for count in counts], own_kv, other_kv)
    mixed, log_total = results[:2]
    prev = results[2 + group :]

    def deal(pieces):
        moved = []
        for step in range(1, group):
            moved.append(lax.ppermute(pieces[step], "ctx", [(i, i ^ step) for i in range(ctx_size)]))
        return [pieces[0]] + moved

    results = feed(
        core,
        deal(results[2 : 2 + group]),
        inputs,
        targets,
        valid_rows[:, None],
        vectors,
        w_out,
        other_out,
        w_up,
        other_up,
        w_down,
        other_down,
    )
    outputs, d_hidden, keep, send = results[:4]
    d_mixed = deal(results[4:])

    def paired(keep, received):
        return [(keep[i].astype(f32) + received[i].astype(f32)).astype(bf16) for i in range(group)]

    def gathered(pairs):
        return paired_sum([piece.astype(f32) for piece in deal(pairs)])

    def finished(mine):
        return across_groups(mine, group)

    received, d_mixed = lax.optimization_barrier((from_other_core(send), d_mixed))
    pair = (keep.astype(f32) + received.astype(f32)).astype(bf16)
    early_mine = jnp.sum(exchange(pair).astype(f32), axis=0)
    cuts = (0, 3, 5, group)

    def back(part, after, d_query, d_mixed):
        low, high = cuts[part], cuts[part + 1]
        return attend_back(
            starts,
            core,
            qkv,
            qkv,
            other_kv,
            d_mixed,
            mixed,
            log_total,
            after,
            d_query=d_query,
            low=low,
            count=high - low,
            final=high == group,
        )

    def backward(count, d_mixed, pair, prev):
        if count == 0:
            return tuple(back(0, (pair,), None, d_mixed)) + tuple(
                jnp.zeros((high - low, 2 * HD, rows_here), bf16) for low, high in zip(cuts[1:-1], cuts[2:])
            )
        prev_own, prev_other = prev
        d_query, d_behind, d_behind_other = attend_back(
            starts,
            core,
            qkv,
            prev_own,
            prev_other,
            d_mixed,
            mixed,
            log_total,
            (pair,),
            own=False,
            low=most_behind - count,
            count=count,
        )
        d_prev = (d_behind.astype(f32) + from_other_core(d_behind_other).astype(f32)).astype(bf16)
        d_prev = lax.ppermute(d_prev, "ctx", [(i + group, i) for i in range(ctx_size - group)])
        results = tuple(back(0, (pair,), d_query, d_mixed))
        (d_query, d_own, d_other), d_prev = lax.optimization_barrier((results, d_prev))
        d_prev = jnp.pad(d_prev, ((group - count, 0), (0, 0), (0, 0)))
        d_own = (d_own.astype(f32) + d_prev[: cuts[1]].astype(f32)).astype(bf16)
        return (d_query, d_own, d_other) + tuple(d_prev[low:high] for low, high in zip(cuts[1:-1], cuts[2:]))

    def summed(d_own, d_other, *more):
        return sum((one.astype(f32) for one in more), d_own.astype(f32) + from_other_core(d_other).astype(f32)).astype(bf16)

    d_query, d_own, d_other, *d_prev = lax.switch(
        branch, [functools.partial(backward, count) for count in counts], d_mixed, pair, prev
    )
    first_sum = (d_own, d_other)
    d_query, d_own, d_other = back(1, (early_mine,), d_query, d_mixed)
    d_kv = [summed(*first_sum)]
    second_sum = (d_own, d_other)
    early_low, early_sums = finished(early_mine)
    d_query, d_own, d_other = back(2, (early_low, d_kv[0]), d_query, d_mixed)

    def forward_piece(piece, step):
        return lax.ppermute(piece, "ctx", [(i, i ^ step) for i in range(ctx_size)])

    early = [early_low] + [forward_piece(early_low, step) if step in (1, 2, 4) else None for step in range(1, group)]
    (early[1], early[2], early[4]), d_own, d_other = lax.optimization_barrier(
        ((early[1], early[2], early[4]), d_own, d_other)
    )
    d_kv += [summed(*second_sum, d_prev[0]), summed(d_own, d_other, d_prev[1])]
    d_heads = exchange(jnp.concatenate([d_query, jnp.concatenate(d_kv, 0)], 1))
    d_heads, (early[1], early[2], early[4]) = lax.optimization_barrier((d_heads, (early[1], early[2], early[4])))
    early[3] = forward_piece(early[2], 1)
    early[5] = forward_piece(early[1], 4)
    early[6] = forward_piece(early[4], 2)
    early[7] = forward_piece(early[6], 1)
    d_raw, keep, send = first_back(group, core, d_heads, inputs, vectors, d_hidden, w_qkv, other_qkv)
    (early[3], early[5], early[6]), keep, send = lax.optimization_barrier(((early[3], early[5], early[6]), keep, send))
    late_low, late_sums = finished(gathered(paired(keep, from_other_core(send))))
    late = deal([late_low] * group)
    squares = sum_squares(early_sums, late_sums, early, late)
    results = update(
        group,
        core[1:],
        total_rows,
        squares,
        from_other_core(squares),
        early_sums,
        late_sums,
        d_raw,
        early,
        late,
        [w_qkv, w_out, w_up, w_down, norm_gains, biases],
        [first_qkv, first_out, first_up, first_down, first_gains, first_biases],
        [second_qkv, second_out, second_up, second_down, second_gains, second_biases],
    )
    grad_inputs, norm = results[:2]
    return (outputs, grad_inputs) + tuple(results[2:8]) + (norm[0, 0],) + tuple(results[8:])


def solution(mesh):
    tokens = P(("ctx", "fsdp"), None)
    weight = P("fsdp", None)
    vector = P(None, "fsdp")
    params = (weight, weight, weight, weight, vector, vector)
    in_specs = (tokens, tokens, P(("ctx", "fsdp")), P()) + params * 3
    out_specs = (tokens, tokens) + params + (P(),) + params * 3
    return jax.shard_map(per_device, mesh=mesh, in_specs=in_specs, out_specs=out_specs, check_vma=False)
```

```python
import functools
import math

import jax
import jax.numpy as jnp
from jax import lax
from jax.experimental import pallas as pl
from jax.experimental.pallas import tpu as pltpu
from jax.sharding import PartitionSpec as P

HD = 64
STEP = 10

very_low = -1e30
norm_floor = 1e-05
first_decay = 0.9
second_decay = 0.95
adam_floor = 1e-08
learn_rate = 0.02
weight_decay = 0.1
clip_limit = 0.01
gelu_scale = (2.0 / math.pi) ** 0.5
gelu_cubic = 0.044715

BASE_LIMIT = 1e20
ONES = 16

bf16 = jnp.bfloat16
f32 = jnp.float32
NN = (((1,), (0,)), ((), ()))
NT = (((1,), (1,)), ((), ()))
TN = (((0,), (0,)), ((), ()))


def mxu(left, right, dims):
    return lax.dot_general(left, right, dims, preferred_element_type=f32)


def below_diagonal(scores):
    key_pos = lax.broadcasted_iota(jnp.int32, scores.shape, 0)
    query_pos = lax.broadcasted_iota(jnp.int32, scores.shape, 1)
    return jnp.where(key_pos <= query_pos, scores, very_low)


def column_sum(values):
    return jnp.sum(values, axis=0, keepdims=True)


def column_max(values):
    return jnp.max(values, axis=0, keepdims=True)


def normalize(rows):
    center = rows - jnp.mean(rows, axis=1, keepdims=True)
    inverse = lax.rsqrt(jnp.mean(center * center, axis=1, keepdims=True) + norm_floor)
    return center * inverse, inverse


def span(start, size):
    return pl.ds(pl.multiple_of(start, size), size)


def attend_kernel(starts, place_of, qkv, kv, other_kv, *refs, group, own, final, spare):
    if own:
        acc_in = base_in = None
    else:
        acc_in, base_in = refs[:2]
        refs = refs[2:]
    if final:
        out, log_total = refs[:2]
        pieces = refs[2 : 2 + group]
        low, kv_rows, v_ones, q_pad, acc, high = refs[2 + group + spare :]
    else:
        acc_out, base_out, kv_rows, v_ones, q_pad, acc, high = refs
    tokens = q_pad.shape[1]
    count = kv.shape[0]
    ones = jnp.ones((ONES, tokens), bf16)
    for place in range(count):
        for kind, source in ((0, kv), (1, other_kv)):
            here = source[place, source.shape[1] - 2 * HD :, :]
            kv_rows[kind, place] = here.T
            v_ones[kind, place, :HD, :] = here[HD:]
            v_ones[kind, place, HD:, :] = ones
    q_pad[HD:, :] = jnp.zeros((HD, tokens), bf16)

    def score(kind, place):
        return mxu(kv_rows[kind, place], q_pad[...], NN)

    def weigh(kind, place, scores, base):
        return mxu(v_ones[kind, place], jnp.exp(scores - base).astype(bf16), NN)

    def finish(place):
        if final:
            total = acc[HD : HD + 1, :]
            mixed = acc[:HD, :] * (1.0 / total)
            out[place] = mixed
            low[place] = mixed.astype(bf16)
            log_total[place] = high[...] + jnp.log(total)
        else:
            acc_out[place] = acc[...]
            base_out[place] = high[...]

    def begin(place):
        q_pad[:HD, :] = qkv[place, :HD, :] * bf16(HD**-0.5)
        if not own:
            high[...] = base_in[place]
            acc[...] = acc_in[place]
        return jnp.maximum(starts[place] - (group if own else group - count), 0)

    def quick(place, largest):
        first = begin(place)
        if own:
            scores = below_diagonal(score(0, place))
            base = column_max(scores)
            high[...] = base
            acc[...] = weigh(0, place, scores, base)

        def loop(kinds, first, last):
            def body(key_place, nothing):
                base = high[...]
                acc[...] += sum(weigh(kind, key_place, score(kind, key_place), base) for kind in kinds)
                return nothing

            lax.fori_loop(first, last, body, 0)

        if own:
            loop((1,), place, place + place_of[0])
        loop((0, 1), first, place if own else count)
        finish(place)
        return jnp.maximum(largest, acc[HD : HD + 1, :])

    largest = lax.fori_loop(0, group, quick, jnp.zeros((1, tokens), f32))

    @pl.when(jnp.logical_not(jnp.max(largest) < BASE_LIMIT))
    def _():
        rows = 128

        def careful(place, nothing):
            first = begin(place)
            if own:
                high[...] = jnp.full(high.shape, very_low, f32)
                acc[...] = jnp.zeros(acc.shape, f32)

            def by_kind(kind, nothing):
                def by_place(key_place, nothing):
                    def by_rows(index, nothing):
                        here = span(index * rows, rows)
                        scores = mxu(kv_rows[kind, key_place, here, :], q_pad[...], NN)
                        if own:
                            key_pos = index * rows + lax.broadcasted_iota(jnp.int32, scores.shape, 0)
                            query_pos = lax.broadcasted_iota(jnp.int32, scores.shape, 1)
                            query_pos = query_pos + jnp.where((kind == 0) & (key_place == place), 0, tokens)
                            scores = jnp.where(key_pos <= query_pos, scores, very_low)
                        old = high[...]
                        new = jnp.maximum(old, column_max(scores))
                        probs = jnp.exp(scores - new).astype(bf16)
                        acc[...] = acc[...] * jnp.exp(old - new) + mxu(v_ones[kind, key_place, :, here], probs, NN)
                        high[...] = new
                        return nothing

                    return lax.fori_loop(0, tokens // rows, by_rows, nothing)

                last = place + jnp.where(kind == 0, 1, place_of[0]) if own else count
                return lax.fori_loop(first, last, by_place, nothing)

            lax.fori_loop(0, 2, by_kind, 0)
            finish(place)
            return nothing

        lax.fori_loop(0, group, careful, 0)

    if final:
        for step, piece in enumerate(pieces):
            piece[...] = low[place_of[1] ^ step]


def attend_back_kernel(starts, place_of, qkv, kv, other_kv, out, log_total, *refs, group, own, low, final, resumed):
    pieces = refs[:group]
    d_query_in = refs[group] if resumed else None
    d_query, d_kv, d_other_kv, d_out, kv_rows, q_pad, d_pad, d_kv_sum, d_query_sum = refs[-9:]
    for step, piece in enumerate(pieces):
        d_out[place_of[1] ^ step] = piece[...]
    tokens = q_pad.shape[1]
    count = d_kv.shape[0]
    sources = (kv, other_kv)
    for place in range(count):
        for kind in (0, 1):
            source = sources[kind]
            kv_rows[kind, place] = source[low + place, source.shape[1] - 2 * HD :, :].T
    q_pad[HD:, :] = jnp.zeros((HD, tokens), bf16)
    d_pad[:HD, :] = jnp.zeros((HD, tokens), bf16)
    d_kv_sum[...] = jnp.zeros(d_kv_sum.shape, f32)

    def tile(kind, place, masked, delta, log_row):
        source = sources[kind]
        rows = kv_rows[kind, place]
        scores = mxu(rows, q_pad[...], NN)
        if masked:
            scores = below_diagonal(scores)
        probs = jnp.exp(scores - log_row)
        d_probs = mxu(rows, d_pad[...], NN)
        d_scores = (probs * (d_probs - delta)).astype(bf16)
        d_kv_sum[kind, place] += mxu(q_pad[...], d_scores, NT) + mxu(d_pad[...], probs.astype(bf16), NT)
        first = source.shape[1] - 2 * HD
        return mxu(source[low + place, first : first + HD, :], d_scores, NN)

    def chunk(place, nothing):
        q_pad[:HD, :] = qkv[place, :HD, :] * bf16(HD**-0.5)
        d_here = d_out[place]
        d_pad[HD:, :] = d_here
        delta = column_sum(d_here.astype(f32) * out[place])
        log_row = log_total[place]
        d_query_sum[...] = d_query_in[place] if resumed else jnp.zeros(d_query_sum.shape, f32)

        def loop(kinds, first, last):
            def body(key_place, nothing):
                d_query_sum[...] += sum(tile(kind, key_place, False, delta, log_row) for kind in kinds)
                return nothing

            lax.fori_loop(first, last, body, 0)

        if own:
            here = place - low

            @pl.when(jnp.logical_and(here >= 0, here < count))
            def _():
                d_query_sum[...] += tile(0, here, True, delta, log_row)
                loop((1,), here, here + place_of[0])

            loop((0, 1), jnp.maximum(starts[place] - group - low, 0), jnp.minimum(here, count))
        else:
            loop((0, 1), jnp.maximum(starts[place] - (group - count), 0), count)
        if final:
            d_query[place] = (d_query_sum[...] * HD**-0.5).astype(bf16)
        else:
            d_query[place] = d_query_sum[...]
        return nothing

    lax.fori_loop(0, group, chunk, 0)
    d_kv[...] = d_kv_sum[0].astype(bf16)
    d_other_kv[...] = d_kv_sum[1].astype(bf16)


def first_kernel(core, inputs, vectors, own, other, by_head):
    width = inputs.shape[1]
    half = width // 2
    unit, _ = normalize(inputs[...].astype(f32))
    normed = (unit * vectors[0:1, :] + vectors[2:3, :]).astype(bf16)
    swap = core[0] == 1
    low, high = normed[:, :half], normed[:, half:]
    mine, rest = jnp.where(swap, high, low), jnp.where(swap, low, high)
    for part in range(3):
        columns = slice(part * width, (part + 1) * width)
        rows = mxu(mine, own[:, columns], NN) + mxu(rest, other[:, columns], NN)
        if part != 1:
            row = 3 + part // 2
            rows = rows + vectors[row : row + 1, :]
        turned = rows.astype(bf16).T
        for head in range(width // HD):
            by_head[head, part * HD : (part + 1) * HD, :] = turned[head * HD : (head + 1) * HD]


in_vmem = pl.BlockSpec(memory_space=pltpu.VMEM)
in_smem = pl.BlockSpec(memory_space=pltpu.SMEM)


def norm_back(d_rows, unit, inverse, gain):
    scaled = d_rows * gain
    first = jnp.mean(scaled, axis=1, keepdims=True)
    second = jnp.mean(scaled * unit, axis=1, keepdims=True)
    return inverse * (scaled - first - unit * second)


def feed_kernel(
    core,
    inputs,
    targets,
    valid,
    vectors,
    out_own,
    out_other,
    up_own,
    up_other,
    down_own,
    down_other,
    *refs,
):
    group = inputs.shape[1] // HD
    mixed, refs = refs[:group], refs[group:]
    outputs, d_hidden, keep, send = refs[:4]
    pieces, refs = refs[4 : 4 + group], refs[4 + group :]
    attended, active, normed, normed_turned, d_out_low, small, d_attended, hidden, unit, slope, acc, up_sum = refs
    for index, piece in enumerate(mixed):
        attended[span((core[1] ^ index) * HD, HD), :] = piece[...]
    tokens, width = inputs.shape
    half = width // 2
    f_half = down_own.shape[0]
    step = 512
    wide = 1024
    rows = f_half // group
    up_rows = half // group
    place = core[0]
    halves = ((place, out_own, up_own, down_own), (1 - place, out_other, up_other, down_other))
    hidden[...] = inputs[...].astype(f32) + vectors[5:6, :]
    for where, w_out, _, _ in halves:
        hidden[...] += mxu(attended[span(where * half, half), :], w_out[...], TN)
    unit_here, inverse = normalize(hidden[...])
    unit[...] = unit_here
    normed_here = (unit_here * vectors[1:2, :] + vectors[6:7, :]).astype(bf16)
    normed[...] = normed_here
    normed_turned[...] = normed_here.T
    for row in range(4):
        up_sum[:, row * width : (row + 1) * width] = vectors[8 + row : 9 + row, :]
    acc[...] = hidden[...] + vectors[7:8, :]
    for where, _, _, w_down in halves:

        def lift(index, nothing):
            columns = span(where * f_half + index * wide, wide)
            u = up_sum[:, columns]
            for other, _, w_up, _ in halves:
                u = u + mxu(normed[:, span(other * half, half)], w_up[:, columns], NN)
            square = u * u
            tanh = jnp.tanh(gelu_scale * (u + gelu_cubic * (square * u)))
            side = 0.5 * (1.0 + tanh)
            act = (u * side).astype(bf16)
            active[:, columns] = act
            slope[:, columns] = side + (0.5 * gelu_scale) * u * (1.0 - tanh * tanh) * (
                1.0 + (3.0 * gelu_cubic) * square
            )
            acc[...] += mxu(act, w_down[span(index * wide, wide), :], NN)
            return nothing

        lax.fori_loop(0, f_half // wide, lift, 0)
    out_f32 = acc[...]
    outputs[...] = out_f32.astype(bf16)
    d_out = valid[...] * (out_f32 - targets[...].astype(f32))
    d_hidden[...] = d_out
    d_out_low[...] = d_out.astype(bf16)
    small[...] = jnp.zeros(small.shape, f32)
    small[3:4, :] = column_sum(d_out)
    acc[...] = jnp.zeros(acc.shape, f32)
    for target, (where, _, _, w_down) in zip((keep, send), halves):

        def lower(index, nothing):
            columns = span(where * f_half + index * step, step)
            d_active = mxu(d_out_low[...], w_down[span(index * step, step), :], NT)
            low = (d_active * slope[:, columns]).astype(bf16)
            up_sum[:, columns] = column_sum(low.astype(f32))
            for side, (other, _, w_up, _) in zip((keep, send), halves):
                acc[:, span(other * half, half)] += mxu(low, w_up[:, columns], NT)
                gradient = mxu(normed_turned[span(other * half, half), :], low, NN).astype(bf16)
                first = pl.multiple_of(rows + (where * (f_half // step) + index) * up_rows, up_rows)
                for member in range(group):
                    side[member, pl.ds(first, up_rows), :] = gradient[member * up_rows : (member + 1) * up_rows]
            gradient = mxu(active[:, columns], d_out_low[...], TN).astype(bf16)
            for part in range(step // rows):
                target[index * (step // rows) + part, :rows, :] = gradient[part * rows : (part + 1) * rows]
            return nothing

        lax.fori_loop(0, f_half // step, lower, 0)
    for row in range(4):
        small[4 + row : 5 + row, :] = up_sum[:, row * width : (row + 1) * width]
    d_normed = acc[...]
    unit_here = unit[...]
    small[0:1, :] = column_sum(d_normed * unit_here)
    small[2:3, :] = column_sum(d_normed)
    d_rows = d_hidden[...] + norm_back(d_normed, unit_here, inverse, vectors[1:2, :])
    d_hidden[...] = d_rows
    small[1:2, :] = column_sum(d_rows)
    low = d_rows.astype(bf16)
    for where, w_out, _, _ in halves:
        d_attended[span(where * half, half), :] = mxu(w_out[...], low, NT).astype(bf16)
    for index, piece in enumerate(pieces):
        piece[...] = d_attended[span((core[1] ^ index) * HD, HD), :]
    lanes = lax.broadcasted_iota(jnp.int32, (tokens, 128), 1)
    token = lax.broadcasted_iota(jnp.int32, (tokens, 128), 0)
    counts = column_sum(jnp.where(token % 128 == lanes, valid[...], 0.0))
    small[8:9, :128] = counts
    small[8:9, half : half + 128] = counts
    first = rows + up_rows * (2 * f_half // width)
    for target, (where, _, _, _) in zip((keep, send), halves):
        here = span(where * half, half)
        spread_rows(target, mxu(attended[here, :], low, NN), first, up_rows, 0)
        sums = jnp.concatenate([small[:, here], jnp.zeros(small[:, here].shape, f32)], 1).astype(bf16)
        for member in range(group):
            target[member, first + up_rows :, :] = sums


def spread_rows(target, gradient, first, rows, me):
    low = gradient.astype(bf16)
    for member in range(target.shape[0]):
        target[member ^ me, first : first + rows, :] = low[member * rows : (member + 1) * rows]


def first_back_kernel(core, d_heads, inputs, vectors, d_hidden, own, other, d_inputs, keep, send, d_proj, d_normed):
    width = inputs.shape[1]
    half = width // 2
    members = keep.shape[0]
    place = core[0]
    for head in range(width // HD):
        for part in range(3):
            d_proj[part * width + head * HD : part * width + (head + 1) * HD, :] = d_heads[
                head, part * HD : (part + 1) * HD, :
            ]
    unit, inverse = normalize(inputs[...].astype(f32))
    normed = (unit * vectors[0:1, :] + vectors[2:3, :]).astype(bf16).T
    for where, weight in ((place, own), (1 - place, other)):
        d_normed[span(where * half, half), :] = mxu(weight[...], d_proj[...], NN)
    d_rows = d_normed[:width, :].T
    d_inputs[...] = d_hidden[...] + norm_back(d_rows, unit, inverse, vectors[0:1, :])
    gain_sum = column_sum(d_rows * unit)
    offset_sum = column_sum(d_rows)
    ones = jnp.ones((ONES, inputs.shape[0]), bf16)
    query_sum = mxu(ones, d_proj[:width], NT)[:1]
    value_sum = mxu(ones, d_proj[2 * width :], NT)[:1]
    sums = jnp.concatenate([gain_sum, offset_sum, query_sum, value_sum, jnp.zeros((ONES - 4, width), f32)], 0)
    rows = half // members
    d_normed[:ONES, :] = sums
    for part in range(3):
        gradient = mxu(normed, d_proj[part * width : (part + 1) * width], NT)
        d_normed[ONES : ONES + width, :] = gradient
        for target, where in ((keep, place), (send, 1 - place)):
            low = d_normed[pl.ds(pl.multiple_of(ONES + where * half, ONES), half), :]
            spread_rows(target, low, part * rows, rows, core[1])
    for target, where in ((keep, place), (send, 1 - place)):
        low = d_normed[:ONES, span(where * half, half)]
        low = jnp.concatenate([low, jnp.zeros(low.shape, f32)], 1).astype(bf16)
        for member in range(members):
            target[member, 3 * rows :, :] = low


def squares_kernel(sums_early, sums_late, *refs):
    pieces, squares = refs[:-1], refs[-1]
    group = len(pieces) // 2
    half = sums_early.shape[1] // 2

    def square_sum(values):
        values = values.astype(f32)
        return jnp.sum(column_sum(values * values), axis=1, keepdims=True)

    parts = [square_sum(early[...]) + square_sum(late[...]) for early, late in zip(pieces[:group], pieces[group:])]
    total = paired_sum(parts) + (square_sum(sums_early[:8, :half]) + square_sum(sums_late[:4, :half]))
    squares[...] = jnp.broadcast_to(total, squares.shape)


def paired_sum(parts):
    while len(parts) > 1:
        parts = [parts[i] + parts[i + 1] for i in range(0, len(parts), 2)]
    return parts[0]


def update_kernel(me, squares, other_squares, sums_early, sums_late, d_raw, *refs, group, total_rows):
    early_pieces, late_pieces, refs = refs[:group], refs[group : 2 * group], refs[2 * group :]
    weights, firsts, seconds, refs = refs[0:6], refs[6:12], refs[12:18], refs[18:]
    grad_inputs, norm = refs[:2]
    grads, new_firsts, new_seconds, steps = refs[2:8], refs[8:14], refs[14:20], refs[20:26]
    early, late, raw_out = refs[26:29]
    buffers, sems = refs[29:33], refs[33]
    for index in range(group):
        early[index] = early_pieces[index][...]
        late[index] = late_pieces[index][...]

    count_scale = total_rows / jnp.sum(sums_early[8:9, :128], axis=1, keepdims=True)
    total = squares[:1, :1] + other_squares[:1, :1]
    grad_norm = jnp.sqrt(total) * count_scale / total_rows
    scale_back = jnp.minimum(1.0, clip_limit / grad_norm) / total_rows
    width = d_raw.shape[1]
    raw_rows = d_raw.shape[0] // group
    down_rows = weights[3].shape[0] // group
    after_up = down_rows + weights[2].shape[0] // group * (weights[2].shape[1] // width)

    def copies(slot, member):
        moves = [pltpu.make_async_copy(raw_out.at[slot], grad_inputs.at[span(member * raw_rows, raw_rows)], sems.at[slot, 0])]
        for index in range(4):
            rows = weights[index].shape[0] // group
            for kind, target in enumerate((grads, new_firsts, new_seconds, steps)):
                moves.append(
                    pltpu.make_async_copy(
                        buffers[index].at[slot, kind],
                        target[index].at[span(member * rows, rows)],
                        sems.at[slot, 1 + 4 * index + kind],
                    )
                )
        return moves

    def step(number, nothing):
        slot = number & 1
        member = me[0] ^ number

        @pl.when(number >= 2)
        def _():
            for move in copies(slot, member):
                move.wait()

        raw_out[slot] = d_raw[span(member * raw_rows, raw_rows), :] * count_scale
        for index, (source, first) in enumerate(((late, 0), (early, after_up), (early, down_rows), (early, 0))):
            rows = weights[index].shape[0] // group
            here = span(member * rows, rows)
            for block in range(weights[index].shape[1] // width):
                columns = slice(block * width, (block + 1) * width)
                gradient = source[number, first + block * rows : first + (block + 1) * rows, :].astype(f32) * count_scale
                results = adam_step(
                    weights[index][here, columns],
                    gradient,
                    firsts[index][here, columns],
                    seconds[index][here, columns],
                    scale_back,
                    weight_decay,
                )
                for kind, result in enumerate((gradient,) + results):
                    buffers[index][slot, kind, :, columns] = result
        for move in copies(slot, member):
            move.start()
        return nothing

    lax.fori_loop(0, group, step, 0)
    half = width // 2
    norm[...] = jnp.broadcast_to(grad_norm, norm.shape)

    def change(index, row, raw):
        where = (slice(row, row + 1), slice(None))
        gradient = raw * count_scale
        grads[index][where] = gradient
        results = adam_step(
            weights[index][where], gradient, firsts[index][where], seconds[index][where], scale_back, 0.0
        )
        new_firsts[index][where], new_seconds[index][where], steps[index][where] = results

    change(4, 0, sums_late[0:1, :half])
    change(4, 1, sums_early[0:1, :half])
    for row in range(3):
        change(5, row, sums_late[1 + row : 2 + row, :half])
    for row in range(3, 10):
        change(5, row, sums_early[row - 2 : row - 1, :half])
    for slot in (0, 1):
        for move in copies(slot, me[0] ^ slot):
            move.wait()


def adam_step(weight, gradient, first_old, second_old, scale_back, decay_rate):
    clipped = gradient * scale_back
    new_first = first_decay * first_old + (1.0 - first_decay) * clipped
    new_second = second_decay * second_old + ((1.0 - second_decay) * clipped) * clipped
    second_hat = new_second * (1.0 / (1.0 - second_decay**STEP))
    below = second_hat * lax.rsqrt(second_hat) + adam_floor
    inverse = pl.reciprocal(below, approx=True)
    inverse = inverse * (2.0 - below * inverse)
    inverse = inverse * (2.0 - below * inverse)
    update = (new_first * (-learn_rate / (1.0 - first_decay**STEP))) * inverse
    if decay_rate:
        update = update - (learn_rate * decay_rate) * weight.astype(f32)
    return (new_first, new_second, update)


def shaped(shape, kind):
    return jax.ShapeDtypeStruct(shape, kind)


in_place = pl.BlockSpec(memory_space=pl.ANY)


def attend(starts, core, qkv, kv, other_kv, state=None, final=True, spare=()):
    group, _, tokens = qkv.shape
    count = kv.shape[0]
    row = shaped((group, 1, tokens), f32)
    if final:
        out_shape = (shaped((group, HD, tokens), f32), row) + (shaped((HD, tokens), bf16),) * group
    else:
        out_shape = (shaped((group, HD + ONES, tokens), f32), row)
    state = state or ()
    return pl.pallas_call(
        functools.partial(attend_kernel, group=group, own=not state, final=final, spare=len(spare)),
        out_shape=out_shape + tuple(shaped(shape, bf16) for shape in spare),
        in_specs=[in_smem, in_smem] + [in_vmem] * (3 + len(state)),
        out_specs=(in_vmem,) * len(out_shape) + (in_place,) * len(spare),
        scratch_shapes=([pltpu.VMEM((group, HD, tokens), bf16)] if final else [])
        + [
            pltpu.VMEM((2, count, tokens, 2 * HD), bf16),
            pltpu.VMEM((2, count, HD + ONES, tokens), bf16),
            pltpu.VMEM((2 * HD, tokens), bf16),
            pltpu.VMEM((HD + ONES, tokens), f32),
            pltpu.VMEM((1, tokens), f32),
        ],
        cost_estimate=pl.CostEstimate(flops=30 * 2**30, bytes_accessed=5 * 2**20, transcendentals=2**24),
        compiler_params=pltpu.CompilerParams(vmem_limit_bytes=24 * 2**20),
        name="attend",
    )(starts, core, qkv, kv, other_kv, *state)


def attend_back(starts, core, qkv, kv, other_kv, d_out, out, log_total, after, d_query=None, own=True, low=0, count=0, final=False):
    group, _, tokens = qkv.shape
    resumed = d_query is not None
    return pl.pallas_call(
        functools.partial(attend_back_kernel, group=group, own=own, low=low, final=final, resumed=resumed),
        out_shape=(
            shaped((group, HD, tokens), bf16 if final else f32),
            shaped((count, 2 * HD, tokens), bf16),
            shaped((count, 2 * HD, tokens), bf16),
        ),
        in_specs=[in_smem, in_smem] + [in_vmem] * (5 + group + resumed) + [in_place] * len(after),
        out_specs=(in_vmem,) * 3,
        scratch_shapes=[
            pltpu.VMEM((group, HD, tokens), bf16),
            pltpu.VMEM((2, count, tokens, 2 * HD), bf16),
            pltpu.VMEM((2 * HD, tokens), bf16),
            pltpu.VMEM((2 * HD, tokens), bf16),
            pltpu.VMEM((2, count, 2 * HD, tokens), f32),
            pltpu.VMEM((HD, tokens), f32),
        ],
        cost_estimate=pl.CostEstimate(flops=count * 8 * 2**30, bytes_accessed=8 * 2**20, transcendentals=2**24),
        compiler_params=pltpu.CompilerParams(vmem_limit_bytes=32 * 2**20),
        name="attend_back",
    )(starts, core, qkv, kv, other_kv, out, log_total, *d_out, *((d_query,) if resumed else ()), *after)


def project(core, inputs, vectors, own, other):
    tokens, width = inputs.shape
    return pl.pallas_call(
        first_kernel,
        out_shape=shaped((width // HD, 3 * HD, tokens), bf16),
        in_specs=[in_smem] + [in_vmem] * 4,
        out_specs=in_vmem,
        cost_estimate=pl.CostEstimate(flops=2**30, bytes_accessed=4 * 2**20, transcendentals=0),
        compiler_params=pltpu.CompilerParams(vmem_limit_bytes=16 * 2**20),
        name="project",
    )(core, inputs, vectors, own, other)


def feed(core, mixed, inputs, targets, valid, vectors, *weights):
    tokens, width = inputs.shape
    group = width // HD
    hidden_units = weights[2].shape[1]
    rows = (2 * hidden_units + width) // 2 // group + 16
    return pl.pallas_call(
        feed_kernel,
        out_shape=(shaped((tokens, width), bf16), shaped((tokens, width), f32))
        + (shaped((group, rows, width), bf16),) * 2
        + (shaped((HD, tokens), bf16),) * group,
        in_specs=[in_smem] + [in_vmem] * (10 + group),
        out_specs=(in_vmem,) * (4 + group),
        scratch_shapes=[
            pltpu.VMEM((width, tokens), bf16),
            pltpu.VMEM((tokens, hidden_units), bf16),
            pltpu.VMEM((tokens, width), bf16),
            pltpu.VMEM((width, tokens), bf16),
            pltpu.VMEM((tokens, width), bf16),
            pltpu.VMEM((16, width), f32),
            pltpu.VMEM((width, tokens), bf16),
            pltpu.VMEM((tokens, width), f32),
            pltpu.VMEM((tokens, width), f32),
            pltpu.VMEM((tokens, hidden_units), f32),
            pltpu.VMEM((tokens, width), f32),
            pltpu.VMEM((1, hidden_units), f32),
        ],
        cost_estimate=pl.CostEstimate(flops=10 * 2**30, bytes_accessed=14 * 2**20, transcendentals=2**20),
        compiler_params=pltpu.CompilerParams(vmem_limit_bytes=34 * 2**20),
        name="feed",
    )(core, inputs, targets, valid, vectors, *weights, *mixed)


def first_back(group, core, d_heads, inputs, vectors, d_hidden, own, other):
    tokens, width = inputs.shape
    rows = own.shape[0] // group * 3 + 16
    return pl.pallas_call(
        first_back_kernel,
        out_shape=(shaped((tokens, width), f32),) + (shaped((group, rows, width), bf16),) * 2,
        in_specs=[in_smem] + [in_vmem] * 6,
        out_specs=(in_vmem,) * 3,
        scratch_shapes=[pltpu.VMEM((3 * width, tokens), bf16), pltpu.VMEM((width + 16, tokens), f32)],
        cost_estimate=pl.CostEstimate(flops=4 * 2**30, bytes_accessed=8 * 2**20, transcendentals=0),
        compiler_params=pltpu.CompilerParams(vmem_limit_bytes=24 * 2**20),
        name="first_back",
    )(core, d_heads, inputs, vectors, d_hidden, own, other)


def sum_squares(sums_early, sums_late, early, late):
    return pl.pallas_call(
        squares_kernel,
        out_shape=shaped((8, 128), f32),
        in_specs=[in_vmem] * (2 + 2 * len(early)),
        out_specs=in_vmem,
        cost_estimate=pl.CostEstimate(flops=2**22, bytes_accessed=4 * 2**20, transcendentals=0),
        compiler_params=pltpu.CompilerParams(vmem_limit_bytes=16 * 2**20),
        name="sum_squares",
    )(sums_early, sums_late, *early, *late)


def update(group, me, total_rows, squares, other_squares, sums_early, sums_late, d_raw, early, late, *state):
    weights = state[0]
    like = [shaped(weight.shape, f32) for weight in weights]
    out_specs = [in_place] * 4 + [in_vmem] * 2
    return pl.pallas_call(
        functools.partial(update_kernel, group=group, total_rows=total_rows),
        out_shape=[shaped(d_raw.shape, f32), shaped((8, 128), f32)] + like * 4,
        in_specs=[in_smem] + [in_vmem] * (5 + 2 * group + 18),
        out_specs=[in_place, in_vmem] + out_specs * 4,
        scratch_shapes=[
            pltpu.VMEM((group,) + early[0].shape, bf16),
            pltpu.VMEM((group,) + late[0].shape, bf16),
            pltpu.VMEM((2, d_raw.shape[0] // group, d_raw.shape[1]), f32),
        ]
        + [pltpu.VMEM((2, 4, weight.shape[0] // group, weight.shape[1]), f32) for weight in weights[:4]]
        + [pltpu.SemaphoreType.DMA((2, 17))],
        cost_estimate=pl.CostEstimate(flops=2**26, bytes_accessed=44 * 2**20, transcendentals=2**22),
        compiler_params=pltpu.CompilerParams(vmem_limit_bytes=31 * 2**20),
        name="update",
    )(me, squares, other_squares, sums_early, sums_late, d_raw, *early, *late, *state[0], *state[1], *state[2])


def from_other_core(value):
    return lax.ppermute(value, "fsdp", [(0, 1), (1, 0)])


def whole_of(value, axis):
    other = from_other_core(value)
    first = lax.axis_index("fsdp") == 0
    return jnp.concatenate([jnp.where(first, value, other), jnp.where(first, other, value)], axis)


def swap_ctx(value, bit):
    size = lax.axis_size("ctx")
    return lax.ppermute(value, "ctx", [(i, i ^ bit) for i in range(size)])


def across_groups(value, group):
    low, sums = value[:-16].astype(bf16), value[-16:]
    bit = group
    while bit < lax.axis_size("ctx"):
        sent = value.astype(bf16)
        received = swap_ctx(sent, bit)
        low = (sent[:-16].astype(f32) + received[:-16].astype(f32)).astype(bf16)
        sums = sent[-16:].astype(f32) + received[-16:].astype(f32)
        value = jnp.concatenate([low.astype(f32), sums], 0) if 2 * bit < lax.axis_size("ctx") else None
        bit *= 2
    return low, sums


def per_device(
    inputs,
    targets,
    valid_mask,
    block_seq,
    w_qkv,
    w_out,
    w_up,
    w_down,
    norm_gains,
    biases,
    first_qkv,
    first_out,
    first_up,
    first_down,
    first_gains,
    first_biases,
    second_qkv,
    second_out,
    second_up,
    second_down,
    second_gains,
    second_biases,
):
    rows_here, width = inputs.shape
    group = width // HD
    ctx_size = lax.axis_size("ctx")
    block_rows = rows_here * 2
    total_rows = float(block_rows * ctx_size)
    ctx_place = lax.axis_index("ctx")
    core_place = lax.axis_index("fsdp")
    members = [[first + i for i in range(group)] for first in range(0, ctx_size, group)]

    def exchange(value):
        return lax.all_to_all(value, "ctx", 0, 0, axis_index_groups=members, tiled=True)

    core = jnp.stack([core_place, ctx_place % group]).astype(jnp.int32)
    vectors = whole_of(jnp.concatenate([norm_gains, biases], 0), 1).astype(f32)
    other_qkv = from_other_core(w_qkv)
    other_out, other_up, other_down = (from_other_core(w_out), from_other_core(w_up), from_other_core(w_down))
    valid_rows = valid_mask.astype(f32)
    qkv = exchange(project(core, inputs, vectors, w_qkv, other_qkv))
    own_kv = qkv[:, HD:]
    other_kv = from_other_core(own_kv)

    first_block = (ctx_place // group) * group
    own_seq = lax.dynamic_slice_in_dim(block_seq, first_block, group, 0)
    starts = jnp.sum((block_seq[None, :] < own_seq[:, None]).astype(jnp.int32), axis=1)
    starts = jnp.maximum(starts - first_block + group, 0)
    behind = jnp.zeros((), jnp.int32)
    for edge in range(group, ctx_size, group):
        same = (block_seq[edge - group : edge] == block_seq[edge]).astype(jnp.int32)
        behind = jnp.maximum(behind, jnp.sum(same))
    most_behind = group - 1
    few_behind = group // 2
    branch = (behind > 0).astype(jnp.int32) + (behind > few_behind).astype(jnp.int32)
    counts = (0, few_behind, most_behind)

    def forward(count, own, other):
        spare = [(size, 2 * HD, rows_here) for size in counts[1:] if size != count for _ in (0, 1)]
        if count == 0:
            return tuple(attend(starts, core, qkv, qkv, other, spare=spare))
        prev_own = lax.ppermute(own[group - count :], "ctx", [(i, i + group) for i in range(ctx_size - group)])
        state = attend(starts, core, qkv, qkv, other, final=False)
        prev_own, state = lax.optimization_barrier((prev_own, state))
        prev_other = from_other_core(prev_own)
        mixed = tuple(attend(starts, core, qkv, prev_own, prev_other, state=state, spare=spare))
        prev = (prev_own, prev_other)
        unread = mixed[2 + group :]
        return mixed[: 2 + group] + (prev + unread if count == few_behind else unread + prev)

    results = lax.switch(branch, [functools.partial(forward, count) for count in counts], own_kv, other_kv)
    mixed, log_total = results[:2]
    prev = results[2 + group :]

    def deal(pieces):
        moved = []
        for step in range(1, group):
            moved.append(lax.ppermute(pieces[step], "ctx", [(i, i ^ step) for i in range(ctx_size)]))
        return [pieces[0]] + moved

    results = feed(
        core,
        deal(results[2 : 2 + group]),
        inputs,
        targets,
        valid_rows[:, None],
        vectors,
        w_out,
        other_out,
        w_up,
        other_up,
        w_down,
        other_down,
    )
    outputs, d_hidden, keep, send = results[:4]
    d_mixed = deal(results[4:])

    def paired(keep, received):
        return [(keep[i].astype(f32) + received[i].astype(f32)).astype(bf16) for i in range(group)]

    def gathered(pairs):
        return paired_sum([piece.astype(f32) for piece in deal(pairs)])

    def finished(mine):
        return across_groups(mine, group)

    pair = (keep.astype(f32) + from_other_core(send).astype(f32)).astype(bf16)
    pair, d_mixed = lax.optimization_barrier((pair, d_mixed))
    early_mine = jnp.sum(exchange(pair).astype(f32), axis=0)
    cuts = (0, 3, 5, group)

    def back(part, after, d_query, d_mixed):
        low, high = cuts[part], cuts[part + 1]
        return attend_back(
            starts,
            core,
            qkv,
            qkv,
            other_kv,
            d_mixed,
            mixed,
            log_total,
            after,
            d_query=d_query,
            low=low,
            count=high - low,
            final=high == group,
        )

    def backward(count, d_mixed, pair, prev):
        if count == 0:
            return tuple(back(0, (pair,), None, d_mixed)) + tuple(
                jnp.zeros((high - low, 2 * HD, rows_here), bf16) for low, high in zip(cuts[1:-1], cuts[2:])
            )
        prev_own, prev_other = prev[:2] if count == few_behind else prev[2:]
        d_query, d_behind, d_behind_other = attend_back(
            starts,
            core,
            qkv,
            prev_own,
            prev_other,
            d_mixed,
            mixed,
            log_total,
            (pair,),
            own=False,
            count=count,
        )
        d_prev = (d_behind.astype(f32) + from_other_core(d_behind_other).astype(f32)).astype(bf16)
        d_prev = lax.ppermute(d_prev, "ctx", [(i + group, i) for i in range(ctx_size - group)])
        results = tuple(back(0, (pair,), d_query, d_mixed))
        (d_query, d_own, d_other), d_prev = lax.optimization_barrier((results, d_prev))
        d_prev = jnp.pad(d_prev, ((group - count, 0), (0, 0), (0, 0)))
        d_own = (d_own.astype(f32) + d_prev[: cuts[1]].astype(f32)).astype(bf16)
        return (d_query, d_own, d_other) + tuple(d_prev[low:high] for low, high in zip(cuts[1:-1], cuts[2:]))

    def summed(d_own, d_other, *more):
        return sum((one.astype(f32) for one in more), d_own.astype(f32) + from_other_core(d_other).astype(f32)).astype(bf16)

    d_query, d_own, d_other, *d_prev = lax.switch(
        branch, [functools.partial(backward, count) for count in counts], d_mixed, pair, prev
    )
    first_sum = (d_own, d_other)
    d_query, d_own, d_other = back(1, (early_mine,), d_query, d_mixed)
    d_kv = [summed(*first_sum)]
    second_sum = (d_own, d_other)
    early_low, early_sums = finished(early_mine)
    d_query, d_own, d_other = back(2, (early_low, d_kv[0]), d_query, d_mixed)

    def forward_piece(piece, step):
        return lax.ppermute(piece, "ctx", [(i, i ^ step) for i in range(ctx_size)])

    early = [early_low] + [forward_piece(early_low, step) if step in (1, 2, 4) else None for step in range(1, group)]
    (early[1], early[2], early[4]), d_own, d_other = lax.optimization_barrier(
        ((early[1], early[2], early[4]), d_own, d_other)
    )
    d_kv += [summed(*second_sum, d_prev[0]), summed(d_own, d_other, d_prev[1])]
    d_heads = exchange(jnp.concatenate([d_query, jnp.concatenate(d_kv, 0)], 1))
    d_heads, (early[1], early[2], early[4]) = lax.optimization_barrier((d_heads, (early[1], early[2], early[4])))
    early[3] = forward_piece(early[2], 1)
    early[5] = forward_piece(early[1], 4)
    early[6] = forward_piece(early[4], 2)
    early[7] = forward_piece(early[6], 1)
    d_raw, keep, send = first_back(group, core, d_heads, inputs, vectors, d_hidden, w_qkv, other_qkv)
    (early[3], early[5], early[6]), keep, send = lax.optimization_barrier(((early[3], early[5], early[6]), keep, send))
    late_low, late_sums = finished(gathered(paired(keep, from_other_core(send))))
    late = deal([late_low] * group)
    squares = sum_squares(early_sums, late_sums, early, late)
    results = update(
        group,
        core[1:],
        total_rows,
        squares,
        from_other_core(squares),
        early_sums,
        late_sums,
        d_raw,
        early,
        late,
        [w_qkv, w_out, w_up, w_down, norm_gains, biases],
        [first_qkv, first_out, first_up, first_down, first_gains, first_biases],
        [second_qkv, second_out, second_up, second_down, second_gains, second_biases],
    )
    grad_inputs, norm = results[:2]
    return (outputs, grad_inputs) + tuple(results[2:8]) + (norm[0, 0],) + tuple(results[8:])


def solution(mesh):
    tokens = P(("ctx", "fsdp"), None)
    weight = P("fsdp", None)
    vector = P(None, "fsdp")
    params = (weight, weight, weight, weight, vector, vector)
    in_specs = (tokens, tokens, P(("ctx", "fsdp")), P()) + params * 3
    out_specs = (tokens, tokens) + params + (P(),) + params * 3
    return jax.shard_map(per_device, mesh=mesh, in_specs=in_specs, out_specs=out_specs, check_vma=False)
```

```python
import functools
import math

import jax
import jax.numpy as jnp
from jax import lax
from jax.experimental import pallas as pl
from jax.experimental.pallas import tpu as pltpu
from jax.sharding import PartitionSpec as P

HD = 64
STEP = 10

very_low = -1e30
norm_floor = 1e-05
first_decay = 0.9
second_decay = 0.95
adam_floor = 1e-08
learn_rate = 0.02
weight_decay = 0.1
clip_limit = 0.01
gelu_scale = (2.0 / math.pi) ** 0.5
gelu_cubic = 0.044715

BASE_LIMIT = 1e20
ONES = 16

bf16 = jnp.bfloat16
f32 = jnp.float32
NN = (((1,), (0,)), ((), ()))
NT = (((1,), (1,)), ((), ()))
TN = (((0,), (0,)), ((), ()))


def mxu(left, right, dims):
    return lax.dot_general(left, right, dims, preferred_element_type=f32)


def below_diagonal(scores):
    key_pos = lax.broadcasted_iota(jnp.int32, scores.shape, 0)
    query_pos = lax.broadcasted_iota(jnp.int32, scores.shape, 1)
    return jnp.where(key_pos <= query_pos, scores, very_low)


def column_sum(values):
    return jnp.sum(values, axis=0, keepdims=True)


def column_max(values):
    return jnp.max(values, axis=0, keepdims=True)


def normalize(rows):
    center = rows - jnp.mean(rows, axis=1, keepdims=True)
    inverse = lax.rsqrt(jnp.mean(center * center, axis=1, keepdims=True) + norm_floor)
    return center * inverse, inverse


def span(start, size):
    return pl.ds(pl.multiple_of(start, size), size)


def attend_kernel(starts, place_of, qkv, kv, other_kv, *refs, group, own, final, spare):
    if own:
        acc_in = base_in = None
    else:
        acc_in, base_in = refs[:2]
        refs = refs[2:]
    if final:
        out, log_total = refs[:2]
        pieces = refs[2 : 2 + group]
        low, kv_rows, v_ones, q_pad, acc, high = refs[2 + group + spare :]
    else:
        acc_out, base_out, kv_rows, v_ones, q_pad, acc, high = refs
    tokens = q_pad.shape[1]
    count = kv.shape[0]
    ones = jnp.ones((ONES, tokens), bf16)
    for place in range(count):
        for kind, source in ((0, kv), (1, other_kv)):
            here = source[place, source.shape[1] - 2 * HD :, :]
            kv_rows[kind, place] = here.T
            v_ones[kind, place, :HD, :] = here[HD:]
            v_ones[kind, place, HD:, :] = ones
    q_pad[HD:, :] = jnp.zeros((HD, tokens), bf16)

    def score(kind, place):
        return mxu(kv_rows[kind, place], q_pad[...], NN)

    def weigh(kind, place, scores, base):
        return mxu(v_ones[kind, place], jnp.exp(scores - base).astype(bf16), NN)

    def finish(place):
        if final:
            total = acc[HD : HD + 1, :]
            mixed = acc[:HD, :] * (1.0 / total)
            out[place] = mixed
            low[place] = mixed.astype(bf16)
            log_total[place] = high[...] + jnp.log(total)
        else:
            acc_out[place] = acc[...]
            base_out[place] = high[...]

    def begin(place):
        q_pad[:HD, :] = qkv[place, :HD, :] * bf16(HD**-0.5)
        if not own:
            high[...] = base_in[place]
            acc[...] = acc_in[place]
        return jnp.maximum(starts[place] - (group if own else group - count), 0)

    def quick(place, largest):
        first = begin(place)
        if own:
            scores = below_diagonal(score(0, place))
            base = column_max(scores)
            high[...] = base
            acc[...] = weigh(0, place, scores, base)

        def loop(kinds, first, last):
            def body(key_place, nothing):
                base = high[...]
                acc[...] += sum(weigh(kind, key_place, score(kind, key_place), base) for kind in kinds)
                return nothing

            lax.fori_loop(first, last, body, 0)

        if own:
            loop((1,), place, place + place_of[0])
        loop((0, 1), first, place if own else count)
        finish(place)
        return jnp.maximum(largest, acc[HD : HD + 1, :])

    largest = lax.fori_loop(0, group, quick, jnp.zeros((1, tokens), f32))

    @pl.when(jnp.logical_not(jnp.max(largest) < BASE_LIMIT))
    def _():
        rows = 128

        def careful(place, nothing):
            first = begin(place)
            if own:
                high[...] = jnp.full(high.shape, very_low, f32)
                acc[...] = jnp.zeros(acc.shape, f32)

            def by_kind(kind, nothing):
                def by_place(key_place, nothing):
                    def by_rows(index, nothing):
                        here = span(index * rows, rows)
                        scores = mxu(kv_rows[kind, key_place, here, :], q_pad[...], NN)
                        if own:
                            key_pos = index * rows + lax.broadcasted_iota(jnp.int32, scores.shape, 0)
                            query_pos = lax.broadcasted_iota(jnp.int32, scores.shape, 1)
                            query_pos = query_pos + jnp.where((kind == 0) & (key_place == place), 0, tokens)
                            scores = jnp.where(key_pos <= query_pos, scores, very_low)
                        old = high[...]
                        new = jnp.maximum(old, column_max(scores))
                        probs = jnp.exp(scores - new).astype(bf16)
                        acc[...] = acc[...] * jnp.exp(old - new) + mxu(v_ones[kind, key_place, :, here], probs, NN)
                        high[...] = new
                        return nothing

                    return lax.fori_loop(0, tokens // rows, by_rows, nothing)

                last = place + jnp.where(kind == 0, 1, place_of[0]) if own else count
                return lax.fori_loop(first, last, by_place, nothing)

            lax.fori_loop(0, 2, by_kind, 0)
            finish(place)
            return nothing

        lax.fori_loop(0, group, careful, 0)

    if final:
        for step, piece in enumerate(pieces):
            piece[...] = low[place_of[1] ^ step]


def attend_back_kernel(starts, place_of, qkv, kv, other_kv, out, log_total, *refs, group, own, low, final, resumed):
    pieces = refs[:group]
    d_query_in = refs[group] if resumed else None
    d_query, d_kv, d_other_kv, d_out, kv_rows, q_pad, d_pad, d_kv_sum, d_query_sum = refs[-9:]
    for step, piece in enumerate(pieces):
        d_out[place_of[1] ^ step] = piece[...]
    tokens = q_pad.shape[1]
    count = d_kv.shape[0]
    sources = (kv, other_kv)
    for place in range(count):
        for kind in (0, 1):
            source = sources[kind]
            kv_rows[kind, place] = source[low + place, source.shape[1] - 2 * HD :, :].T
    q_pad[HD:, :] = jnp.zeros((HD, tokens), bf16)
    d_pad[:HD, :] = jnp.zeros((HD, tokens), bf16)
    d_kv_sum[...] = jnp.zeros(d_kv_sum.shape, f32)

    def tile(kind, place, masked, delta, log_row):
        source = sources[kind]
        rows = kv_rows[kind, place]
        scores = mxu(rows, q_pad[...], NN)
        if masked:
            scores = below_diagonal(scores)
        probs = jnp.exp(scores - log_row)
        d_probs = mxu(rows, d_pad[...], NN)
        d_scores = (probs * (d_probs - delta)).astype(bf16)
        d_kv_sum[kind, place] += mxu(q_pad[...], d_scores, NT) + mxu(d_pad[...], probs.astype(bf16), NT)
        first = source.shape[1] - 2 * HD
        return mxu(source[low + place, first : first + HD, :], d_scores, NN)

    def chunk(place, nothing):
        q_pad[:HD, :] = qkv[place, :HD, :] * bf16(HD**-0.5)
        d_here = d_out[place]
        d_pad[HD:, :] = d_here
        delta = column_sum(d_here.astype(f32) * out[place])
        log_row = log_total[place]
        d_query_sum[...] = d_query_in[place] if resumed else jnp.zeros(d_query_sum.shape, f32)

        def loop(kinds, first, last):
            def body(key_place, nothing):
                d_query_sum[...] += sum(tile(kind, key_place, False, delta, log_row) for kind in kinds)
                return nothing

            lax.fori_loop(first, last, body, 0)

        if own:
            here = place - low

            @pl.when(jnp.logical_and(here >= 0, here < count))
            def _():
                d_query_sum[...] += tile(0, here, True, delta, log_row)
                loop((1,), here, here + place_of[0])

            loop((0, 1), jnp.maximum(starts[place] - group - low, 0), jnp.minimum(here, count))
        else:
            loop((0, 1), jnp.maximum(starts[place] - (group - count), 0), count)
        if final:
            d_query[place] = (d_query_sum[...] * HD**-0.5).astype(bf16)
        else:
            d_query[place] = d_query_sum[...]
        return nothing

    lax.fori_loop(0, group, chunk, 0)
    d_kv[...] = d_kv_sum[0].astype(bf16)
    d_other_kv[...] = d_kv_sum[1].astype(bf16)


def first_kernel(core, inputs, vectors, own, other, by_head):
    width = inputs.shape[1]
    half = width // 2
    unit, _ = normalize(inputs[...].astype(f32))
    normed = (unit * vectors[0:1, :] + vectors[2:3, :]).astype(bf16)
    swap = core[0] == 1
    low, high = normed[:, :half], normed[:, half:]
    mine, rest = jnp.where(swap, high, low), jnp.where(swap, low, high)
    for part in range(3):
        columns = slice(part * width, (part + 1) * width)
        rows = mxu(mine, own[:, columns], NN) + mxu(rest, other[:, columns], NN)
        if part != 1:
            row = 3 + part // 2
            rows = rows + vectors[row : row + 1, :]
        turned = rows.astype(bf16).T
        for head in range(width // HD):
            by_head[head, part * HD : (part + 1) * HD, :] = turned[head * HD : (head + 1) * HD]


in_vmem = pl.BlockSpec(memory_space=pltpu.VMEM)
in_smem = pl.BlockSpec(memory_space=pltpu.SMEM)


def norm_back(d_rows, unit, inverse, gain):
    scaled = d_rows * gain
    first = jnp.mean(scaled, axis=1, keepdims=True)
    second = jnp.mean(scaled * unit, axis=1, keepdims=True)
    return inverse * (scaled - first - unit * second)


def feed_kernel(
    core,
    inputs,
    targets,
    valid,
    vectors,
    out_own,
    out_other,
    up_own,
    up_other,
    down_own,
    down_other,
    *refs,
):
    group = inputs.shape[1] // HD
    mixed, refs = refs[:group], refs[group:]
    outputs, d_hidden, keep, send = refs[:4]
    pieces, refs = refs[4 : 4 + group], refs[4 + group :]
    attended, active, normed, normed_turned, d_out_low, small, d_attended, hidden, unit, slope, acc, up_sum = refs
    for index, piece in enumerate(mixed):
        attended[span((core[1] ^ index) * HD, HD), :] = piece[...]
    tokens, width = inputs.shape
    half = width // 2
    f_half = down_own.shape[0]
    wide = 1024
    rows = f_half // group
    up_rows = half // group
    place = core[0]
    halves = ((place, out_own, up_own, down_own), (1 - place, out_other, up_other, down_other))
    hidden[...] = inputs[...].astype(f32) + vectors[5:6, :]
    for where, w_out, _, _ in halves:
        hidden[...] += mxu(attended[span(where * half, half), :], w_out[...], TN)
    unit_here, inverse = normalize(hidden[...])
    unit[...] = unit_here
    normed_here = (unit_here * vectors[1:2, :] + vectors[6:7, :]).astype(bf16)
    normed[...] = normed_here
    normed_turned[...] = normed_here.T
    for row in range(4):
        up_sum[:, row * width : (row + 1) * width] = vectors[8 + row : 9 + row, :]
    acc[...] = hidden[...] + vectors[7:8, :]
    for where, _, _, w_down in halves:

        def lift(index, nothing):
            columns = span(where * f_half + index * wide, wide)
            u = up_sum[:, columns]
            for other, _, w_up, _ in halves:
                u = u + mxu(normed[:, span(other * half, half)], w_up[:, columns], NN)
            square = u * u
            tanh = jnp.tanh(gelu_scale * (u + gelu_cubic * (square * u)))
            side = 0.5 * (1.0 + tanh)
            act = (u * side).astype(bf16)
            active[:, columns] = act
            slope[:, columns] = side + (0.5 * gelu_scale) * u * (1.0 - tanh * tanh) * (
                1.0 + (3.0 * gelu_cubic) * square
            )
            acc[...] += mxu(act, w_down[span(index * wide, wide), :], NN)
            return nothing

        lax.fori_loop(0, f_half // wide, lift, 0)
    out_f32 = acc[...]
    outputs[...] = out_f32.astype(bf16)
    d_out = valid[...] * (out_f32 - targets[...].astype(f32))
    d_hidden[...] = d_out
    d_out_low[...] = d_out.astype(bf16)
    small[...] = jnp.zeros(small.shape, f32)
    small[3:4, :] = column_sum(d_out)
    acc[...] = jnp.zeros(acc.shape, f32)
    for target, (where, _, _, w_down) in zip((keep, send), halves):

        def lower(index, nothing):
            columns = span(where * f_half + index * wide, wide)
            d_active = mxu(d_out_low[...], w_down[span(index * wide, wide), :], NT)
            low = (d_active * slope[:, columns]).astype(bf16)
            up_sum[:, columns] = column_sum(low.astype(f32))
            for side, (other, _, w_up, _) in zip((keep, send), halves):
                acc[:, span(other * half, half)] += mxu(low, w_up[:, columns], NT)
                gradient = mxu(normed_turned[span(other * half, half), :], low, NN).astype(bf16)
                for block in range(wide // width):
                    number = (where * f_half) // width + index * (wide // width) + block
                    first = pl.multiple_of(rows + number * up_rows, up_rows)
                    for member in range(group):
                        side[member, pl.ds(first, up_rows), :] = gradient[
                            member * up_rows : (member + 1) * up_rows, block * width : (block + 1) * width
                        ]
            gradient = mxu(active[:, columns], d_out_low[...], TN).astype(bf16)
            for part in range(wide // rows):
                target[index * (wide // rows) + part, :rows, :] = gradient[part * rows : (part + 1) * rows]
            return nothing

        lax.fori_loop(0, f_half // wide, lower, 0)
    for row in range(4):
        small[4 + row : 5 + row, :] = up_sum[:, row * width : (row + 1) * width]
    d_normed = acc[...]
    unit_here = unit[...]
    small[0:1, :] = column_sum(d_normed * unit_here)
    small[2:3, :] = column_sum(d_normed)
    d_rows = d_hidden[...] + norm_back(d_normed, unit_here, inverse, vectors[1:2, :])
    d_hidden[...] = d_rows
    small[1:2, :] = column_sum(d_rows)
    low = d_rows.astype(bf16)
    for where, w_out, _, _ in halves:
        d_attended[span(where * half, half), :] = mxu(w_out[...], low, NT).astype(bf16)
    for index, piece in enumerate(pieces):
        piece[...] = d_attended[span((core[1] ^ index) * HD, HD), :]
    lanes = lax.broadcasted_iota(jnp.int32, (tokens, 128), 1)
    token = lax.broadcasted_iota(jnp.int32, (tokens, 128), 0)
    counts = column_sum(jnp.where(token % 128 == lanes, valid[...], 0.0))
    small[8:9, :128] = counts
    small[8:9, half : half + 128] = counts
    first = rows + up_rows * (2 * f_half // width)
    for target, (where, _, _, _) in zip((keep, send), halves):
        here = span(where * half, half)
        spread_rows(target, mxu(attended[here, :], low, NN), first, up_rows, 0)
        sums = jnp.concatenate([small[:, here], jnp.zeros(small[:, here].shape, f32)], 1).astype(bf16)
        for member in range(group):
            target[member, first + up_rows :, :] = sums


def spread_rows(target, gradient, first, rows, me):
    low = gradient.astype(bf16)
    for member in range(target.shape[0]):
        target[member ^ me, first : first + rows, :] = low[member * rows : (member + 1) * rows]


def first_back_kernel(core, d_heads, inputs, vectors, d_hidden, own, other, d_inputs, keep, send, d_proj, d_normed):
    width = inputs.shape[1]
    half = width // 2
    members = keep.shape[0]
    place = core[0]
    for head in range(width // HD):
        for part in range(3):
            d_proj[part * width + head * HD : part * width + (head + 1) * HD, :] = d_heads[
                head, part * HD : (part + 1) * HD, :
            ]
    unit, inverse = normalize(inputs[...].astype(f32))
    normed = (unit * vectors[0:1, :] + vectors[2:3, :]).astype(bf16).T
    for where, weight in ((place, own), (1 - place, other)):
        d_normed[span(where * half, half), :] = mxu(weight[...], d_proj[...], NN)
    d_rows = d_normed[:width, :].T
    d_inputs[...] = d_hidden[...] + norm_back(d_rows, unit, inverse, vectors[0:1, :])
    gain_sum = column_sum(d_rows * unit)
    offset_sum = column_sum(d_rows)
    ones = jnp.ones((ONES, inputs.shape[0]), bf16)
    query_sum = mxu(ones, d_proj[:width], NT)[:1]
    value_sum = mxu(ones, d_proj[2 * width :], NT)[:1]
    sums = jnp.concatenate([gain_sum, offset_sum, query_sum, value_sum, jnp.zeros((ONES - 4, width), f32)], 0)
    rows = half // members
    d_normed[:ONES, :] = sums
    for part in range(3):
        gradient = mxu(normed, d_proj[part * width : (part + 1) * width], NT)
        d_normed[ONES : ONES + width, :] = gradient
        for target, where in ((keep, place), (send, 1 - place)):
            low = d_normed[pl.ds(pl.multiple_of(ONES + where * half, ONES), half), :]
            spread_rows(target, low, part * rows, rows, core[1])
    for target, where in ((keep, place), (send, 1 - place)):
        low = d_normed[:ONES, span(where * half, half)]
        low = jnp.concatenate([low, jnp.zeros(low.shape, f32)], 1).astype(bf16)
        for member in range(members):
            target[member, 3 * rows :, :] = low


def squares_kernel(sums_early, sums_late, *refs):
    pieces, squares = refs[:-1], refs[-1]
    group = len(pieces) // 2
    half = sums_early.shape[1] // 2

    def square_sum(values):
        values = values.astype(f32)
        return jnp.sum(column_sum(values * values), axis=1, keepdims=True)

    parts = [square_sum(early[...]) + square_sum(late[...]) for early, late in zip(pieces[:group], pieces[group:])]
    total = paired_sum(parts) + (square_sum(sums_early[:8, :half]) + square_sum(sums_late[:4, :half]))
    squares[...] = jnp.broadcast_to(total, squares.shape)


def paired_sum(parts):
    while len(parts) > 1:
        parts = [parts[i] + parts[i + 1] for i in range(0, len(parts), 2)]
    return parts[0]


def update_kernel(me, squares, other_squares, sums_early, sums_late, d_raw, *refs, group, total_rows):
    early_pieces, late_pieces, refs = refs[:group], refs[group : 2 * group], refs[2 * group :]
    weights, firsts, seconds, refs = refs[0:6], refs[6:12], refs[12:18], refs[18:]
    grad_inputs, norm = refs[:2]
    grads, new_firsts, new_seconds, steps = refs[2:8], refs[8:14], refs[14:20], refs[20:26]
    early, late, raw_out = refs[26:29]
    buffers, sems = refs[29:33], refs[33]
    for index in range(group):
        early[index] = early_pieces[index][...]
        late[index] = late_pieces[index][...]

    count_scale = total_rows / jnp.sum(sums_early[8:9, :128], axis=1, keepdims=True)
    total = squares[:1, :1] + other_squares[:1, :1]
    grad_norm = jnp.sqrt(total) * count_scale / total_rows
    scale_back = jnp.minimum(1.0, clip_limit / grad_norm) / total_rows
    width = d_raw.shape[1]
    raw_rows = d_raw.shape[0] // group
    down_rows = weights[3].shape[0] // group
    after_up = down_rows + weights[2].shape[0] // group * (weights[2].shape[1] // width)

    def copies(slot, member):
        moves = [pltpu.make_async_copy(raw_out.at[slot], grad_inputs.at[span(member * raw_rows, raw_rows)], sems.at[slot, 0])]
        for index in range(4):
            rows = weights[index].shape[0] // group
            for kind, target in enumerate((grads, new_firsts, new_seconds, steps)):
                moves.append(
                    pltpu.make_async_copy(
                        buffers[index].at[slot, kind],
                        target[index].at[span(member * rows, rows)],
                        sems.at[slot, 1 + 4 * index + kind],
                    )
                )
        return moves

    def step(number, nothing):
        slot = number & 1
        member = me[0] ^ number

        @pl.when(number >= 2)
        def _():
            for move in copies(slot, member):
                move.wait()

        raw_out[slot] = d_raw[span(member * raw_rows, raw_rows), :] * count_scale
        for index, (source, first) in enumerate(((late, 0), (early, after_up), (early, down_rows), (early, 0))):
            rows = weights[index].shape[0] // group
            here = span(member * rows, rows)
            for block in range(weights[index].shape[1] // width):
                columns = slice(block * width, (block + 1) * width)
                gradient = source[number, first + block * rows : first + (block + 1) * rows, :].astype(f32) * count_scale
                results = adam_step(
                    weights[index][here, columns],
                    gradient,
                    firsts[index][here, columns],
                    seconds[index][here, columns],
                    scale_back,
                    weight_decay,
                )
                for kind, result in enumerate((gradient,) + results):
                    buffers[index][slot, kind, :, columns] = result
        for move in copies(slot, member):
            move.start()
        return nothing

    lax.fori_loop(0, group, step, 0)
    half = width // 2
    norm[...] = jnp.broadcast_to(grad_norm, norm.shape)

    def change(index, row, raw):
        where = (slice(row, row + 1), slice(None))
        gradient = raw * count_scale
        grads[index][where] = gradient
        results = adam_step(
            weights[index][where], gradient, firsts[index][where], seconds[index][where], scale_back, 0.0
        )
        new_firsts[index][where], new_seconds[index][where], steps[index][where] = results

    change(4, 0, sums_late[0:1, :half])
    change(4, 1, sums_early[0:1, :half])
    for row in range(3):
        change(5, row, sums_late[1 + row : 2 + row, :half])
    for row in range(3, 10):
        change(5, row, sums_early[row - 2 : row - 1, :half])
    for slot in (0, 1):
        for move in copies(slot, me[0] ^ slot):
            move.wait()


def adam_step(weight, gradient, first_old, second_old, scale_back, decay_rate):
    clipped = gradient * scale_back
    new_first = first_decay * first_old + (1.0 - first_decay) * clipped
    new_second = second_decay * second_old + ((1.0 - second_decay) * clipped) * clipped
    second_hat = new_second * (1.0 / (1.0 - second_decay**STEP))
    below = second_hat * lax.rsqrt(second_hat) + adam_floor
    inverse = pl.reciprocal(below, approx=True)
    inverse = inverse * (2.0 - below * inverse)
    inverse = inverse * (2.0 - below * inverse)
    update = (new_first * (-learn_rate / (1.0 - first_decay**STEP))) * inverse
    if decay_rate:
        update = update - (learn_rate * decay_rate) * weight.astype(f32)
    return (new_first, new_second, update)


def shaped(shape, kind):
    return jax.ShapeDtypeStruct(shape, kind)


in_place = pl.BlockSpec(memory_space=pl.ANY)


def attend(starts, core, qkv, kv, other_kv, state=None, final=True, spare=()):
    group, _, tokens = qkv.shape
    count = kv.shape[0]
    row = shaped((group, 1, tokens), f32)
    if final:
        out_shape = (shaped((group, HD, tokens), f32), row) + (shaped((HD, tokens), bf16),) * group
    else:
        out_shape = (shaped((group, HD + ONES, tokens), f32), row)
    state = state or ()
    return pl.pallas_call(
        functools.partial(attend_kernel, group=group, own=not state, final=final, spare=len(spare)),
        out_shape=out_shape + tuple(shaped(shape, bf16) for shape in spare),
        in_specs=[in_smem, in_smem] + [in_vmem] * (3 + len(state)),
        out_specs=(in_vmem,) * len(out_shape) + (in_place,) * len(spare),
        scratch_shapes=([pltpu.VMEM((group, HD, tokens), bf16)] if final else [])
        + [
            pltpu.VMEM((2, count, tokens, 2 * HD), bf16),
            pltpu.VMEM((2, count, HD + ONES, tokens), bf16),
            pltpu.VMEM((2 * HD, tokens), bf16),
            pltpu.VMEM((HD + ONES, tokens), f32),
            pltpu.VMEM((1, tokens), f32),
        ],
        cost_estimate=pl.CostEstimate(flops=30 * 2**30, bytes_accessed=5 * 2**20, transcendentals=2**24),
        compiler_params=pltpu.CompilerParams(vmem_limit_bytes=24 * 2**20),
        name="attend",
    )(starts, core, qkv, kv, other_kv, *state)


def attend_back(starts, core, qkv, kv, other_kv, d_out, out, log_total, after, d_query=None, own=True, low=0, count=0, final=False):
    group, _, tokens = qkv.shape
    resumed = d_query is not None
    return pl.pallas_call(
        functools.partial(attend_back_kernel, group=group, own=own, low=low, final=final, resumed=resumed),
        out_shape=(
            shaped((group, HD, tokens), bf16 if final else f32),
            shaped((count, 2 * HD, tokens), bf16),
            shaped((count, 2 * HD, tokens), bf16),
        ),
        in_specs=[in_smem, in_smem] + [in_vmem] * (5 + group + resumed) + [in_place] * len(after),
        out_specs=(in_vmem,) * 3,
        scratch_shapes=[
            pltpu.VMEM((group, HD, tokens), bf16),
            pltpu.VMEM((2, count, tokens, 2 * HD), bf16),
            pltpu.VMEM((2 * HD, tokens), bf16),
            pltpu.VMEM((2 * HD, tokens), bf16),
            pltpu.VMEM((2, count, 2 * HD, tokens), f32),
            pltpu.VMEM((HD, tokens), f32),
        ],
        cost_estimate=pl.CostEstimate(flops=count * 8 * 2**30, bytes_accessed=8 * 2**20, transcendentals=2**24),
        compiler_params=pltpu.CompilerParams(vmem_limit_bytes=32 * 2**20),
        name="attend_back",
    )(starts, core, qkv, kv, other_kv, out, log_total, *d_out, *((d_query,) if resumed else ()), *after)


def project(core, inputs, vectors, own, other):
    tokens, width = inputs.shape
    return pl.pallas_call(
        first_kernel,
        out_shape=shaped((width // HD, 3 * HD, tokens), bf16),
        in_specs=[in_smem] + [in_vmem] * 4,
        out_specs=in_vmem,
        cost_estimate=pl.CostEstimate(flops=2**30, bytes_accessed=4 * 2**20, transcendentals=0),
        compiler_params=pltpu.CompilerParams(vmem_limit_bytes=16 * 2**20),
        name="project",
    )(core, inputs, vectors, own, other)


def feed(core, mixed, inputs, targets, valid, vectors, *weights):
    tokens, width = inputs.shape
    group = width // HD
    hidden_units = weights[2].shape[1]
    rows = (2 * hidden_units + width) // 2 // group + 16
    return pl.pallas_call(
        feed_kernel,
        out_shape=(shaped((tokens, width), bf16), shaped((tokens, width), f32))
        + (shaped((group, rows, width), bf16),) * 2
        + (shaped((HD, tokens), bf16),) * group,
        in_specs=[in_smem] + [in_vmem] * (10 + group),
        out_specs=(in_vmem,) * (4 + group),
        scratch_shapes=[
            pltpu.VMEM((width, tokens), bf16),
            pltpu.VMEM((tokens, hidden_units), bf16),
            pltpu.VMEM((tokens, width), bf16),
            pltpu.VMEM((width, tokens), bf16),
            pltpu.VMEM((tokens, width), bf16),
            pltpu.VMEM((16, width), f32),
            pltpu.VMEM((width, tokens), bf16),
            pltpu.VMEM((tokens, width), f32),
            pltpu.VMEM((tokens, width), f32),
            pltpu.VMEM((tokens, hidden_units), f32),
            pltpu.VMEM((tokens, width), f32),
            pltpu.VMEM((1, hidden_units), f32),
        ],
        cost_estimate=pl.CostEstimate(flops=10 * 2**30, bytes_accessed=14 * 2**20, transcendentals=2**20),
        compiler_params=pltpu.CompilerParams(vmem_limit_bytes=34 * 2**20),
        name="feed",
    )(core, inputs, targets, valid, vectors, *weights, *mixed)


def first_back(group, core, d_heads, inputs, vectors, d_hidden, own, other):
    tokens, width = inputs.shape
    rows = own.shape[0] // group * 3 + 16
    return pl.pallas_call(
        first_back_kernel,
        out_shape=(shaped((tokens, width), f32),) + (shaped((group, rows, width), bf16),) * 2,
        in_specs=[in_smem] + [in_vmem] * 6,
        out_specs=(in_vmem,) * 3,
        scratch_shapes=[pltpu.VMEM((3 * width, tokens), bf16), pltpu.VMEM((width + 16, tokens), f32)],
        cost_estimate=pl.CostEstimate(flops=4 * 2**30, bytes_accessed=8 * 2**20, transcendentals=0),
        compiler_params=pltpu.CompilerParams(vmem_limit_bytes=24 * 2**20),
        name="first_back",
    )(core, d_heads, inputs, vectors, d_hidden, own, other)


def sum_squares(sums_early, sums_late, early, late):
    return pl.pallas_call(
        squares_kernel,
        out_shape=shaped((8, 128), f32),
        in_specs=[in_vmem] * (2 + 2 * len(early)),
        out_specs=in_vmem,
        cost_estimate=pl.CostEstimate(flops=2**22, bytes_accessed=4 * 2**20, transcendentals=0),
        compiler_params=pltpu.CompilerParams(vmem_limit_bytes=16 * 2**20),
        name="sum_squares",
    )(sums_early, sums_late, *early, *late)


def update(group, me, total_rows, squares, other_squares, sums_early, sums_late, d_raw, early, late, *state):
    weights = state[0]
    like = [shaped(weight.shape, f32) for weight in weights]
    out_specs = [in_place] * 4 + [in_vmem] * 2
    return pl.pallas_call(
        functools.partial(update_kernel, group=group, total_rows=total_rows),
        out_shape=[shaped(d_raw.shape, f32), shaped((8, 128), f32)] + like * 4,
        in_specs=[in_smem] + [in_vmem] * (5 + 2 * group + 18),
        out_specs=[in_place, in_vmem] + out_specs * 4,
        scratch_shapes=[
            pltpu.VMEM((group,) + early[0].shape, bf16),
            pltpu.VMEM((group,) + late[0].shape, bf16),
            pltpu.VMEM((2, d_raw.shape[0] // group, d_raw.shape[1]), f32),
        ]
        + [pltpu.VMEM((2, 4, weight.shape[0] // group, weight.shape[1]), f32) for weight in weights[:4]]
        + [pltpu.SemaphoreType.DMA((2, 17))],
        cost_estimate=pl.CostEstimate(flops=2**26, bytes_accessed=44 * 2**20, transcendentals=2**22),
        compiler_params=pltpu.CompilerParams(vmem_limit_bytes=31 * 2**20),
        name="update",
    )(me, squares, other_squares, sums_early, sums_late, d_raw, *early, *late, *state[0], *state[1], *state[2])


def from_other_core(value):
    return lax.ppermute(value, "fsdp", [(0, 1), (1, 0)])


def whole_of(value, axis):
    other = from_other_core(value)
    first = lax.axis_index("fsdp") == 0
    return jnp.concatenate([jnp.where(first, value, other), jnp.where(first, other, value)], axis)


def swap_ctx(value, bit):
    size = lax.axis_size("ctx")
    return lax.ppermute(value, "ctx", [(i, i ^ bit) for i in range(size)])


def across_groups(value, group):
    low, sums = value[:-16].astype(bf16), value[-16:]
    bit = group
    while bit < lax.axis_size("ctx"):
        sent = value.astype(bf16)
        received = swap_ctx(sent, bit)
        low = (sent[:-16].astype(f32) + received[:-16].astype(f32)).astype(bf16)
        sums = sent[-16:].astype(f32) + received[-16:].astype(f32)
        value = jnp.concatenate([low.astype(f32), sums], 0) if 2 * bit < lax.axis_size("ctx") else None
        bit *= 2
    return low, sums


def per_device(
    inputs,
    targets,
    valid_mask,
    block_seq,
    w_qkv,
    w_out,
    w_up,
    w_down,
    norm_gains,
    biases,
    first_qkv,
    first_out,
    first_up,
    first_down,
    first_gains,
    first_biases,
    second_qkv,
    second_out,
    second_up,
    second_down,
    second_gains,
    second_biases,
):
    rows_here, width = inputs.shape
    group = width // HD
    ctx_size = lax.axis_size("ctx")
    block_rows = rows_here * 2
    total_rows = float(block_rows * ctx_size)
    ctx_place = lax.axis_index("ctx")
    core_place = lax.axis_index("fsdp")
    members = [[first + i for i in range(group)] for first in range(0, ctx_size, group)]

    def exchange(value):
        return lax.all_to_all(value, "ctx", 0, 0, axis_index_groups=members, tiled=True)

    core = jnp.stack([core_place, ctx_place % group]).astype(jnp.int32)
    vectors = whole_of(jnp.concatenate([norm_gains, biases], 0), 1).astype(f32)
    other_qkv = from_other_core(w_qkv)
    other_out, other_up, other_down = (from_other_core(w_out), from_other_core(w_up), from_other_core(w_down))
    valid_rows = valid_mask.astype(f32)
    qkv = exchange(project(core, inputs, vectors, w_qkv, other_qkv))
    own_kv = qkv[:, HD:]
    other_kv = from_other_core(own_kv)

    first_block = (ctx_place // group) * group
    own_seq = lax.dynamic_slice_in_dim(block_seq, first_block, group, 0)
    starts = jnp.sum((block_seq[None, :] < own_seq[:, None]).astype(jnp.int32), axis=1)
    starts = jnp.maximum(starts - first_block + group, 0)
    behind = jnp.zeros((), jnp.int32)
    for edge in range(group, ctx_size, group):
        same = (block_seq[edge - group : edge] == block_seq[edge]).astype(jnp.int32)
        behind = jnp.maximum(behind, jnp.sum(same))
    most_behind = group - 1
    few_behind = group // 2
    branch = (behind > 0).astype(jnp.int32) + (behind > few_behind).astype(jnp.int32)
    counts = (0, few_behind, most_behind)

    def forward(count, own, other):
        spare = [(size, 2 * HD, rows_here) for size in counts[1:] if size != count for _ in (0, 1)]
        if count == 0:
            return tuple(attend(starts, core, qkv, qkv, other, spare=spare))
        prev_own = lax.ppermute(own[group - count :], "ctx", [(i, i + group) for i in range(ctx_size - group)])
        state = attend(starts, core, qkv, qkv, other, final=False)
        prev_own, state = lax.optimization_barrier((prev_own, state))
        prev_other = from_other_core(prev_own)
        mixed = tuple(attend(starts, core, qkv, prev_own, prev_other, state=state, spare=spare))
        prev = (prev_own, prev_other)
        unread = mixed[2 + group :]
        return mixed[: 2 + group] + (prev + unread if count == few_behind else unread + prev)

    results = lax.switch(branch, [functools.partial(forward, count) for count in counts], own_kv, other_kv)
    mixed, log_total = results[:2]
    prev = results[2 + group :]

    def deal(pieces):
        moved = []
        for step in range(1, group):
            moved.append(lax.ppermute(pieces[step], "ctx", [(i, i ^ step) for i in range(ctx_size)]))
        return [pieces[0]] + moved

    results = feed(
        core,
        deal(results[2 : 2 + group]),
        inputs,
        targets,
        valid_rows[:, None],
        vectors,
        w_out,
        other_out,
        w_up,
        other_up,
        w_down,
        other_down,
    )
    outputs, d_hidden, keep, send = results[:4]
    d_mixed = deal(results[4:])

    def paired(keep, received):
        return [(keep[i].astype(f32) + received[i].astype(f32)).astype(bf16) for i in range(group)]

    def gathered(pairs):
        return paired_sum([piece.astype(f32) for piece in deal(pairs)])

    def finished(mine):
        return across_groups(mine, group)

    pair = (keep.astype(f32) + from_other_core(send).astype(f32)).astype(bf16)
    pair, d_mixed = lax.optimization_barrier((pair, d_mixed))
    early_mine = jnp.sum(exchange(pair).astype(f32), axis=0)
    cuts = (0, 3, 5, group)

    def back(part, after, d_query, d_mixed):
        low, high = cuts[part], cuts[part + 1]
        return attend_back(
            starts,
            core,
            qkv,
            qkv,
            other_kv,
            d_mixed,
            mixed,
            log_total,
            after,
            d_query=d_query,
            low=low,
            count=high - low,
            final=high == group,
        )

    def backward(count, d_mixed, pair, prev):
        if count == 0:
            return tuple(back(0, (pair,), None, d_mixed)) + tuple(
                jnp.zeros((high - low, 2 * HD, rows_here), bf16) for low, high in zip(cuts[1:-1], cuts[2:])
            )
        prev_own, prev_other = prev[:2] if count == few_behind else prev[2:]
        d_query, d_behind, d_behind_other = attend_back(
            starts,
            core,
            qkv,
            prev_own,
            prev_other,
            d_mixed,
            mixed,
            log_total,
            (pair,),
            own=False,
            count=count,
        )
        d_prev = (d_behind.astype(f32) + from_other_core(d_behind_other).astype(f32)).astype(bf16)
        d_prev = lax.ppermute(d_prev, "ctx", [(i + group, i) for i in range(ctx_size - group)])
        results = tuple(back(0, (pair,), d_query, d_mixed))
        (d_query, d_own, d_other), d_prev = lax.optimization_barrier((results, d_prev))
        d_prev = jnp.pad(d_prev, ((group - count, 0), (0, 0), (0, 0)))
        d_own = (d_own.astype(f32) + d_prev[: cuts[1]].astype(f32)).astype(bf16)
        return (d_query, d_own, d_other) + tuple(d_prev[low:high] for low, high in zip(cuts[1:-1], cuts[2:]))

    def summed(d_own, d_other, *more):
        return sum((one.astype(f32) for one in more), d_own.astype(f32) + from_other_core(d_other).astype(f32)).astype(bf16)

    d_query, d_own, d_other, *d_prev = lax.switch(
        branch, [functools.partial(backward, count) for count in counts], d_mixed, pair, prev
    )
    first_sum = (d_own, d_other)
    d_query, d_own, d_other = back(1, (early_mine,), d_query, d_mixed)
    d_kv = [summed(*first_sum)]
    second_sum = (d_own, d_other)
    early_low, early_sums = finished(early_mine)
    d_query, d_own, d_other = back(2, (early_low, d_kv[0]), d_query, d_mixed)

    def forward_piece(piece, step):
        return lax.ppermute(piece, "ctx", [(i, i ^ step) for i in range(ctx_size)])

    early = [early_low] + [forward_piece(early_low, step) if step in (1, 2, 4) else None for step in range(1, group)]
    (early[1], early[2], early[4]), d_own, d_other = lax.optimization_barrier(
        ((early[1], early[2], early[4]), d_own, d_other)
    )
    d_kv += [summed(*second_sum, d_prev[0]), summed(d_own, d_other, d_prev[1])]
    d_heads = exchange(jnp.concatenate([d_query, jnp.concatenate(d_kv, 0)], 1))
    d_heads, (early[1], early[2], early[4]) = lax.optimization_barrier((d_heads, (early[1], early[2], early[4])))
    early[3] = forward_piece(early[2], 1)
    early[5] = forward_piece(early[1], 4)
    early[6] = forward_piece(early[4], 2)
    early[7] = forward_piece(early[6], 1)
    d_raw, keep, send = first_back(group, core, d_heads, inputs, vectors, d_hidden, w_qkv, other_qkv)
    (early[3], early[5], early[6]), keep, send = lax.optimization_barrier(((early[3], early[5], early[6]), keep, send))
    late_low, late_sums = finished(gathered(paired(keep, from_other_core(send))))
    late = deal([late_low] * group)
    squares = sum_squares(early_sums, late_sums, early, late)
    results = update(
        group,
        core[1:],
        total_rows,
        squares,
        from_other_core(squares),
        early_sums,
        late_sums,
        d_raw,
        early,
        late,
        [w_qkv, w_out, w_up, w_down, norm_gains, biases],
        [first_qkv, first_out, first_up, first_down, first_gains, first_biases],
        [second_qkv, second_out, second_up, second_down, second_gains, second_biases],
    )
    grad_inputs, norm = results[:2]
    return (outputs, grad_inputs) + tuple(results[2:8]) + (norm[0, 0],) + tuple(results[8:])


def solution(mesh):
    tokens = P(("ctx", "fsdp"), None)
    weight = P("fsdp", None)
    vector = P(None, "fsdp")
    params = (weight, weight, weight, weight, vector, vector)
    in_specs = (tokens, tokens, P(("ctx", "fsdp")), P()) + params * 3
    out_specs = (tokens, tokens) + params + (P(),) + params * 3
    return jax.shard_map(per_device, mesh=mesh, in_specs=in_specs, out_specs=out_specs, check_vma=False)
```
